32 devices in a mesh: shard: 4 (over x, core), ctx: 2 (over y), tp: 4 (over z).
Axes of the slice: x: 2, y: 2, z: 4, core: 2. Of those that a mesh axis runs over, the one named last changes fastest.
Arguments:
- tokens: bfloat16 [8192, 2048], P(('shard', 'ctx')), may hold values from -6 to 6
- cotangent: bfloat16 [8192, 2048], P(('shard', 'ctx')), may hold values from -6 to 6
- lengths: int32 [4], P('shard'), may hold values from 1024 to 2048, as said below
- qkv_weight: float32 [3, 2048, 2048], P(None, ('shard', 'ctx'), 'tp'), may hold values from -0.125 to 0.125
- out_weight: float32 [2048, 2048], P('tp', ('shard', 'ctx')), may hold values from -2 to 2
- gate_up_weight: float32 [2, 2048, 8192], P(None, ('shard', 'ctx'), 'tp'), may hold values from -0.125 to 0.125
- down_weight: float32 [8192, 2048], P('tp', ('shard', 'ctx')), may hold values from -0.0625 to 0.0625
- norm_gains: float32 [2, 2048], P(None, ('shard', 'ctx')), may hold values from 0.5 to 1.5
- qkv_first: float32 [3, 2048, 2048], P(None, ('shard', 'ctx'), 'tp'), may hold values from -34.212654 to 34.212654
- out_first: float32 [2048, 2048], P('tp', ('shard', 'ctx')), may hold values from -0.6 to 0.6
- gate_up_first: float32 [2, 2048, 8192], P(None, ('shard', 'ctx'), 'tp'), may hold values from -0.6 to 0.6
- down_first: float32 [8192, 2048], P('tp', ('shard', 'ctx')), may hold values from -0.6 to 0.6
- gains_first: float32 [2, 2048], P(None, ('shard', 'ctx')), may hold values from -54.3058 to 54.3058
- qkv_second: float32 [3, 2048, 2048], P(None, ('shard', 'ctx'), 'tp'), may hold values from 491.52 to 1638.4
- out_second: float32 [2048, 2048], P('tp', ('shard', 'ctx')), may hold values from 44.2368 to 147.456
- gate_up_second: float32 [2, 2048, 8192], P(None, ('shard', 'ctx'), 'tp'), may hold values from 30.72 to 102.4
- down_second: float32 [8192, 2048], P('tp', ('shard', 'ctx')), may hold values from 122.88 to 409.6
- gains_second: float32 [2, 2048], P(None, ('shard', 'ctx')), may hold values from 491.52 to 1638.4
Outputs:
- out_tokens: bfloat16 [8192, 2048], P(('shard', 'ctx'))
- input_grad: bfloat16 [8192, 2048], P(('shard', 'ctx'))
- qkv_grad: float32 [3, 2048, 2048], P(None, ('shard', 'ctx'), 'tp')
- out_grad: float32 [2048, 2048], P('tp', ('shard', 'ctx'))
- gate_up_grad: float32 [2, 2048, 8192], P(None, ('shard', 'ctx'), 'tp')
- down_grad: float32 [8192, 2048], P('tp', ('shard', 'ctx'))
- gains_grad: float32 [2, 2048], P(None, ('shard', 'ctx'))
- qkv_new: float32 [3, 2048, 2048], P(None, ('shard', 'ctx'), 'tp')
- out_step: float32 [2048, 2048], P('tp', ('shard', 'ctx'))
- gate_up_new: float32 [2, 2048, 8192], P(None, ('shard', 'ctx'), 'tp')
- down_new: float32 [8192, 2048], P('tp', ('shard', 'ctx'))
- gains_step: float32 [2, 2048], P(None, ('shard', 'ctx'))
- qkv_first_new: float32 [3, 2048, 2048], P(None, ('shard', 'ctx'), 'tp')
- out_first_new: float32 [2048, 2048], P('tp', ('shard', 'ctx'))
- gate_up_first_new: float32 [2, 2048, 8192], P(None, ('shard', 'ctx'), 'tp')
- down_first_new: float32 [8192, 2048], P('tp', ('shard', 'ctx'))
- gains_first_new: float32 [2, 2048], P(None, ('shard', 'ctx'))
- qkv_second_new: float32 [3, 2048, 2048], P(None, ('shard', 'ctx'), 'tp')
- out_second_new: float32 [2048, 2048], P('tp', ('shard', 'ctx'))
- gate_up_second_new: float32 [2, 2048, 8192], P(None, ('shard', 'ctx'), 'tp')
- down_second_new: float32 [8192, 2048], P('tp', ('shard', 'ctx'))
- gains_second_new: float32 [2, 2048], P(None, ('shard', 'ctx'))
The draws below stay inside these ranges and needn't reach their ends.
Inputs may be any that keep to these rules, and one draw needn't show every extreme that they name: lengths[s] is the length of the sequence of pack s; the first pack's sequence fills its whole pack of 2048 rows.
All inputs are finite; a program needn't handle non-finite values.
Results may differ from the reference program's by a relative error of at most 0.015.
The reference program's roundings to bfloat16 on the way count: a program that leaves them out, or rounds other values in their place, can miss the bound.
Values may be sent and summed in bfloat16 or wider, within the bound.
A program may use at most 384 MiB of HBM per device.

```python
import math
import jax
import jax.numpy as jnp
from jax import lax

D = 2048
HEADS = 32
HEAD = 64
FF = 8192
GROUP = 2048
TOKENS = 8192
N_SHARD = 4


def draw_lengths(key, part):
    drawn = jax.random.randint(key, (N_SHARD,), GROUP // 2, GROUP + 1, dtype=jnp.int32)
    first = jnp.arange(N_SHARD, dtype=jnp.int32) == 0
    return jnp.where(first, GROUP, drawn).astype(jnp.int32)


def level_of(key, dims, shards, least, high):
    level, own = 1.0, jax.random.fold_in(key, 6)
    for axis_at, parts in shards:
        heights = jnp.exp(jax.random.uniform(jax.random.fold_in(own, axis_at), (parts,), jnp.float32, least / len(shards), high / len(shards)))
        level = level * jnp.repeat(heights, dims[axis_at] // parts).reshape([-1 if axis == axis_at else 1 for axis in range(len(dims))])
    return level


def noise(rng, dims, width, reach, cuts=(), kind=jnp.bfloat16):
    factor_of = level_of(rng, dims, cuts, -0.22, 0.18) if cuts else 1.0
    array = jax.random.normal(rng, dims, jnp.float32) * width * factor_of
    return jnp.minimum(jnp.maximum(array, -reach), reach).astype(kind)


def setup_inputs(seed: int = 0) -> dict:
    seeds = jax.random.split(jax.random.key(seed), 19)
    return {
        "tokens": noise(seeds[0], (TOKENS, D), 1.0, 6.0, ((0, 8),)),
        "cotangent": noise(seeds[1], (TOKENS, D), 1.0, 6.0, ((0, 8),)),
        "lengths": draw_lengths(jax.random.fold_in(seeds[18], 71), 0),
        "qkv_weight": noise(seeds[3], (3, D, D), D ** -0.5, 0.125, ((1, 8), (2, 4)), jnp.float32),
        "out_weight": noise(seeds[4], (D, D), (max(D // 256, 1)) ** -0.5, 2.0, ((0, 4), (1, 8)), jnp.float32),
        "gate_up_weight": noise(seeds[5], (2, D, FF), D ** -0.5, 0.125, ((1, 8), (2, 4)), jnp.float32),
        "down_weight": noise(seeds[6], (FF, D), FF ** -0.5, 0.0625, ((0, 4), (1, 8)), jnp.float32),
        "norm_gains": jnp.clip(1.0 + 0.1 * jax.random.normal(seeds[7], (2, D), jnp.float32), 0.5, 1.5),
        "qkv_first": noise(seeds[8], (3, D, D), (0.063 * TOKENS ** 0.5), 34.212654, ((1, 8), (2, 4)), jnp.float32),
        "out_first": noise(seeds[9], (D, D), 0.1, 0.6, ((0, 4), (1, 8)), jnp.float32),
        "gate_up_first": noise(seeds[10], (2, D, FF), 0.1, 0.6, ((1, 8), (2, 4)), jnp.float32),
        "down_first": noise(seeds[11], (FF, D), 0.1, 0.6, ((0, 4), (1, 8)), jnp.float32),
        "gains_first": noise(seeds[12], (2, D), (0.1 * TOKENS ** 0.5), 54.3058, ((1, 8),), jnp.float32),
        "qkv_second": jnp.clip(jnp.exp(math.log(1638.4) - 1.2039728 * jax.random.uniform(seeds[13], (3, D, D), jnp.float32) ** level_of(seeds[13], (3, D, D), ((1, 8), (2, 4)), -0.2, 0.2)), 491.52, 1638.4),
        "out_second": jnp.clip(jnp.exp(math.log(147.456) - 1.2039727 * jax.random.uniform(seeds[14], (D, D), jnp.float32) ** level_of(seeds[14], (D, D), ((0, 4), (1, 8)), -0.2, 0.2)), 44.2368, 147.456),
        "gate_up_second": jnp.clip(jnp.exp(math.log(102.4) - 1.2039728 * jax.random.uniform(seeds[15], (2, D, FF), jnp.float32) ** level_of(seeds[15], (2, D, FF), ((1, 8), (2, 4)), -0.2, 0.2)), 30.72, 102.4),
        "down_second": jnp.clip(jnp.exp(math.log(409.6) - 1.2039728 * jax.random.uniform(seeds[16], (FF, D), jnp.float32) ** level_of(seeds[16], (FF, D), ((0, 4), (1, 8)), -0.2, 0.2)), 122.88, 409.6),
        "gains_second": jnp.clip(jnp.exp(math.log(1638.4) - 1.2039728 * jax.random.uniform(seeds[17], (2, D), jnp.float32) ** level_of(seeds[17], (2, D), ((1, 8),), -0.2, 0.2)), 491.52, 1638.4),
    }


@jax.custom_vjp
def low(v):
    return lax.optimization_barrier(v.astype(jnp.bfloat16)).astype(jnp.float32)

@jax.custom_vjp
def low_back(v):
    return v

def low_keep(v):
    return (low(v), None)

def low_pass(kept, grad):
    return (grad,)

def back_keep(v):
    return (v, None)

def back_low(kept, grad):
    return (low(grad),)
low.defvjp(low_keep, low_pass)
low_back.defvjp(back_keep, back_low)
norm_eps = 1e-05
rope_base = 130000.0
beta_one = 0.9
beta_two = 0.95
learn_rate = 0.02
decay_rate = 0.1
adam_eps = 1e-08
step_count = 4.0

def matmul(left, right):
    return jnp.dot(left, right, precision=lax.Precision.HIGHEST, preferred_element_type=jnp.float32)

def rotation(position, head_size):
    half = head_size // 2
    freqs = rope_base ** (-(jnp.arange(half, dtype=jnp.float32) * 2.0) / head_size)
    angle = position.astype(jnp.float32)[:, None] * freqs[None, :]
    return (jnp.cos(angle)[:, None, :], jnp.sin(angle)[:, None, :])

def rotate(values, cosine, sine):
    half = values.shape[-1] // 2
    first, second = (values[..., :half], values[..., half:])
    return jnp.concatenate([first * cosine - second * sine, second * cosine + first * sine], -1)

def attend_block(query, keys, values, key_mask):
    raw = jnp.einsum('qhd,khd->hqk', query, keys, precision=lax.Precision.HIGHEST)
    scores = low_back(raw * 0.125)
    scores = jnp.where(key_mask[None], scores, -1e+30)
    peak = lax.optimization_barrier(jnp.max(scores, axis=-1, keepdims=True))
    expo = jnp.exp(scores - peak)
    probs = low(expo / lax.optimization_barrier(jnp.sum(expo, axis=-1, keepdims=True)))
    return jnp.einsum('hqk,khd->qhd', probs, values, precision=lax.Precision.HIGHEST)

def layer_pack(stream, weights, live):
    w_query, w_key, w_value, w_out, w_gate, w_up, w_down, gain_one, gain_two = weights
    row_count = stream.shape[0]
    index = jnp.arange(row_count, dtype=jnp.int32)
    scale_one = lax.rsqrt(lax.optimization_barrier(jnp.mean(stream * stream, axis=-1, keepdims=True)) + norm_eps)
    normed_one = low(stream * scale_one * gain_one)
    cosine, sine = rotation(index, HEAD)
    shape3 = (row_count, HEADS, HEAD)
    query = low(rotate(low_back(matmul(normed_one, w_query)).reshape(shape3), cosine, sine))
    keys = low(rotate(low_back(matmul(normed_one, w_key)).reshape(shape3), cosine, sine))
    values = low(low_back(matmul(normed_one, w_value))).reshape(shape3)
    key_mask = (index[None, :] <= index[:, None]) & ((index[:, None] < live) | (index[None, :] == index[:, None]))
    block = min(512, row_count)
    query_blocks = query.reshape(row_count // block, block, HEADS, HEAD)
    mask_blocks = key_mask.reshape(row_count // block, block, row_count)
    attend = jax.checkpoint(lambda pair: attend_block(pair[0], keys, values, pair[1]))
    mixed = lax.map(attend, (query_blocks, mask_blocks)).reshape(row_count, D)
    mixed = low(low_back(mixed))
    middle = stream + low_back(matmul(mixed, w_out))
    scale_two = lax.rsqrt(lax.optimization_barrier(jnp.mean(middle * middle, axis=-1, keepdims=True)) + norm_eps)
    normed_two = low(middle * scale_two * gain_two)
    gate = low_back(matmul(normed_two, w_gate))
    upward = low_back(matmul(normed_two, w_up))
    hidden = low(gate * jax.nn.sigmoid(gate) * upward)
    return middle + low_back(matmul(hidden, w_down))

def adam_update(weight, first, second, grad, decay):
    first_new = beta_one * first + (1.0 - beta_one) * grad
    second_new = beta_two * second + (1.0 - beta_two) * grad * grad
    first_hat = first_new / (1.0 - beta_one ** step_count)
    second_hat = second_new / (1.0 - beta_two ** step_count)
    update = learn_rate * (first_hat / (jnp.sqrt(second_hat) + adam_eps) + decay * weight)
    return (update, first_new, second_new)

def reference(tokens, cotangent, lengths, qkv_weight, out_weight, gate_up_weight, down_weight, norm_gains, qkv_first, out_first, gate_up_first, down_first, gains_first, qkv_second, out_second, gate_up_second, down_second, gains_second):
    group_rows = tokens.shape[0] // N_SHARD

    def forward(stream, qkv, w_out, gate_up, w_down, gains):
        qkv_low = low(qkv)
        gate_up_low = low(gate_up)
        gains_low = low(gains)
        weights = (qkv_low[0], qkv_low[1], qkv_low[2], low(w_out), gate_up_low[0], gate_up_low[1], low(w_down), gains_low[0], gains_low[1])
        packs = stream.reshape(N_SHARD, group_rows, D)
        result = lax.map(lambda item: layer_pack(item[0], weights, item[1]), (packs, lengths))
        return result.reshape(stream.shape)
    output, pullback = jax.vjp(forward, tokens.astype(jnp.float32), qkv_weight, out_weight, gate_up_weight, down_weight, norm_gains)
    grads = pullback(cotangent.astype(jnp.float32))
    qkv_step, qkv_first_new, qkv_second_new = adam_update(qkv_weight, qkv_first, qkv_second, grads[1], decay_rate)
    out_step, out_first_new, out_second_new = adam_update(out_weight, out_first, out_second, grads[2], decay_rate)
    gate_up_step, gate_up_first_new, gate_up_second_new = adam_update(gate_up_weight, gate_up_first, gate_up_second, grads[3], decay_rate)
    down_step, down_first_new, down_second_new = adam_update(down_weight, down_first, down_second, grads[4], decay_rate)
    gains_step, gains_first_new, gains_second_new = adam_update(norm_gains, gains_first, gains_second, grads[5], 0.0)
    qkv_new = qkv_weight - qkv_step
    gate_up_new = gate_up_weight - gate_up_step
    down_new = down_weight - down_step
    return (output.astype(jnp.bfloat16), grads[0].astype(jnp.bfloat16), grads[1], grads[2], grads[3], grads[4], grads[5], qkv_new, out_step, gate_up_new, down_new, gains_step, qkv_first_new, out_first_new, gate_up_first_new, down_first_new, gains_first_new, qkv_second_new, out_second_new, gate_up_second_new, down_second_new, gains_second_new)
```

```python
import jax
import jax.numpy as jnp
from jax import lax
from jax.experimental import pallas as pl
from jax.experimental.pallas import tpu as pltpu
from jax.sharding import PartitionSpec as P

HEAD = 64
PAIR = 128
BLOCK = 256
MASKED = -1e30


def dot(left, right, contract):
    return lax.dot_general(
        left, right, ((contract[:1], contract[1:]), ((), ())), preferred_element_type=jnp.float32
    )


def one_head(values, head):
    lane = lax.broadcasted_iota(jnp.int32, values.shape, 1)
    return jnp.where((lane < HEAD) == (head == 0), values, jnp.zeros_like(values))


def causal(scores):
    key = lax.broadcasted_iota(jnp.int32, scores.shape, 0)
    query = lax.broadcasted_iota(jnp.int32, scores.shape, 1)
    return jnp.where(key <= query, scores, MASKED)


def attend_kernel(info, q_ref, k_ref, v_ref, kp_ref, vp_ref, o_ref, l_ref):
    block = q_ref.shape[0]
    blocks = k_ref.shape[0] // block
    step = pl.program_id(1)
    late = info[0]
    first_row = late * k_ref.shape[0] + step * block

    def run(own, with_prev):
        query = q_ref[...]
        mixed = []
        for head in range(2):
            rows = one_head(query, head)
            parts = []
            if with_prev:
                parts.append((dot(kp_ref[...], rows, (1, 1)), vp_ref[...]))
            if own:
                parts.append(
                    (dot(k_ref[: own * block], rows, (1, 1)), v_ref[: own * block])
                )
            diag = pl.ds(own * block, block)
            parts.append((causal(dot(k_ref[diag], rows, (1, 1))), v_ref[diag]))
            peak = parts[0][0].max(0, keepdims=True)
            for scores, _ in parts[1:]:
                peak = jnp.maximum(peak, scores.max(0, keepdims=True))
            expo = [jnp.exp(scores - peak) for scores, _ in parts]
            denom = expo[0].sum(0, keepdims=True)
            for e in expo[1:]:
                denom = denom + e.sum(0, keepdims=True)
            inverse = 1.0 / denom
            total = None
            for e, (_, value) in zip(expo, parts):
                probs = (e * inverse).astype(jnp.bfloat16)
                term = dot(value, probs, (0, 0))
                total = term if total is None else total + term
            mixed.append(total[head * HEAD : (head + 1) * HEAD])
            index = first_row + lax.broadcasted_iota(jnp.int32, peak.shape, 1)
            l_ref[0, head : head + 1, :] = jnp.where(index < info[1], peak + jnp.log(denom), -MASKED)
        result = jnp.concatenate(mixed, 0).T
        index = first_row + lax.broadcasted_iota(jnp.int32, result.shape, 0)
        own_value = v_ref[pl.ds(own * block, block)].astype(jnp.float32)
        o_ref[...] = jnp.where(index < info[1], result, own_value).astype(jnp.bfloat16)

    for own in range(blocks):
        for with_prev in (False, True):
            pl.when((step == own) & (late == int(with_prev)))(
                lambda own=own, with_prev=with_prev: run(own, with_prev)
            )


def attend_forward(info, query, keys, values, keys_prev, values_prev):
    rows, width = query.shape
    block = min(BLOCK, rows)
    pairs = width // PAIR
    part = pl.BlockSpec((block, PAIR), lambda p, i, info: (i, p))
    whole = pl.BlockSpec((rows, PAIR), lambda p, i, info: (0, p))
    return pl.pallas_call(
        attend_kernel,
        out_shape=(
            jax.ShapeDtypeStruct((rows, width), jnp.bfloat16),
            jax.ShapeDtypeStruct((pairs, 2, rows), jnp.float32),
        ),
        grid_spec=pltpu.PrefetchScalarGridSpec(
            num_scalar_prefetch=1,
            grid=(pairs, rows // block),
            in_specs=[part, whole, whole, whole, whole],
            out_specs=[part, pl.BlockSpec((1, 2, block), lambda p, i, info: (p, 0, i))],
        ),
        compiler_params=pltpu.CompilerParams(vmem_limit_bytes=48 * 2**20),
        cost_estimate=pl.CostEstimate(
            flops=rows * rows * width * 6, bytes_accessed=8 * rows * width * 2,
            transcendentals=rows * rows * width // HEAD,
        ),
        name="attend_forward",
    )(info, query, keys, values, keys_prev, values_prev)


def rotate_lanes(values, cosine, sine):
    lane = lax.broadcasted_iota(jnp.int32, values.shape, 1) % HEAD
    width = values.shape[1]
    ahead = pltpu.roll(values, width - HEAD // 2, 1)
    behind = pltpu.roll(values, HEAD // 2, 1)
    return values * cosine + jnp.where(lane < HEAD // 2, -ahead, behind) * sine


def attend_back_kernel(
    info, q_ref, k_ref, v_ref, kp_ref, vp_ref, o_ref, do_ref, l_ref, cos_ref, sin_ref,
    dq_ref, dk_ref, dv_ref, dkp_ref, dvp_ref, dkp_acc, dvp_acc,
):
    block = q_ref.shape[0]
    blocks = k_ref.shape[0] // block
    step = pl.program_id(1)
    late = info[0]
    first_row = late * k_ref.shape[0] + step * block

    @pl.when(step == 0)
    def _():
        dk_ref[...] = jnp.zeros_like(dk_ref)
        dv_ref[...] = jnp.zeros_like(dv_ref)
        dkp_acc[...] = jnp.zeros_like(dkp_acc)
        dvp_acc[...] = jnp.zeros_like(dvp_acc)

    query = q_ref[...]
    upstream = do_ref[...]
    product = (upstream.astype(jnp.float32) * o_ref[...].astype(jnp.float32)).T
    queries = [one_head(query, head) for head in range(2)]
    upstreams = [one_head(upstream, head) for head in range(2)]
    inner = [product[head * HEAD : (head + 1) * HEAD].sum(0, keepdims=True) for head in range(2)]
    totals = [l_ref[0, head : head + 1, :] for head in range(2)]
    query_both = jnp.concatenate(queries, 0)
    upstream_both = jnp.concatenate(upstreams, 0)

    def tile(keys, values, masked):
        grads, probs_all, out = [], [], []
        for head in range(2):
            scores = dot(keys, queries[head], (1, 1))
            if masked:
                scores = causal(scores)
            probs = jnp.exp(scores - totals[head])
            prob_grad = dot(values, upstreams[head], (1, 1))
            score_grad = (probs * (prob_grad - inner[head])).astype(jnp.bfloat16)
            probs_all.append(probs.astype(jnp.bfloat16))
            grads.append(score_grad)
            out.append(dot(keys, score_grad, (0, 0))[head * HEAD : (head + 1) * HEAD])
        key_grad = dot(jnp.concatenate(grads, 1), query_both, (1, 0))
        value_grad = dot(jnp.concatenate(probs_all, 1), upstream_both, (1, 0))
        return jnp.concatenate(out, 0), key_grad, value_grad

    def run(own, with_prev):
        diag = pl.ds(own * block, block)
        query_grad, key_grad, value_grad = tile(k_ref[diag], v_ref[diag], True)
        index = first_row + lax.broadcasted_iota(jnp.int32, upstream.shape, 0)
        dk_ref[diag] += key_grad
        dv_ref[diag] += value_grad + jnp.where(
            index < info[1], 0.0, upstream.astype(jnp.float32)
        )
        for at in range(own):
            here = pl.ds(at * block, block)
            more, key_grad, value_grad = tile(k_ref[here], v_ref[here], False)
            query_grad += more
            dk_ref[here] += key_grad
            dv_ref[here] += value_grad
        if with_prev:
            for at in range(blocks):
                here = pl.ds(at * block, block)
                more, key_grad, value_grad = tile(kp_ref[here], vp_ref[here], False)
                query_grad += more
                dkp_acc[here] += key_grad
                dvp_acc[here] += value_grad
        grad = rotate_lanes(query_grad.T * 0.125, cos_ref[...], -sin_ref[...])
        dq_ref[...] = grad.astype(jnp.bfloat16)

    for own in range(blocks):
        for with_prev in (False, True):
            pl.when((step == own) & (late == int(with_prev)))(
                lambda own=own, with_prev=with_prev: run(own, with_prev)
            )

    @pl.when(step == blocks - 1)
    def _():
        dkp_ref[...] = dkp_acc[...].astype(jnp.bfloat16)
        dvp_ref[...] = dvp_acc[...].astype(jnp.bfloat16)


def attend_back(info, query, keys, values, keys_prev, values_prev, mixed, upstream, totals, cosine, sine):
    rows, width = query.shape
    block = min(BLOCK, rows)
    pairs = width // PAIR
    part = pl.BlockSpec((block, PAIR), lambda p, i, info: (i, p))
    whole = pl.BlockSpec((rows, PAIR), lambda p, i, info: (0, p))
    table = pl.BlockSpec((block, PAIR), lambda p, i, info: (i, 0))
    return pl.pallas_call(
        attend_back_kernel,
        out_shape=(
            jax.ShapeDtypeStruct((rows, width), jnp.bfloat16),
            jax.ShapeDtypeStruct((rows, width), jnp.float32),
            jax.ShapeDtypeStruct((rows, width), jnp.float32),
            jax.ShapeDtypeStruct((rows, width), jnp.bfloat16),
            jax.ShapeDtypeStruct((rows, width), jnp.bfloat16),
        ),
        grid_spec=pltpu.PrefetchScalarGridSpec(
            num_scalar_prefetch=1,
            grid=(pairs, rows // block),
            in_specs=[part, whole, whole, whole, whole, part, part,
                      pl.BlockSpec((1, 2, block), lambda p, i, info: (p, 0, i)), table, table],
            out_specs=[part, whole, whole, whole, whole],
            scratch_shapes=[pltpu.VMEM((rows, PAIR), jnp.float32)] * 2,
        ),
        compiler_params=pltpu.CompilerParams(vmem_limit_bytes=48 * 2**20),
        cost_estimate=pl.CostEstimate(
            flops=rows * rows * width * 15, bytes_accessed=16 * rows * width * 2,
            transcendentals=rows * rows * width // HEAD,
        ),
        name="attend_back",
    )(info, query, keys, values, keys_prev, values_prev, mixed, upstream, totals, cosine, sine)


norm_eps = 1e-05
rope_base = 130000.0
beta_one = 0.9
beta_two = 0.95
learn_rate = 0.02
decay_rate = 0.1
adam_eps = 1e-08
step_count = 4.0


def rotation(position, head_size):
    half = head_size // 2
    freqs = rope_base ** (-(jnp.arange(half, dtype=jnp.float32) * 2.0) / head_size)
    angle = position.astype(jnp.float32)[:, None] * freqs[None, :]
    return (jnp.cos(angle)[:, None, :], jnp.sin(angle)[:, None, :])


def outer_sum(left, right):
    return lax.dot_general(
        left, right, (((0,), (0,)), ((), ())), preferred_element_type=jnp.float32
    )


def back_dot(grad, weight):
    return lax.dot_general(
        grad, weight, (((1,), (1,)), ((), ())), preferred_element_type=jnp.float32
    )


def normalize(stream, gain):
    scale = lax.rsqrt(jnp.mean(stream * stream, axis=-1, keepdims=True) + norm_eps)
    return ((stream * scale * gain).astype(jnp.bfloat16), scale)


def normalize_back(stream, scale, gain, upstream):
    gain_grad = jnp.sum(upstream * stream * scale, axis=0)
    inner = jnp.sum(upstream * gain * stream, axis=-1, keepdims=True)
    stream_grad = (
        scale * gain * upstream - stream * (scale * scale * scale / stream.shape[-1]) * inner
    )
    return (stream_grad, gain_grad)


def scatter_low(grad):
    return lax.psum_scatter(
        grad.astype(jnp.bfloat16), ("shard", "ctx"), scatter_dimension=1, tiled=True
    ).astype(jnp.float32)


def adam_update(weight, first, second, grad, decay):
    first_new = beta_one * first + (1.0 - beta_one) * grad
    second_new = beta_two * second + (1.0 - beta_two) * grad * grad
    first_hat = first_new / (1.0 - beta_one**step_count)
    second_hat = second_new / (1.0 - beta_two**step_count)
    update = learn_rate * (first_hat / (jnp.sqrt(second_hat) + adam_eps) + decay * weight)
    return (update, first_new, second_new)


def body(
    tokens,
    cotangent,
    lengths,
    qkv_weight,
    out_weight,
    gate_up_weight,
    down_weight,
    norm_gains,
    qkv_first,
    out_first,
    gate_up_first,
    down_first,
    gains_first,
    qkv_second,
    out_second,
    gate_up_second,
    down_second,
    gains_second,
):
    row_count = tokens.shape[0]
    live = lengths[0]
    offset = lax.axis_index("ctx") * row_count
    query_index = offset + jnp.arange(row_count, dtype=jnp.int32)
    late = lax.axis_index("ctx")
    info = jnp.stack([late.astype(jnp.int32), live])
    qkv_low = qkv_weight.astype(jnp.bfloat16)
    out_low = out_weight.astype(jnp.bfloat16)
    gate_up_low = gate_up_weight.astype(jnp.bfloat16)
    down_low = down_weight.astype(jnp.bfloat16)
    gains_low = norm_gains.astype(jnp.bfloat16)
    qkv_full, out_full, gate_up_full, down_full, gains_full = (
        lax.all_gather(qkv_low, ("shard", "ctx"), axis=1, tiled=True),
        lax.all_gather(out_low, ("shard", "ctx"), axis=1, tiled=True),
        lax.all_gather(gate_up_low, ("shard", "ctx"), axis=1, tiled=True),
        lax.all_gather(down_low, ("shard", "ctx"), axis=1, tiled=True),
        lax.all_gather(gains_low, ("shard", "ctx"), axis=1, tiled=True),
    )
    gain_one = gains_full[0].astype(jnp.float32)
    gain_two = gains_full[1].astype(jnp.float32)
    stream = tokens.astype(jnp.float32)
    normed_one, scale_one = normalize(stream, gain_one)
    cosine, sine = rotation(query_index, HEAD)
    cosine, sine = (jnp.concatenate([c[:, 0]] * 4, 1) for c in (cosine, sine))
    local_width = qkv_full.shape[2]
    wide = lambda table: jnp.concatenate([table] * (local_width // PAIR), 1)
    cos_wide, sin_wide = wide(cosine), wide(sine)

    def rotate_wide(values, sine_wide):
        lane = lax.broadcasted_iota(jnp.int32, values.shape, 1) % HEAD
        half = HEAD // 2
        ahead = jnp.roll(values, -half, 1)
        behind = jnp.roll(values, half, 1)
        return values * cos_wide + jnp.where(lane < half, -ahead, behind) * sine_wide

    products = [
        jnp.dot(normed_one, qkv_full[i], preferred_element_type=jnp.float32) for i in range(3)
    ]
    query = (rotate_wide(products[0], sin_wide) * 0.125).astype(jnp.bfloat16)
    keys_own = rotate_wide(products[1], sin_wide).astype(jnp.bfloat16)
    values_own = products[2].astype(jnp.bfloat16)
    keys_prev, values_prev = (lax.ppermute(a, "ctx", [(0, 1)]) for a in (keys_own, values_own))
    mixed_low, totals = attend_forward(info, query, keys_own, values_own, keys_prev, values_prev)
    attn_part = jnp.dot(mixed_low, out_full, preferred_element_type=jnp.float32)
    middle = stream + lax.psum(attn_part.astype(jnp.bfloat16), "tp").astype(jnp.float32)
    normed_two, scale_two = normalize(middle, gain_two)
    gate = jnp.dot(normed_two, gate_up_full[0], preferred_element_type=jnp.float32)
    upward = jnp.dot(normed_two, gate_up_full[1], preferred_element_type=jnp.float32)
    sigma = jax.nn.sigmoid(gate)
    swish = gate * sigma
    hidden = (swish * upward).astype(jnp.bfloat16)
    mlp_part = jnp.dot(hidden, down_full, preferred_element_type=jnp.float32)
    out_tokens = (
        middle + lax.psum(mlp_part.astype(jnp.bfloat16), "tp").astype(jnp.float32)
    ).astype(jnp.bfloat16)
    qkv_use, out_use, gate_up_use, down_use = (qkv_full, out_full, gate_up_full, down_full)
    upstream = cotangent.astype(jnp.float32)
    upstream_low = upstream.astype(jnp.bfloat16)
    down_grad_local = outer_sum(hidden, upstream_low)
    hidden_grad = back_dot(upstream_low, down_use)
    gate_grad = (hidden_grad * upward * sigma * (1.0 + gate * (1.0 - sigma))).astype(jnp.bfloat16)
    upward_grad = (hidden_grad * swish).astype(jnp.bfloat16)
    gate_up_grad_local = jnp.stack(
        [outer_sum(normed_two, gate_grad), outer_sum(normed_two, upward_grad)]
    )
    mlp_back_part = back_dot(gate_grad, gate_up_use[0]) + back_dot(upward_grad, gate_up_use[1])
    normed_two_grad = lax.psum(mlp_back_part.astype(jnp.bfloat16), "tp").astype(jnp.float32)
    middle_norm_grad, gain_two_grad = normalize_back(middle, scale_two, gain_two, normed_two_grad)
    middle_grad = upstream + middle_norm_grad
    middle_low = middle_grad.astype(jnp.bfloat16)
    out_grad_local = outer_sum(mixed_low, middle_low)
    mixed_grad = back_dot(middle_low, out_use).astype(jnp.bfloat16)
    query_low, key_grad, value_grad, key_prev_grad, value_prev_grad = attend_back(
        info, query, keys_own, values_own, keys_prev, values_prev, mixed_low, mixed_grad,
        totals, cosine, sine,
    )
    key_more, value_more = (
        lax.ppermute(a, "ctx", [(1, 0)]).astype(jnp.float32)
        for a in (key_prev_grad, value_prev_grad)
    )
    key_low = rotate_wide(key_grad + key_more, -sin_wide).astype(jnp.bfloat16)
    value_low = (value_grad + value_more).astype(jnp.bfloat16)
    qkv_grad_local = jnp.stack(
        [
            outer_sum(normed_one, query_low),
            outer_sum(normed_one, key_low),
            outer_sum(normed_one, value_low),
        ]
    )
    attn_back_part = (
        back_dot(query_low, qkv_use[0])
        + back_dot(key_low, qkv_use[1])
        + back_dot(value_low, qkv_use[2])
    )
    normed_one_grad = lax.psum(attn_back_part.astype(jnp.bfloat16), "tp").astype(jnp.float32)
    stream_grad, gain_one_grad = normalize_back(stream, scale_one, gain_one, normed_one_grad)
    input_grad = (middle_grad + stream_grad).astype(jnp.bfloat16)
    gains_local = jnp.stack([gain_one_grad, gain_two_grad])
    qkv_grad, out_grad, gate_up_grad, down_grad, gains_grad = (
        scatter_low(qkv_grad_local),
        scatter_low(out_grad_local),
        scatter_low(gate_up_grad_local),
        scatter_low(down_grad_local),
        lax.psum_scatter(gains_local, ("shard", "ctx"), scatter_dimension=1, tiled=True),
    )
    qkv_step, qkv_first_new, qkv_second_new = adam_update(
        qkv_weight, qkv_first, qkv_second, qkv_grad, decay_rate
    )
    out_step, out_first_new, out_second_new = adam_update(
        out_weight, out_first, out_second, out_grad, decay_rate
    )
    gate_up_step, gate_up_first_new, gate_up_second_new = adam_update(
        gate_up_weight, gate_up_first, gate_up_second, gate_up_grad, decay_rate
    )
    down_step, down_first_new, down_second_new = adam_update(
        down_weight, down_first, down_second, down_grad, decay_rate
    )
    gains_step, gains_first_new, gains_second_new = adam_update(
        norm_gains, gains_first, gains_second, gains_grad, 0.0
    )
    qkv_new = qkv_weight - qkv_step
    gate_up_new = gate_up_weight - gate_up_step
    down_new = down_weight - down_step
    return (
        out_tokens,
        input_grad,
        qkv_grad,
        out_grad,
        gate_up_grad,
        down_grad,
        gains_grad,
        qkv_new,
        out_step,
        gate_up_new,
        down_new,
        gains_step,
        qkv_first_new,
        out_first_new,
        gate_up_first_new,
        down_first_new,
        gains_first_new,
        qkv_second_new,
        out_second_new,
        gate_up_second_new,
        down_second_new,
        gains_second_new,
    )


def solution(mesh):
    return jax.shard_map(
        body,
        mesh=mesh,
        in_specs=(
            P(("shard", "ctx"), None),
            P(("shard", "ctx"), None),
            P("shard"),
            P(None, ("shard", "ctx"), "tp"),
            P("tp", ("shard", "ctx")),
            P(None, ("shard", "ctx"), "tp"),
            P("tp", ("shard", "ctx")),
            P(None, ("shard", "ctx")),
            P(None, ("shard", "ctx"), "tp"),
            P("tp", ("shard", "ctx")),
            P(None, ("shard", "ctx"), "tp"),
            P("tp", ("shard", "ctx")),
            P(None, ("shard", "ctx")),
            P(None, ("shard", "ctx"), "tp"),
            P("tp", ("shard", "ctx")),
            P(None, ("shard", "ctx"), "tp"),
            P("tp", ("shard", "ctx")),
            P(None, ("shard", "ctx")),
        ),
        out_specs=(
            P(("shard", "ctx"), None),
            P(("shard", "ctx"), None),
            P(None, ("shard", "ctx"), "tp"),
            P("tp", ("shard", "ctx")),
            P(None, ("shard", "ctx"), "tp"),
            P("tp", ("shard", "ctx")),
            P(None, ("shard", "ctx")),
            P(None, ("shard", "ctx"), "tp"),
            P("tp", ("shard", "ctx")),
            P(None, ("shard", "ctx"), "tp"),
            P("tp", ("shard", "ctx")),
            P(None, ("shard", "ctx")),
            P(None, ("shard", "ctx"), "tp"),
            P("tp", ("shard", "ctx")),
            P(None, ("shard", "ctx"), "tp"),
            P("tp", ("shard", "ctx")),
            P(None, ("shard", "ctx")),
            P(None, ("shard", "ctx"), "tp"),
            P("tp", ("shard", "ctx")),
            P(None, ("shard", "ctx"), "tp"),
            P("tp", ("shard", "ctx")),
            P(None, ("shard", "ctx")),
        ),
        check_vma=False,
    )
```

```python
import functools
import jax
import jax.numpy as jnp
from jax import lax
from jax.experimental import pallas as pl
from jax.experimental.pallas import tpu as pltpu
from jax.sharding import PartitionSpec as P

HEAD = 64
PAIR = 128
BLOCK = 256
CHUNK = 64
MASKED = -1e30
MESH = pl.DeviceIdType.MESH


norm_eps = 1e-05
rope_base = 130000.0
beta_one = 0.9
beta_two = 0.95
learn_rate = 0.02
decay_rate = 0.1
adam_eps = 1e-08
step_count = 4.0


def rotation(position, head_size):
    half = head_size // 2
    freqs = rope_base ** (-(jnp.arange(half, dtype=jnp.float32) * 2.0) / head_size)
    angle = position.astype(jnp.float32)[:, None] * freqs[None, :]
    return (jnp.cos(angle)[:, None, :], jnp.sin(angle)[:, None, :])


def outer_sum(left, right):
    return lax.dot_general(
        left, right, (((0,), (0,)), ((), ())), preferred_element_type=jnp.float32
    )


def back_dot(grad, weight):
    return lax.dot_general(
        grad, weight, (((1,), (1,)), ((), ())), preferred_element_type=jnp.float32
    )


def dot(left, right, contract):
    return lax.dot_general(
        left, right, ((contract[:1], contract[1:]), ((), ())), preferred_element_type=jnp.float32
    )


def one_head(values, head):
    lane = lax.broadcasted_iota(jnp.int32, values.shape, 1)
    return jnp.where((lane < HEAD) == (head == 0), values, jnp.zeros_like(values))


def causal(scores):
    key = lax.broadcasted_iota(jnp.int32, scores.shape, 0)
    query = lax.broadcasted_iota(jnp.int32, scores.shape, 1)
    return jnp.where(key <= query, scores, MASKED)


def rotate_lanes(values, cosine, sine):
    lane = lax.broadcasted_iota(jnp.int32, values.shape, 1) % HEAD
    width = values.shape[1]
    ahead = pltpu.roll(values, width - HEAD // 2, 1)
    behind = pltpu.roll(values, HEAD // 2, 1)
    return values * cosine + jnp.where(lane < HEAD // 2, -ahead, behind) * sine


def greet(me, count, more=0):
    barrier = pltpu.get_barrier_semaphore()

    @pl.when(me > 0)
    def _():
        pl.semaphore_signal(barrier, inc=1, device_id={"tp": me - 1}, device_id_type=MESH)

    @pl.when(me < count - 1)
    def _():
        pl.semaphore_signal(barrier, inc=1, device_id={"tp": me + 1}, device_id_type=MESH)

    @pl.when((me > 0) & (me < count - 1))
    def _():
        pl.semaphore_wait(barrier, 2 + more)

    @pl.when((me == 0) | (me == count - 1))
    def _():
        pl.semaphore_wait(barrier, 1 + more)


def chain_parts(count, part_ref, out_ref, slots, send, recv, finish, size):
    me = lax.axis_index("tp")
    half = out_ref.shape[0] // 2
    chunks = half // size

    def copy(stream, at, source, target, device):
        return pltpu.make_async_remote_copy(
            src_ref=source, dst_ref=target, send_sem=send.at[stream, at],
            recv_sem=recv.at[stream, at], device_id={"tp": device}, device_id_type=MESH,
        )

    def ends(way):
        place = me if way == 1 else count - 1 - me
        return place, me + way

    def reduce_copy(way, at, device):
        index = 0 if way == 1 else 1
        rows = pl.ds(pl.multiple_of(at * size, size), size)
        return copy(index, at, slots.at[index, rows], slots.at[index, rows], device)

    def spread_copy(way, at, device):
        base = 0 if way == 1 else half
        rows = pl.ds(pl.multiple_of(base + at * size, size), size)
        return copy(2 if way == 1 else 3, at, out_ref.at[rows], out_ref.at[rows], device)

    def reduce_step(way, tick):
        place, ahead = ends(way)
        index = 0 if way == 1 else 1
        base = half if way == 1 else 0
        at = tick - place

        @pl.when((at >= 0) & (at < chunks))
        def _():
            local = pl.ds(pl.multiple_of(at * size, size), size)
            rows = pl.ds(pl.multiple_of(base + at * size, size), size)

            @pl.when(place == 0)
            def _():
                slots[index, local] = part_ref[rows]

            @pl.when(place > 0)
            def _():
                reduce_copy(way, at, ahead).wait_recv()

            @pl.when((place > 0) & (place < count - 1))
            def _():
                slots[index, local] = (
                    slots[index, local].astype(jnp.float32) + part_ref[rows].astype(jnp.float32)
                ).astype(jnp.bfloat16)

            @pl.when(place < count - 1)
            def _():
                reduce_copy(way, at, ahead).start()

            @pl.when(place == count - 1)
            def _():
                total = slots[index, local].astype(jnp.float32) + part_ref[rows].astype(jnp.float32)
                out_ref[rows] = finish(rows, total)
                spread_copy(-way, at, me - way).start()

    def spread_step(way, tick):
        place, ahead = ends(way)
        at = tick - (count - 1) - place

        @pl.when((at >= 0) & (at < chunks) & (place > 0))
        def _():
            spread_copy(way, at, ahead).wait_recv()

            @pl.when(place < count - 1)
            def _():
                spread_copy(way, at, ahead).start()

    def step(tick):
        for way in (1, -1):
            reduce_step(way, tick)
        for way in (1, -1):
            spread_step(way, tick)

    def drain():
        @pl.loop(0, chunks)
        def _(at):
            for way in (1, -1):
                place, ahead = ends(way)

                @pl.when(place < count - 1)
                def _():
                    reduce_copy(way, at, ahead).wait_send()
                    spread_copy(way, at, ahead).wait_send()

    return step, drain, chunks + 2 * (count - 1)


def chain(count, part_ref, out_ref, slots, send, recv, finish):
    step, drain, ticks = chain_parts(count, part_ref, out_ref, slots, send, recv, finish, CHUNK)
    pl.loop(0, ticks)(step)
    drain()


def unit_scale(stream):
    return lax.rsqrt(jnp.mean(stream * stream, axis=-1, keepdims=True) + norm_eps)


def fold(values):
    return values.reshape(-1, 8, values.shape[1]).sum(0)


def norm_back(stream, gain, upstream):
    scale = unit_scale(stream)
    gain_grad = fold(upstream * stream * scale)
    inner = jnp.sum(upstream * gain * stream, axis=-1, keepdims=True)
    grad = scale * gain * upstream - stream * (scale * scale * scale / stream.shape[-1]) * inner
    return grad, gain_grad


def middle_kernel(count, part_ref, tokens_ref, gain_ref, out_ref, middle_ref, slots, send, recv):
    greet(lax.axis_index("tp"), count)
    middle_ref[...] = jnp.zeros_like(middle_ref)

    def finish(rows, total):
        middle = tokens_ref[rows].astype(jnp.float32) + total
        middle_ref[rows] = middle
        return (middle * unit_scale(middle) * gain_ref[...]).astype(jnp.bfloat16)

    chain(count, part_ref, out_ref, slots, send, recv, finish)


def middle_back_kernel(
    count, part_ref, middle_ref, cotangent_ref, gain_ref, out_ref, grad_ref, gain_grad_ref, slots, send, recv
):
    greet(lax.axis_index("tp"), count)
    grad_ref[...] = jnp.zeros_like(grad_ref)
    gain_grad_ref[...] = jnp.zeros_like(gain_grad_ref)

    def finish(rows, total):
        grad, gain_grad = norm_back(middle_ref[rows], gain_ref[...], total)
        gain_grad_ref[...] += gain_grad
        grad = cotangent_ref[rows].astype(jnp.float32) + grad
        grad_ref[rows] = grad
        return grad.astype(jnp.bfloat16)

    chain(count, part_ref, out_ref, slots, send, recv, finish)


def input_back_kernel(
    count, part_ref, tokens_ref, grad_ref, gain_ref, out_ref, gain_grad_ref, slots, send, recv
):
    greet(lax.axis_index("tp"), count)
    gain_grad_ref[...] = jnp.zeros_like(gain_grad_ref)

    def finish(rows, total):
        grad, gain_grad = norm_back(tokens_ref[rows].astype(jnp.float32), gain_ref[...], total)
        gain_grad_ref[...] += gain_grad
        return (grad_ref[rows] + grad).astype(jnp.bfloat16)

    chain(count, part_ref, out_ref, slots, send, recv, finish)


def run_chain(kernel, name, number, count, inputs, extra):
    rows, width = inputs[0].shape
    vmem = pl.BlockSpec(memory_space=pltpu.VMEM)
    chunks = rows // 2 // CHUNK
    outs = (jax.ShapeDtypeStruct((rows, width), jnp.bfloat16),) + tuple(extra)
    return pl.pallas_call(
        functools.partial(kernel, count),
        out_shape=outs,
        in_specs=[vmem] * len(inputs),
        out_specs=(vmem,) * len(outs),
        scratch_shapes=[
            pltpu.VMEM((2, rows // 2, width), jnp.bfloat16),
            pltpu.SemaphoreType.DMA((4, chunks)),
            pltpu.SemaphoreType.DMA((4, chunks)),
        ],
        compiler_params=pltpu.CompilerParams(
            collective_id=number, has_side_effects=True, vmem_limit_bytes=56 * 2**20
        ),
        cost_estimate=pl.CostEstimate(
            flops=100 * 10**9, bytes_accessed=12 * rows * width, transcendentals=0
        ),
        name=name,
    )(*inputs)


def rotate_pairs(values, cosine, sine):
    parts = [
        rotate_lanes(values[:, at : at + PAIR], cosine, sine)
        for at in range(0, values.shape[1], PAIR)
    ]
    return jnp.concatenate(parts, 1)


def greet_partner(late):
    barrier = pltpu.get_barrier_semaphore()
    pl.semaphore_signal(barrier, inc=1, device_id={"ctx": 1 - late}, device_id_type=MESH)
    pl.semaphore_wait(barrier, 1)


def front_kernel(
    live_ref, tokens_ref, weight_ref, gain_ref, cos_ref, sin_ref,
    h_ref, q_ref, k_ref, v_ref, kp_ref, vp_ref, o_ref, l_ref, send, recv,
):
    late = lax.axis_index("ctx")
    rows, width = q_ref.shape
    block = min(BLOCK, rows)
    blocks = rows // block
    pairs = width // PAIR
    greet_partner(late)

    def here(at):
        return pl.ds(pl.multiple_of(at * block, block), block)

    def lanes(pair):
        return pl.ds(pl.multiple_of(pair * PAIR, PAIR), PAIR)

    @pl.loop(0, blocks)
    def _(at):
        stream = tokens_ref[here(at)].astype(jnp.float32)
        normed = (stream * unit_scale(stream) * gain_ref[...]).astype(jnp.bfloat16)
        h_ref[here(at)] = normed
        keys = dot(normed, weight_ref[1], (1, 0))
        k_ref[here(at)] = rotate_pairs(keys, cos_ref[here(at)], sin_ref[here(at)]).astype(jnp.bfloat16)
        v_ref[here(at)] = dot(normed, weight_ref[2], (1, 0)).astype(jnp.bfloat16)

    def exchange(pair):
        return [
            pltpu.make_async_remote_copy(
                src_ref=own.at[:, lanes(pair)], dst_ref=prev.at[:, lanes(pair)],
                send_sem=send.at[which, pair], recv_sem=recv.at[which, pair],
                device_id={"ctx": 1 - late}, device_id_type=MESH,
            )
            for which, own, prev in ((0, k_ref, kp_ref), (1, v_ref, vp_ref))
        ]

    @pl.when(late == 0)
    def _():
        @pl.loop(0, pairs)
        def _(pair):
            for copy in exchange(pair):
                copy.start()

    @pl.loop(0, blocks)
    def _(at):
        query = dot(h_ref[here(at)], weight_ref[0], (1, 0))
        query = rotate_pairs(query, cos_ref[here(at)], sin_ref[here(at)]) * 0.125
        q_ref[here(at)] = query.astype(jnp.bfloat16)

    def attend(pair, own, with_prev):
        column = lanes(pair)
        mine = slice(own * block, (own + 1) * block)
        query = q_ref[mine, column]
        mixed = []
        for head in range(2):
            queries = one_head(query, head)
            parts = []
            if with_prev:
                parts.append((dot(kp_ref[:, column], queries, (1, 1)), vp_ref[:, column]))
            if own:
                before = slice(0, own * block)
                parts.append((dot(k_ref[before, column], queries, (1, 1)), v_ref[before, column]))
            parts.append((causal(dot(k_ref[mine, column], queries, (1, 1))), v_ref[mine, column]))
            peak = parts[0][0].max(0, keepdims=True)
            for scores, _ in parts[1:]:
                peak = jnp.maximum(peak, scores.max(0, keepdims=True))
            expo = [jnp.exp(scores - peak) for scores, _ in parts]
            denom = expo[0].sum(0, keepdims=True)
            for e in expo[1:]:
                denom = denom + e.sum(0, keepdims=True)
            inverse = 1.0 / denom
            total = None
            for e, (_, value) in zip(expo, parts):
                term = dot(value, (e * inverse).astype(jnp.bfloat16), (0, 0))
                total = term if total is None else total + term
            mixed.append(total[head * HEAD : (head + 1) * HEAD])
            index = late * rows + own * block + lax.broadcasted_iota(jnp.int32, peak.shape, 1)
            l_ref[pair, head : head + 1, mine] = jnp.where(
                index < live_ref[0], peak + jnp.log(denom), -MASKED
            )
        result = jnp.concatenate(mixed, 0).T
        index = late * rows + own * block + lax.broadcasted_iota(jnp.int32, result.shape, 0)
        own_value = v_ref[mine, column].astype(jnp.float32)
        o_ref[mine, column] = jnp.where(index < live_ref[0], result, own_value).astype(jnp.bfloat16)

    @pl.loop(0, pairs)
    def _(pair):
        @pl.when(late == 0)
        def _():
            for own in range(blocks):
                attend(pair, own, False)

        @pl.when(late == 1)
        def _():
            for copy in exchange(pair):
                copy.wait_recv()
            for own in range(blocks):
                attend(pair, own, True)

    @pl.when(late == 0)
    def _():
        @pl.loop(0, pairs)
        def _(pair):
            for copy in exchange(pair):
                copy.wait_send()


VMEM_SPEC = pl.BlockSpec(memory_space=pltpu.VMEM)
SMEM_SPEC = pl.BlockSpec(memory_space=pltpu.SMEM)


def layer_front(live, tokens, weight, gain, cosine, sine):
    rows, depth = tokens.shape
    width = weight.shape[2]
    pairs = width // PAIR
    part = jax.ShapeDtypeStruct((rows, width), jnp.bfloat16)
    outs = (
        jax.ShapeDtypeStruct((rows, depth), jnp.bfloat16), part, part, part, part, part, part,
        jax.ShapeDtypeStruct((pairs, 2, rows), jnp.float32),
    )
    return pl.pallas_call(
        front_kernel,
        out_shape=outs,
        in_specs=[SMEM_SPEC] + [VMEM_SPEC] * 5,
        out_specs=(VMEM_SPEC,) * len(outs),
        scratch_shapes=[pltpu.SemaphoreType.DMA((2, pairs))] * 2,
        compiler_params=pltpu.CompilerParams(
            collective_id=4, has_side_effects=True, vmem_limit_bytes=56 * 2**20
        ),
        cost_estimate=pl.CostEstimate(
            flops=80 * 10**9, bytes_accessed=40 * 2**20, transcendentals=0
        ),
        name="layer_front",
    )(live, tokens, weight, gain, cosine, sine)


def attend_back_kernel(
    count, live_ref, q_ref, k_ref, v_ref, kp_ref, vp_ref, o_ref, do_ref, l_ref, cos_ref, sin_ref,
    part_ref, dq_ref, dk_ref, dv_ref, out_ref,
    dq_acc, dk_acc, dv_acc, dkp_acc, dvp_acc, leave, arrive, slots, send, recv, chain_send, chain_recv,
):
    late = lax.axis_index("ctx")
    me = lax.axis_index("tp")
    rows, width = q_ref.shape
    block = min(BLOCK, rows)
    blocks = rows // block
    pairs = width // PAIR
    barrier = pltpu.get_barrier_semaphore()
    pl.semaphore_signal(barrier, inc=1, device_id={"ctx": 1 - late}, device_id_type=MESH)
    greet(me, count, 1)
    tick, drain, ticks = chain_parts(
        count, part_ref, out_ref, slots, chain_send, chain_recv,
        lambda at, total: total.astype(jnp.bfloat16), 32,
    )

    def here(at):
        return pl.ds(pl.multiple_of(at * block, block), block)

    def lanes(pair):
        return pl.ds(pl.multiple_of(pair * PAIR, PAIR), PAIR)

    def prepare(pair, step):
        column = lanes(pair)
        query = q_ref[here(step), column]
        upstream = do_ref[here(step), column]
        product = (upstream.astype(jnp.float32) * o_ref[here(step), column].astype(jnp.float32)).T
        queries = [one_head(query, head) for head in range(2)]
        upstreams = [one_head(upstream, head) for head in range(2)]
        inner = [
            product[head * HEAD : (head + 1) * HEAD].sum(0, keepdims=True) for head in range(2)
        ]
        totals = [l_ref[pair, head : head + 1, here(step)] for head in range(2)]
        query_both = jnp.concatenate(queries, 0)
        upstream_both = jnp.concatenate(upstreams, 0)

        def tile(keys, values, masked):
            grads, probs_all, out = [], [], []
            for head in range(2):
                scores = dot(keys, queries[head], (1, 1))
                if masked:
                    scores = causal(scores)
                probs = jnp.exp(scores - totals[head])
                prob_grad = dot(values, upstreams[head], (1, 1))
                score_grad = (probs * (prob_grad - inner[head])).astype(jnp.bfloat16)
                probs_all.append(probs.astype(jnp.bfloat16))
                grads.append(score_grad)
                out.append(dot(keys, score_grad, (0, 0))[head * HEAD : (head + 1) * HEAD])
            key_grad = dot(jnp.concatenate(grads, 1), query_both, (1, 0))
            value_grad = dot(jnp.concatenate(probs_all, 1), upstream_both, (1, 0))
            return jnp.concatenate(out, 0), key_grad, value_grad

        return tile, upstream

    def exchange(pair):
        return pltpu.make_async_remote_copy(
            src_ref=leave.at[pair], dst_ref=arrive.at[pair], send_sem=send.at[pair],
            recv_sem=recv.at[pair], device_id={"ctx": 1 - late}, device_id_type=MESH,
        )

    def prev_step(pair, step):
        column = lanes(pair)
        tile, _ = prepare(pair, step)

        @pl.when(step == 0)
        def _():
            dkp_acc[...] = jnp.zeros_like(dkp_acc)
            dvp_acc[...] = jnp.zeros_like(dvp_acc)

        query_grad = None
        for at in range(blocks):
            mine = slice(at * block, (at + 1) * block)
            more, key_grad, value_grad = tile(kp_ref[mine, column], vp_ref[mine, column], False)
            query_grad = more if query_grad is None else query_grad + more
            dkp_acc[mine] += key_grad
            dvp_acc[mine] += value_grad
        dq_acc[pair, :, here(step)] = query_grad

        @pl.when(step == blocks - 1)
        def _():
            leave[pair, 0] = dkp_acc[...].astype(jnp.bfloat16)
            leave[pair, 1] = dvp_acc[...].astype(jnp.bfloat16)
            exchange(pair).start()

    def own_step(pair, step):
        column = lanes(pair)
        tile, upstream = prepare(pair, step)
        query_grad, key_grad, value_grad = tile(k_ref[here(step), column], v_ref[here(step), column], True)
        index = late * rows + step * block + lax.broadcasted_iota(jnp.int32, upstream.shape, 0)
        dk_acc[here(step), column] = key_grad
        dv_acc[here(step), column] = value_grad + jnp.where(
            index < live_ref[0], 0.0, upstream.astype(jnp.float32)
        )
        dq_acc[pair, :, here(step)] += query_grad

        @pl.loop(0, step)
        def _(at):
            more, key_grad, value_grad = tile(k_ref[here(at), column], v_ref[here(at), column], False)
            dk_acc[here(at), column] += key_grad
            dv_acc[here(at), column] += value_grad
            dq_acc[pair, :, here(step)] += more

        grad = dq_acc[pair, :, here(step)].T * 0.125
        grad = rotate_lanes(grad, cos_ref[here(step)], -sin_ref[here(step)])
        dq_ref[here(step), column] = grad.astype(jnp.bfloat16)

    @pl.when(late == 0)
    def _():
        dq_acc[...] = jnp.zeros_like(dq_acc)

    steps = pairs * blocks

    @pl.loop(0, 2 * steps)
    def _(at):
        @pl.when(at < ticks)
        def _():
            tick(at)

        @pl.when((late == 1) & (at < steps))
        def _():
            prev_step(at // blocks, at % blocks)

        @pl.when(at >= steps)
        def _():
            own_step((at - steps) // blocks, at % blocks)

    if ticks > 2 * steps:
        pl.loop(2 * steps, ticks)(tick)

    @pl.loop(0, pairs)
    def _(pair):
        column = lanes(pair)

        @pl.when(late == 0)
        def _():
            exchange(pair).wait_recv()
            dk_acc[:, column] += arrive[pair, 0].astype(jnp.float32)
            dv_acc[:, column] += arrive[pair, 1].astype(jnp.float32)

        @pl.when(late == 1)
        def _():
            exchange(pair).wait_send()

        dk_ref[:, column] = rotate_lanes(dk_acc[:, column], cos_ref[...], -sin_ref[...]).astype(
            jnp.bfloat16
        )
        dv_ref[:, column] = dv_acc[:, column].astype(jnp.bfloat16)

    drain()


def attend_back(live, arrays, cosine, sine, out_part, count):
    rows, width = arrays[0].shape
    pairs = width // PAIR
    part = jax.ShapeDtypeStruct((rows, width), jnp.bfloat16)
    outs = (part, part, part, jax.ShapeDtypeStruct(out_part.shape, jnp.bfloat16))
    chunks = rows // 2 // 32
    return pl.pallas_call(
        functools.partial(attend_back_kernel, count),
        out_shape=outs,
        in_specs=[SMEM_SPEC] + [VMEM_SPEC] * 11,
        out_specs=(VMEM_SPEC,) * len(outs),
        scratch_shapes=[
            pltpu.VMEM((pairs, PAIR, rows), jnp.float32),
            pltpu.VMEM((rows, width), jnp.float32),
            pltpu.VMEM((rows, width), jnp.float32),
            pltpu.VMEM((rows, PAIR), jnp.float32),
            pltpu.VMEM((rows, PAIR), jnp.float32),
            pltpu.VMEM((pairs, 2, rows, PAIR), jnp.bfloat16),
            pltpu.VMEM((pairs, 2, rows, PAIR), jnp.bfloat16),
            pltpu.VMEM((2, rows // 2, out_part.shape[1]), jnp.bfloat16),
            pltpu.SemaphoreType.DMA((pairs,)),
            pltpu.SemaphoreType.DMA((pairs,)),
            pltpu.SemaphoreType.DMA((4, chunks)),
            pltpu.SemaphoreType.DMA((4, chunks)),
        ],
        compiler_params=pltpu.CompilerParams(
            collective_id=5, has_side_effects=True, vmem_limit_bytes=58 * 2**20
        ),
        cost_estimate=pl.CostEstimate(
            flops=100 * 10**9, bytes_accessed=40 * 2**20, transcendentals=0
        ),
        name="attend_back",
    )(live, *arrays, cosine, sine, out_part)


def scatter_low(grad):
    return lax.psum_scatter(
        grad.astype(jnp.bfloat16), ("shard", "ctx"), scatter_dimension=1, tiled=True
    ).astype(jnp.float32)


def after(array, *others):
    return lax.optimization_barrier((array, *others))[0]


def adam_update(weight, first, second, grad, decay):
    first_new = beta_one * first + (1.0 - beta_one) * grad
    second_new = beta_two * second + (1.0 - beta_two) * grad * grad
    first_hat = first_new / (1.0 - beta_one**step_count)
    second_hat = second_new / (1.0 - beta_two**step_count)
    update = learn_rate * (first_hat / (jnp.sqrt(second_hat) + adam_eps) + decay * weight)
    return (update, first_new, second_new)


def body(
    tokens,
    cotangent,
    lengths,
    qkv_weight,
    out_weight,
    gate_up_weight,
    down_weight,
    norm_gains,
    qkv_first,
    out_first,
    gate_up_first,
    down_first,
    gains_first,
    qkv_second,
    out_second,
    gate_up_second,
    down_second,
    gains_second,
):
    row_count = tokens.shape[0]
    count = lax.axis_size("tp")
    offset = lax.axis_index("ctx") * row_count
    query_index = offset + jnp.arange(row_count, dtype=jnp.int32)
    qkv_low = qkv_weight.astype(jnp.bfloat16)
    out_low = out_weight.astype(jnp.bfloat16)
    gate_up_low = gate_up_weight.astype(jnp.bfloat16)
    down_low = down_weight.astype(jnp.bfloat16)
    gains_low = norm_gains.astype(jnp.bfloat16)
    qkv_full, out_full, gate_up_full, down_full, gains_full = (
        lax.all_gather(qkv_low, ("shard", "ctx"), axis=1, tiled=True),
        lax.all_gather(out_low, ("shard", "ctx"), axis=1, tiled=True),
        lax.all_gather(gate_up_low, ("shard", "ctx"), axis=1, tiled=True),
        lax.all_gather(down_low, ("shard", "ctx"), axis=1, tiled=True),
        lax.all_gather(gains_low, ("shard", "ctx"), axis=1, tiled=True),
    )
    gain_one = gains_full[0:1].astype(jnp.float32)
    gain_two = gains_full[1:2].astype(jnp.float32)
    cosine, sine = rotation(query_index, HEAD)
    cosine, sine = (jnp.concatenate([c[:, 0]] * 4, 1) for c in (cosine, sine))
    normed_one, query, keys, values, keys_prev, values_prev, mixed_low, totals = layer_front(
        lengths, tokens, qkv_full, gain_one, cosine, sine
    )
    attn_part = jnp.dot(mixed_low, out_full, preferred_element_type=jnp.float32)
    whole = jax.ShapeDtypeStruct(attn_part.shape, jnp.float32)
    eight = jax.ShapeDtypeStruct((8, attn_part.shape[1]), jnp.float32)
    normed_two, middle = run_chain(
        middle_kernel, "sum_middle", 1, count,
        [attn_part.astype(jnp.bfloat16), tokens, gain_two], [whole],
    )
    gate = jnp.dot(normed_two, gate_up_full[0], preferred_element_type=jnp.float32)
    upward = jnp.dot(normed_two, gate_up_full[1], preferred_element_type=jnp.float32)
    sigma = jax.nn.sigmoid(gate)
    swish = gate * sigma
    hidden = (swish * upward).astype(jnp.bfloat16)
    mlp_part = jnp.dot(hidden, down_full, preferred_element_type=jnp.float32)
    out_part = (middle + mlp_part).astype(jnp.bfloat16)
    down_grad_local = outer_sum(hidden, cotangent).astype(jnp.bfloat16)
    hidden_grad = back_dot(cotangent, down_full)
    gate_grad = (hidden_grad * upward * sigma * (1.0 + gate * (1.0 - sigma))).astype(jnp.bfloat16)
    upward_grad = (hidden_grad * swish).astype(jnp.bfloat16)
    gate_up_grad_local = jnp.stack(
        [outer_sum(normed_two, gate_grad), outer_sum(normed_two, upward_grad)]
    ).astype(jnp.bfloat16)
    mlp_back_part = (
        back_dot(gate_grad, gate_up_full[0]) + back_dot(upward_grad, gate_up_full[1])
    ).astype(jnp.bfloat16)
    mlp_back_part, down_grad_local, gate_up_grad_local, out_part = lax.optimization_barrier(
        (mlp_back_part, down_grad_local, gate_up_grad_local, out_part)
    )
    down_grad = scatter_low(down_grad_local)
    middle_low, middle_grad, gain_two_grad = run_chain(
        middle_back_kernel, "sum_middle_back", 2, count,
        [mlp_back_part, middle, cotangent, gain_two], [whole, eight],
    )
    gate_up_grad = scatter_low(after(gate_up_grad_local, down_grad, middle_low))
    out_grad_local = outer_sum(mixed_low, middle_low).astype(jnp.bfloat16)
    mixed_grad = back_dot(middle_low, out_full).astype(jnp.bfloat16)
    query_low, key_low, value_low, out_tokens = attend_back(
        lengths,
        [query, keys, values, keys_prev, values_prev, mixed_low, mixed_grad, totals],
        cosine, sine, out_part, count,
    )
    qkv_grad_local = jnp.stack(
        [
            outer_sum(normed_one, query_low),
            outer_sum(normed_one, key_low),
            outer_sum(normed_one, value_low),
        ]
    ).astype(jnp.bfloat16)
    attn_back_part = (
        back_dot(query_low, qkv_full[0])
        + back_dot(key_low, qkv_full[1])
        + back_dot(value_low, qkv_full[2])
    ).astype(jnp.bfloat16)
    attn_back_part, qkv_grad_local, out_grad_local, _ = lax.optimization_barrier(
        (attn_back_part, qkv_grad_local, out_grad_local, gate_up_grad)
    )
    out_grad = scatter_low(out_grad_local)
    qkv_grad = scatter_low(after(qkv_grad_local, out_grad))
    input_grad, gain_one_grad = run_chain(
        input_back_kernel, "sum_input_back", 3, count,
        [attn_back_part, tokens, middle_grad, gain_one], [eight],
    )
    gains_local = lax.psum(
        jnp.stack([gain_one_grad.sum(0), gain_two_grad.sum(0)]), ("shard", "ctx", "tp")
    )
    gains_grad = lax.dynamic_slice_in_dim(
        gains_local, lax.axis_index(("shard", "ctx")) * norm_gains.shape[1], norm_gains.shape[1], 1
    )
    qkv_step, qkv_first_new, qkv_second_new = adam_update(
        qkv_weight, qkv_first, qkv_second, qkv_grad, decay_rate
    )
    out_step, out_first_new, out_second_new = adam_update(
        out_weight, out_first, out_second, out_grad, decay_rate
    )
    gate_up_step, gate_up_first_new, gate_up_second_new = adam_update(
        gate_up_weight, gate_up_first, gate_up_second, gate_up_grad, decay_rate
    )
    down_step, down_first_new, down_second_new = adam_update(
        down_weight, down_first, down_second, down_grad, decay_rate
    )
    gains_step, gains_first_new, gains_second_new = adam_update(
        norm_gains, gains_first, gains_second, gains_grad, 0.0
    )
    qkv_new = qkv_weight - qkv_step
    gate_up_new = gate_up_weight - gate_up_step
    down_new = down_weight - down_step
    return (
        out_tokens,
        input_grad,
        qkv_grad,
        out_grad,
        gate_up_grad,
        down_grad,
        gains_grad,
        qkv_new,
        out_step,
        gate_up_new,
        down_new,
        gains_step,
        qkv_first_new,
        out_first_new,
        gate_up_first_new,
        down_first_new,
        gains_first_new,
        qkv_second_new,
        out_second_new,
        gate_up_second_new,
        down_second_new,
        gains_second_new,
    )


def solution(mesh):
    return jax.shard_map(
        body,
        mesh=mesh,
        in_specs=(
            P(("shard", "ctx"), None),
            P(("shard", "ctx"), None),
            P("shard"),
            P(None, ("shard", "ctx"), "tp"),
            P("tp", ("shard", "ctx")),
            P(None, ("shard", "ctx"), "tp"),
            P("tp", ("shard", "ctx")),
            P(None, ("shard", "ctx")),
            P(None, ("shard", "ctx"), "tp"),
            P("tp", ("shard", "ctx")),
            P(None, ("shard", "ctx"), "tp"),
            P("tp", ("shard", "ctx")),
            P(None, ("shard", "ctx")),
            P(None, ("shard", "ctx"), "tp"),
            P("tp", ("shard", "ctx")),
            P(None, ("shard", "ctx"), "tp"),
            P("tp", ("shard", "ctx")),
            P(None, ("shard", "ctx")),
        ),
        out_specs=(
            P(("shard", "ctx"), None),
            P(("shard", "ctx"), None),
            P(None, ("shard", "ctx"), "tp"),
            P("tp", ("shard", "ctx")),
            P(None, ("shard", "ctx"), "tp"),
            P("tp", ("shard", "ctx")),
            P(None, ("shard", "ctx")),
            P(None, ("shard", "ctx"), "tp"),
            P("tp", ("shard", "ctx")),
            P(None, ("shard", "ctx"), "tp"),
            P("tp", ("shard", "ctx")),
            P(None, ("shard", "ctx")),
            P(None, ("shard", "ctx"), "tp"),
            P("tp", ("shard", "ctx")),
            P(None, ("shard", "ctx"), "tp"),
            P("tp", ("shard", "ctx")),
            P(None, ("shard", "ctx")),
            P(None, ("shard", "ctx"), "tp"),
            P("tp", ("shard", "ctx")),
            P(None, ("shard", "ctx"), "tp"),
            P("tp", ("shard", "ctx")),
            P(None, ("shard", "ctx")),
        ),
        check_vma=False,
    )
```

```python
import functools
import jax
import jax.numpy as jnp
from jax import lax
from jax.experimental import pallas as pl
from jax.experimental.pallas import tpu as pltpu
from jax.sharding import PartitionSpec as P

HEAD = 64
PAIR = 128
BLOCK = 256
CHUNK = 16
LAG = 2
BACK_CHUNK = 16
BACK_LAG = 4
WIDE = 256
BACK_TICKS = 2
SPACING = 5
MASKED = -1e30
MESH = pl.DeviceIdType.MESH
VMEM_SPEC = pl.BlockSpec(memory_space=pltpu.VMEM)
SMEM_SPEC = pl.BlockSpec(memory_space=pltpu.SMEM)


norm_eps = 1e-05
rope_base = 130000.0
beta_one = 0.9
beta_two = 0.95
learn_rate = 0.02
decay_rate = 0.1
adam_eps = 1e-08
step_count = 4.0


def rotation(position, head_size):
    half = head_size // 2
    freqs = rope_base ** (-(jnp.arange(half, dtype=jnp.float32) * 2.0) / head_size)
    angle = position.astype(jnp.float32)[:, None] * freqs[None, :]
    return (jnp.cos(angle)[:, None, :], jnp.sin(angle)[:, None, :])


def back_dot(grad, weight):
    return lax.dot_general(
        grad, weight, (((1,), (1,)), ((), ())), preferred_element_type=jnp.float32
    )


def dot(left, right, contract):
    return lax.dot_general(
        left, right, ((contract[:1], contract[1:]), ((), ())), preferred_element_type=jnp.float32
    )


def one_head(values, head):
    lane = lax.broadcasted_iota(jnp.int32, values.shape, 1)
    return jnp.where((lane < HEAD) == (head == 0), values, jnp.zeros_like(values))


def causal(scores):
    key = lax.broadcasted_iota(jnp.int32, scores.shape, 0)
    query = lax.broadcasted_iota(jnp.int32, scores.shape, 1)
    return jnp.where(key <= query, scores, MASKED)


def rotate_lanes(values, cosine, sine):
    lane = lax.broadcasted_iota(jnp.int32, values.shape, 1) % HEAD
    width = values.shape[1]
    ahead = pltpu.roll(values, width - HEAD // 2, 1)
    behind = pltpu.roll(values, HEAD // 2, 1)
    return values * cosine + jnp.where(lane < HEAD // 2, -ahead, behind) * sine


def greet(me, count, more=0, more_ends=0):
    barrier = pltpu.get_barrier_semaphore()

    @pl.when(me > 0)
    def _():
        pl.semaphore_signal(barrier, inc=1, device_id={"tp": me - 1}, device_id_type=MESH)

    @pl.when(me < count - 1)
    def _():
        pl.semaphore_signal(barrier, inc=1, device_id={"tp": me + 1}, device_id_type=MESH)

    @pl.when((me > 0) & (me < count - 1))
    def _():
        pl.semaphore_wait(barrier, 2 + more)

    @pl.when((me == 0) | (me == count - 1))
    def _():
        pl.semaphore_wait(barrier, 1 + more + more_ends)


def chain_parts(count, part_ref, out_ref, slots, send, recv, finish, size, lag=1, land=None):
    me = lax.axis_index("tp")
    apart = land is not None
    land = land if apart else out_ref
    half = out_ref.shape[0] // 2
    chunks = half // size

    def copy(stream, at, source, target, device):
        return pltpu.make_async_remote_copy(
            src_ref=source, dst_ref=target, send_sem=send.at[stream, at],
            recv_sem=recv.at[stream, at], device_id={"tp": device}, device_id_type=MESH,
        )

    def ends(way):
        place = me if way == 1 else count - 1 - me
        return place, me + way

    def reduce_copy(way, at, device):
        index = 0 if way == 1 else 1
        rows = pl.ds(pl.multiple_of(at * size, size), size)
        return copy(index, at, slots.at[index, rows], slots.at[index, rows], device)

    def spread_copy(way, at, device):
        base = 0 if way == 1 else half
        rows = pl.ds(pl.multiple_of(base + at * size, size), size)
        return copy(2 if way == 1 else 3, at, land.at[rows], land.at[rows], device)

    def reduce_step(way, tick):
        place, ahead = ends(way)
        index = 0 if way == 1 else 1
        base = half if way == 1 else 0
        at = tick - lag * place

        @pl.when((at >= 0) & (at < chunks))
        def _():
            local = pl.ds(pl.multiple_of(at * size, size), size)
            rows = pl.ds(pl.multiple_of(base + at * size, size), size)

            @pl.when(place == 0)
            def _():
                slots[index, local] = part_ref[rows]

            @pl.when(place > 0)
            def _():
                reduce_copy(way, at, ahead).wait_recv()

            @pl.when((place > 0) & (place < count - 1))
            def _():
                slots[index, local] = (
                    slots[index, local].astype(jnp.float32) + part_ref[rows].astype(jnp.float32)
                ).astype(jnp.bfloat16)

            @pl.when(place < count - 1)
            def _():
                reduce_copy(way, at, ahead).start()

            @pl.when(place == count - 1)
            def _():
                total = slots[index, local].astype(jnp.float32) + part_ref[rows].astype(jnp.float32)
                land[rows] = finish(rows, local, total)
                if apart:
                    out_ref[rows] = land[rows]
                spread_copy(-way, at, me - way).start()

    def spread_step(way, tick):
        place, ahead = ends(way)
        at = tick - lag * (count - 1) - lag * place

        @pl.when((at >= 0) & (at < chunks) & (place > 0))
        def _():
            spread_copy(way, at, ahead).wait_recv()

            @pl.when(place < count - 1)
            def _():
                spread_copy(way, at, ahead).start()

            if apart:
                base = 0 if way == 1 else half
                rows = pl.ds(pl.multiple_of(base + at * size, size), size)
                out_ref[rows] = land[rows]

    def step(tick):
        for way in (1, -1):
            reduce_step(way, tick)
        for way in (1, -1):
            spread_step(way, tick)

    def drain():
        @pl.loop(0, chunks)
        def _(at):
            for way in (1, -1):
                place, ahead = ends(way)

                @pl.when(place < count - 1)
                def _():
                    reduce_copy(way, at, ahead).wait_send()
                    spread_copy(way, at, ahead).wait_send()

    return step, drain, chunks + 2 * lag * (count - 1)


def run_ticks(parts, start):
    step, drain, ticks = parts
    tick = pl.program_id(0)
    pl.when(tick == 0)(start)
    step(tick)
    pl.when(tick == ticks - 1)(drain)
    return tick


def tick_count(rows, count):
    return rows // 2 // CHUNK + 2 * LAG * (count - 1)


def unit_scale(stream):
    return lax.rsqrt(jnp.mean(stream * stream, axis=-1, keepdims=True) + norm_eps)


def fold(values):
    return values.reshape(-1, 8, values.shape[1]).sum(0)


def norm_back(stream, gain, upstream):
    scale = unit_scale(stream)
    gain_grad = fold(upstream * stream * scale)
    inner = jnp.sum(upstream * gain * stream, axis=-1, keepdims=True)
    grad = scale * gain * upstream - stream * (scale * scale * scale / stream.shape[-1]) * inner
    return grad, gain_grad


def middle_kernel(
    count, blocks, mixed_ref, weight_ref, tokens_ref, gain_ref, cotangent_ref, down_ref,
    out_ref, middle_ref, hidden_grad_ref, slots, land, part_ref, send, recv,
):
    def start():
        greet(lax.axis_index("tp"), count)

        @pl.loop(0, part_ref.shape[0] // BLOCK)
        def _(at):
            here = pl.ds(pl.multiple_of(at * BLOCK, BLOCK), BLOCK)
            part_ref[here] = dot(mixed_ref[here], weight_ref[...], (1, 0)).astype(jnp.bfloat16)

    def finish(rows, local, total):
        middle = tokens_ref[rows].astype(jnp.float32) + total
        middle_ref[local] = middle
        return (middle * unit_scale(middle) * gain_ref[...]).astype(jnp.bfloat16)

    parts = chain_parts(count, part_ref, out_ref, slots, send, recv, finish, CHUNK, LAG, land)
    tick = run_ticks(parts, start)

    @pl.when((tick % SPACING == 1) & (tick < blocks * SPACING))
    def _():
        hidden_grad_ref[...] = dot(cotangent_ref[...], down_ref[...], (1, 1))


def middle_back_kernel(
    count, part_ref, middle_ref, cotangent_ref, gain_ref, hidden_ref, down_ref,
    out_ref, grad_ref, gain_grad_ref, layer_ref, slots, land, send, recv,
):
    def start():
        greet(lax.axis_index("tp"), count)
        gain_grad_ref[...] = jnp.zeros_like(gain_grad_ref)

    def finish(rows, local, total):
        grad, gain_grad = norm_back(middle_ref[local], gain_ref[...], total)
        gain_grad_ref[...] += gain_grad
        grad = cotangent_ref[rows].astype(jnp.float32) + grad
        grad_ref[local] = grad
        return grad.astype(jnp.bfloat16)

    parts = chain_parts(count, part_ref, out_ref, slots, send, recv, finish, CHUNK, LAG, land)
    tick = run_ticks(parts, start)

    @pl.when((tick % SPACING == 1) & (tick < part_ref.shape[1] // WIDE * SPACING))
    def _():
        skip = down_ref.shape[0] - hidden_ref.shape[1]
        layer_ref[...] = dot(hidden_ref[...], down_ref[skip:], (1, 0)).astype(jnp.bfloat16)


def input_back_kernel(
    count, part_ref, tokens_ref, grad_ref, gain_ref, other_ref,
    out_ref, gains_ref, slots, land, local, landed, along, send, recv, plane_send, plane_recv, line_send, line_recv,
):
    me = lax.axis_index("tp")
    size, index, peer = plane_peers()
    width = gains_ref.shape[1]
    last = (me == 0) | (me == count - 1)

    def start():
        @pl.when(last)
        def _():
            greet_plane(size, peer)

        greet(me, count, 0, size - 1)
        local[0:8] = jnp.zeros((8, local.shape[1]), jnp.float32)
        local[8:16] = other_ref[...]

    def finish(rows, part, total):
        grad, gain_grad = norm_back(tokens_ref[rows].astype(jnp.float32), gain_ref[...], total)
        local[0:8] += gain_grad
        return (grad_ref[part] + grad).astype(jnp.bfloat16)

    step, drain, ticks = chain_parts(
        count, part_ref, out_ref, slots, send, recv, finish, CHUNK, LAG, land
    )

    def columns(at):
        return pl.ds(pl.multiple_of(at * width, width), width)

    def plane_copy(distance):
        at, device = peer(distance)
        return pltpu.make_async_remote_copy(
            src_ref=local.at[:, columns(at)], dst_ref=landed.at[distance],
            send_sem=plane_send.at[distance], recv_sem=plane_recv.at[distance],
            device_id=device, device_id_type=MESH,
        )

    def line_copy(way):
        which = 0 if way == 1 else 1
        return pltpu.make_async_remote_copy(
            src_ref=along.at[which], dst_ref=along.at[which],
            send_sem=line_send.at[which], recv_sem=line_recv.at[which],
            device_id={"tp": me + way}, device_id_type=MESH,
        )

    done = out_ref.shape[0] // 2 // CHUNK + LAG * (count - 1)

    tick = pl.program_id(0)
    pl.when(tick == 0)(start)
    step(tick)

    @pl.when(last & (tick == done - 1))
    def _():
        for distance in range(1, size):
            plane_copy(distance).start()

    @pl.when(last & (tick == done + LAG))
    def _():
        total = local[:, columns(index)]
        for distance in range(1, size):
            plane_copy(distance).wait()
            total = total + landed[distance]

        @pl.when(me == 0)
        def _():
            along[0] = total
            line_copy(1).start()

        @pl.when(me == count - 1)
        def _():
            along[1] = total
            line_copy(-1).start()

    @pl.when(tick == ticks - 1)
    def _():
        for way in (1, -1):
            place = me if way == 1 else count - 1 - me

            @pl.when(place > 0)
            def _():
                line_copy(way).wait_recv()

            @pl.when((place > 0) & (place < count - 1))
            def _():
                line_copy(way).start()

        for way in (1, -1):
            place = me if way == 1 else count - 1 - me

            @pl.when(place < count - 1)
            def _():
                line_copy(way).wait_send()

        sums = along[0] + along[1]
        gains_ref[0:1] = sums[0:8].sum(0, keepdims=True)
        gains_ref[1:2] = sums[8:16].sum(0, keepdims=True)
        drain()


def chain_call(kernel, name, number, count, shape, inputs, outs, scratch):
    rows, width = shape
    chunks = rows // 2 // CHUNK
    arrays, in_specs = zip(*inputs)
    out_shape, out_specs = zip(*outs)
    return pl.pallas_call(
        kernel,
        out_shape=out_shape,
        grid=(tick_count(rows, count),),
        in_specs=in_specs,
        out_specs=out_specs,
        scratch_shapes=[
            pltpu.VMEM((2, rows // 2, width), jnp.bfloat16),
            pltpu.VMEM((rows, width), jnp.bfloat16),
            *scratch[:3],
            pltpu.SemaphoreType.DMA((4, chunks)),
            pltpu.SemaphoreType.DMA((4, chunks)),
            *scratch[3:],
        ],
        compiler_params=pltpu.CompilerParams(
            collective_id=number, has_side_effects=True, vmem_limit_bytes=60 * 2**20
        ),
        cost_estimate=pl.CostEstimate(
            flops=100 * 10**9, bytes_accessed=12 * rows * width, transcendentals=0
        ),
        name=name,
    )(*arrays)


def kept(shape, dtype):
    return jax.ShapeDtypeStruct(shape, dtype), VMEM_SPEC


def sum_middle(mixed, both, tokens, gain, cotangent, count):
    rows, width = tokens.shape
    inner = mixed.shape[1]
    hidden = both.shape[0] - inner
    last = hidden // WIDE - 1
    at = lambda i: jnp.minimum(i // SPACING, last)
    return chain_call(
        functools.partial(middle_kernel, count, last + 1), "sum_middle", 1, count, tokens.shape,
        [
            (mixed, VMEM_SPEC),
            (both, pl.BlockSpec((inner, width), lambda i: (0, 0), pipeline_mode=pl.Buffered(1))),
            (tokens, VMEM_SPEC), (gain, VMEM_SPEC), (cotangent, VMEM_SPEC),
            (both, pl.BlockSpec((WIDE, width), lambda i: (inner // WIDE + at(i), 0))),
        ],
        [
            kept(tokens.shape, jnp.bfloat16),
            kept((rows // 2, width), jnp.float32),
            (
                jax.ShapeDtypeStruct((rows, hidden), jnp.float32),
                pl.BlockSpec((rows, WIDE), lambda i: (0, at(i))),
            ),
        ],
        [pltpu.VMEM(tokens.shape, jnp.bfloat16)],
    )


def sum_middle_back(part, middle, cotangent, gain, hidden, both, count):
    rows, width = part.shape
    last = width // WIDE - 1
    at = lambda i: jnp.minimum(i // SPACING, last)
    return chain_call(
        functools.partial(middle_back_kernel, count), "sum_middle_back", 2, count, part.shape,
        [
            (part, VMEM_SPEC), (middle, VMEM_SPEC), (cotangent, VMEM_SPEC), (gain, VMEM_SPEC),
            (hidden, VMEM_SPEC), (both, pl.BlockSpec((both.shape[0], WIDE), lambda i: (0, at(i)))),
        ],
        [
            kept(part.shape, jnp.bfloat16),
            kept((rows // 2, width), jnp.float32),
            kept((8, width), jnp.float32),
            (
                jax.ShapeDtypeStruct(part.shape, jnp.bfloat16),
                pl.BlockSpec((rows, WIDE), lambda i: (0, at(i))),
            ),
        ],
        [],
    )


def sum_input_back(part, tokens, grad, gain, other, size, count):
    width = part.shape[1]
    plane = width // size
    return chain_call(
        functools.partial(input_back_kernel, count), "sum_input_back", 3, count, part.shape,
        [(a, VMEM_SPEC) for a in (part, tokens, grad, gain, other)],
        [kept(part.shape, jnp.bfloat16), kept((2, size), jnp.float32)],
        [
            pltpu.VMEM((16, width), jnp.float32),
            pltpu.VMEM((plane, 16, size), jnp.float32),
            pltpu.VMEM((2, 16, size), jnp.float32),
            pltpu.SemaphoreType.DMA((plane,)),
            pltpu.SemaphoreType.DMA((plane,)),
            pltpu.SemaphoreType.DMA((2,)),
            pltpu.SemaphoreType.DMA((2,)),
        ],
    )


def rotate_pairs(values, cosine, sine):
    parts = [
        rotate_lanes(values[:, at : at + PAIR], cosine, sine)
        for at in range(0, values.shape[1], PAIR)
    ]
    return jnp.concatenate(parts, 1)


def plane_peers():
    ctx = lax.axis_size("ctx")
    size = lax.axis_size("shard") * ctx
    mine = lax.axis_index("shard") * ctx + lax.axis_index("ctx")

    def peer(distance):
        index = lax.rem(mine + distance, size)
        return index, {"shard": index // ctx, "ctx": lax.rem(index, ctx)}

    return size, mine, peer


def greet_plane(size, peer):
    barrier = pltpu.get_barrier_semaphore()
    for distance in range(1, size):
        pl.semaphore_signal(barrier, inc=1, device_id=peer(distance)[1], device_id_type=MESH)


def front_kernel(
    live_ref, tokens_ref, weight_ref, own_gain_ref, cos_ref, sin_ref,
    h_ref, q_ref, k_ref, v_ref, kp_ref, vp_ref, o_ref, l_ref, gain_ref,
    send, recv, gain_send, gain_recv,
):
    late = lax.axis_index("ctx")
    rows, width = q_ref.shape
    block = min(BLOCK, rows)
    blocks = rows // block
    pairs = width // PAIR
    size, index, peer = plane_peers()
    part = own_gain_ref.shape[1]
    greet_plane(size, peer)
    pl.semaphore_wait(pltpu.get_barrier_semaphore(), size - 1)
    mine = pl.ds(pl.multiple_of(index * part, part), part)
    gain_ref[:, mine] = own_gain_ref[...]

    def gain_copy(distance):
        return pltpu.make_async_remote_copy(
            src_ref=own_gain_ref, dst_ref=gain_ref.at[:, mine],
            send_sem=gain_send.at[distance], recv_sem=gain_recv.at[distance],
            device_id=peer(distance)[1], device_id_type=MESH,
        )

    for distance in range(1, size):
        gain_copy(distance).start()
    for distance in range(1, size):
        gain_copy(distance).wait()

    def here(at):
        return pl.ds(pl.multiple_of(at * block, block), block)

    def lanes(pair):
        return pl.ds(pl.multiple_of(pair * PAIR, PAIR), PAIR)

    @pl.loop(0, blocks)
    def _(at):
        stream = tokens_ref[here(at)].astype(jnp.float32)
        normed = (stream * unit_scale(stream) * gain_ref[0:1]).astype(jnp.bfloat16)
        h_ref[here(at)] = normed
        keys = dot(normed, weight_ref[1], (1, 0))
        k_ref[here(at)] = rotate_pairs(keys, cos_ref[here(at)], sin_ref[here(at)]).astype(jnp.bfloat16)
        v_ref[here(at)] = dot(normed, weight_ref[2], (1, 0)).astype(jnp.bfloat16)

    def exchange(pair):
        return [
            pltpu.make_async_remote_copy(
                src_ref=own.at[:, lanes(pair)], dst_ref=prev.at[:, lanes(pair)],
                send_sem=send.at[which, pair], recv_sem=recv.at[which, pair],
                device_id={"ctx": 1 - late}, device_id_type=MESH,
            )
            for which, own, prev in ((0, k_ref, kp_ref), (1, v_ref, vp_ref))
        ]

    @pl.when(late == 0)
    def _():
        @pl.loop(0, pairs)
        def _(pair):
            for copy in exchange(pair):
                copy.start()

    @pl.loop(0, blocks)
    def _(at):
        query = dot(h_ref[here(at)], weight_ref[0], (1, 0))
        query = rotate_pairs(query, cos_ref[here(at)], sin_ref[here(at)]) * 0.125
        q_ref[here(at)] = query.astype(jnp.bfloat16)

    def attend(pair, own, with_prev):
        column = lanes(pair)
        mine = slice(own * block, (own + 1) * block)
        query = q_ref[mine, column]
        mixed = []
        for head in range(2):
            queries = one_head(query, head)
            parts = []
            if with_prev:
                parts.append((dot(kp_ref[:, column], queries, (1, 1)), vp_ref[:, column]))
            if own:
                before = slice(0, own * block)
                parts.append((dot(k_ref[before, column], queries, (1, 1)), v_ref[before, column]))
            parts.append((causal(dot(k_ref[mine, column], queries, (1, 1))), v_ref[mine, column]))
            peak = parts[0][0].max(0, keepdims=True)
            for scores, _ in parts[1:]:
                peak = jnp.maximum(peak, scores.max(0, keepdims=True))
            expo = [jnp.exp(scores - peak) for scores, _ in parts]
            denom = expo[0].sum(0, keepdims=True)
            for e in expo[1:]:
                denom = denom + e.sum(0, keepdims=True)
            inverse = 1.0 / denom
            total = None
            for e, (_, value) in zip(expo, parts):
                term = dot(value, (e * inverse).astype(jnp.bfloat16), (0, 0))
                total = term if total is None else total + term
            mixed.append(total[head * HEAD : (head + 1) * HEAD])
            index = late * rows + own * block + lax.broadcasted_iota(jnp.int32, peak.shape, 1)
            l_ref[pair, head : head + 1, mine] = jnp.where(
                index < live_ref[0], peak + jnp.log(denom), -MASKED
            )
        result = jnp.concatenate(mixed, 0).T
        index = late * rows + own * block + lax.broadcasted_iota(jnp.int32, result.shape, 0)
        own_value = v_ref[mine, column].astype(jnp.float32)
        o_ref[mine, column] = jnp.where(index < live_ref[0], result, own_value).astype(jnp.bfloat16)

    @pl.loop(0, pairs)
    def _(pair):
        @pl.when(late == 0)
        def _():
            for own in range(blocks):
                attend(pair, own, False)

        @pl.when(late == 1)
        def _():
            for copy in exchange(pair):
                copy.wait_recv()
            for own in range(blocks):
                attend(pair, own, True)

    @pl.when(late == 0)
    def _():
        @pl.loop(0, pairs)
        def _(pair):
            for copy in exchange(pair):
                copy.wait_send()


def layer_front(live, tokens, weight, gain, cosine, sine):
    rows, depth = tokens.shape
    width = weight.shape[2]
    pairs = width // PAIR
    part = jax.ShapeDtypeStruct((rows, width), jnp.bfloat16)
    outs = (
        jax.ShapeDtypeStruct((rows, depth), jnp.bfloat16), part, part, part, part, part, part,
        jax.ShapeDtypeStruct((pairs, 2, rows), jnp.float32),
        jax.ShapeDtypeStruct((8, depth), jnp.float32),
    )
    size = lax.axis_size("shard") * lax.axis_size("ctx")
    return pl.pallas_call(
        front_kernel,
        out_shape=outs,
        in_specs=[SMEM_SPEC] + [VMEM_SPEC] * 5,
        out_specs=(VMEM_SPEC,) * len(outs),
        scratch_shapes=[pltpu.SemaphoreType.DMA((2, pairs))] * 2
        + [pltpu.SemaphoreType.DMA((size,))] * 2,
        compiler_params=pltpu.CompilerParams(
            collective_id=4, has_side_effects=True, vmem_limit_bytes=56 * 2**20
        ),
        cost_estimate=pl.CostEstimate(
            flops=80 * 10**9, bytes_accessed=40 * 2**20, transcendentals=0
        ),
        name="layer_front",
    )(live, tokens, weight, gain, cosine, sine)


def attend_back_kernel(
    count, live_ref, q_ref, k_ref, v_ref, kp_ref, vp_ref, o_ref, do_ref, l_ref, cos_ref, sin_ref,
    part_ref, middle_ref, dq_ref, dk_ref, dv_ref, out_ref,
    dq_acc, dk_acc, dv_acc, dkp_acc, dvp_acc, leave, arrive, slots, send, recv, chain_send, chain_recv,
):
    late = lax.axis_index("ctx")
    me = lax.axis_index("tp")
    rows, width = q_ref.shape
    block = min(BLOCK, rows)
    blocks = rows // block
    pairs = width // PAIR
    barrier = pltpu.get_barrier_semaphore()
    pl.semaphore_signal(barrier, inc=1, device_id={"ctx": 1 - late}, device_id_type=MESH)
    greet(me, count, 1)
    tick, drain, ticks = chain_parts(
        count, part_ref, out_ref, slots, chain_send, chain_recv,
        lambda rows, part, total: (middle_ref[part] + total).astype(jnp.bfloat16), BACK_CHUNK, BACK_LAG,
    )

    def here(at):
        return pl.ds(pl.multiple_of(at * block, block), block)

    def lanes(pair):
        return pl.ds(pl.multiple_of(pair * PAIR, PAIR), PAIR)

    def prepare(pair, step):
        column = lanes(pair)
        query = q_ref[here(step), column]
        upstream = do_ref[here(step), column]
        product = (upstream.astype(jnp.float32) * o_ref[here(step), column].astype(jnp.float32)).T
        queries = [one_head(query, head) for head in range(2)]
        upstreams = [one_head(upstream, head) for head in range(2)]
        inner = [
            product[head * HEAD : (head + 1) * HEAD].sum(0, keepdims=True) for head in range(2)
        ]
        totals = [l_ref[pair, head : head + 1, here(step)] for head in range(2)]
        query_both = jnp.concatenate(queries, 0)
        upstream_both = jnp.concatenate(upstreams, 0)

        def tile(keys, values, masked):
            grads, probs_all, out = [], [], []
            for head in range(2):
                scores = dot(keys, queries[head], (1, 1))
                if masked:
                    scores = causal(scores)
                probs = jnp.exp(scores - totals[head])
                prob_grad = dot(values, upstreams[head], (1, 1))
                score_grad = (probs * (prob_grad - inner[head])).astype(jnp.bfloat16)
                probs_all.append(probs.astype(jnp.bfloat16))
                grads.append(score_grad)
                out.append(dot(keys, score_grad, (0, 0))[head * HEAD : (head + 1) * HEAD])
            key_grad = dot(jnp.concatenate(grads, 1), query_both, (1, 0))
            value_grad = dot(jnp.concatenate(probs_all, 1), upstream_both, (1, 0))
            return jnp.concatenate(out, 0), key_grad, value_grad

        return tile, upstream

    def exchange(pair):
        return pltpu.make_async_remote_copy(
            src_ref=leave.at[pair], dst_ref=arrive.at[pair], send_sem=send.at[pair],
            recv_sem=recv.at[pair], device_id={"ctx": 1 - late}, device_id_type=MESH,
        )

    def prev_step(pair, step):
        column = lanes(pair)
        tile, _ = prepare(pair, step)

        @pl.when(step == 0)
        def _():
            dkp_acc[...] = jnp.zeros_like(dkp_acc)
            dvp_acc[...] = jnp.zeros_like(dvp_acc)

        query_grad = None
        for at in range(blocks):
            mine = slice(at * block, (at + 1) * block)
            more, key_grad, value_grad = tile(kp_ref[mine, column], vp_ref[mine, column], False)
            query_grad = more if query_grad is None else query_grad + more
            dkp_acc[mine] += key_grad
            dvp_acc[mine] += value_grad
        dq_acc[pair, :, here(step)] = query_grad

        @pl.when(step == blocks - 1)
        def _():
            leave[pair, 0] = dkp_acc[...].astype(jnp.bfloat16)
            leave[pair, 1] = dvp_acc[...].astype(jnp.bfloat16)
            exchange(pair).start()

    def own_step(pair, step):
        column = lanes(pair)
        tile, upstream = prepare(pair, step)
        query_grad, key_grad, value_grad = tile(k_ref[here(step), column], v_ref[here(step), column], True)
        index = late * rows + step * block + lax.broadcasted_iota(jnp.int32, upstream.shape, 0)
        dk_acc[here(step), column] = key_grad
        dv_acc[here(step), column] = value_grad + jnp.where(
            index < live_ref[0], 0.0, upstream.astype(jnp.float32)
        )
        dq_acc[pair, :, here(step)] += query_grad

        @pl.loop(0, step)
        def _(at):
            more, key_grad, value_grad = tile(k_ref[here(at), column], v_ref[here(at), column], False)
            dk_acc[here(at), column] += key_grad
            dv_acc[here(at), column] += value_grad
            dq_acc[pair, :, here(step)] += more

        grad = dq_acc[pair, :, here(step)].T * 0.125
        grad = rotate_lanes(grad, cos_ref[here(step)], -sin_ref[here(step)])
        dq_ref[here(step), column] = grad.astype(jnp.bfloat16)

    @pl.when(late == 0)
    def _():
        dq_acc[...] = jnp.zeros_like(dq_acc)

    steps = pairs * blocks

    @pl.loop(0, 2 * steps)
    def _(at):
        for more in range(BACK_TICKS):

            @pl.when(at * BACK_TICKS + more < ticks)
            def _():
                tick(at * BACK_TICKS + more)

        @pl.when((late == 1) & (at < steps))
        def _():
            prev_step(at // blocks, at % blocks)

        @pl.when(at >= steps)
        def _():
            own_step((at - steps) // blocks, at % blocks)

    if ticks > 2 * steps * BACK_TICKS:
        pl.loop(2 * steps * BACK_TICKS, ticks)(tick)

    @pl.loop(0, pairs)
    def _(pair):
        column = lanes(pair)

        @pl.when(late == 0)
        def _():
            exchange(pair).wait_recv()
            dk_acc[:, column] += arrive[pair, 0].astype(jnp.float32)
            dv_acc[:, column] += arrive[pair, 1].astype(jnp.float32)

        @pl.when(late == 1)
        def _():
            exchange(pair).wait_send()

        dk_ref[:, column] = rotate_lanes(dk_acc[:, column], cos_ref[...], -sin_ref[...]).astype(
            jnp.bfloat16
        )
        dv_ref[:, column] = dv_acc[:, column].astype(jnp.bfloat16)

    drain()


def attend_back(live, arrays, cosine, sine, out_part, middle, count):
    rows, width = arrays[0].shape
    pairs = width // PAIR
    part = jax.ShapeDtypeStruct((rows, width), jnp.bfloat16)
    outs = (part, part, part, jax.ShapeDtypeStruct(out_part.shape, jnp.bfloat16))
    chunks = rows // 2 // BACK_CHUNK
    return pl.pallas_call(
        functools.partial(attend_back_kernel, count),
        out_shape=outs,
        in_specs=[SMEM_SPEC] + [VMEM_SPEC] * 12,
        out_specs=(VMEM_SPEC,) * len(outs),
        scratch_shapes=[
            pltpu.VMEM((pairs, PAIR, rows), jnp.float32),
            pltpu.VMEM((rows, width), jnp.float32),
            pltpu.VMEM((rows, width), jnp.float32),
            pltpu.VMEM((rows, PAIR), jnp.float32),
            pltpu.VMEM((rows, PAIR), jnp.float32),
            pltpu.VMEM((pairs, 2, rows, PAIR), jnp.bfloat16),
            pltpu.VMEM((pairs, 2, rows, PAIR), jnp.bfloat16),
            pltpu.VMEM((2, rows // 2, out_part.shape[1]), jnp.bfloat16),
            pltpu.SemaphoreType.DMA((pairs,)),
            pltpu.SemaphoreType.DMA((pairs,)),
            pltpu.SemaphoreType.DMA((4, chunks)),
            pltpu.SemaphoreType.DMA((4, chunks)),
        ],
        compiler_params=pltpu.CompilerParams(
            collective_id=5, has_side_effects=True, vmem_limit_bytes=58 * 2**20
        ),
        cost_estimate=pl.CostEstimate(
            flops=100 * 10**9, bytes_accessed=40 * 2**20, transcendentals=0
        ),
        name="attend_back",
    )(live, *arrays, cosine, sine, out_part, middle)


def mlp_kernel(
    normed_ref, weight_ref, hidden_grad_ref, cotangent_ref,
    hidden_ref, down_grad_ref, gate_up_grad_ref, back_ref, turned, total,
):
    step = pl.program_id(0)

    @pl.when(step == 0)
    def _():
        turned[...] = normed_ref[...].T
        total[...] = jnp.zeros_like(total)

    gate = dot(normed_ref[...], weight_ref[0], (1, 0))
    upward = dot(normed_ref[...], weight_ref[1], (1, 0))
    hidden_grad = hidden_grad_ref[...]
    sigma = jax.nn.sigmoid(gate)
    swish = gate * sigma
    hidden = (swish * upward).astype(jnp.bfloat16)
    hidden_ref[...] = hidden
    gate_grad = (hidden_grad * upward * sigma * (1.0 + gate * (1.0 - sigma))).astype(jnp.bfloat16)
    upward_grad = (hidden_grad * swish).astype(jnp.bfloat16)
    both = jnp.concatenate([gate_grad, upward_grad], 1)
    weights = jnp.concatenate([weight_ref[0], weight_ref[1]], 1)
    total[...] += dot(both, weights, (1, 1))
    gate_up_grad_ref[0] = dot(turned[...], gate_grad, (1, 0)).astype(jnp.bfloat16)
    gate_up_grad_ref[1] = dot(turned[...], upward_grad, (1, 0)).astype(jnp.bfloat16)
    down_grad_ref[...] = dot(hidden.T, cotangent_ref[...], (1, 0)).astype(jnp.bfloat16)

    @pl.when(step == pl.num_programs(0) - 1)
    def _():
        back_ref[...] = total[...].astype(jnp.bfloat16)


def mlp(normed, weight, hidden_grad, cotangent):
    rows, depth = normed.shape
    width = weight.shape[2]
    whole = pl.BlockSpec((rows, depth), lambda j: (0, 0), pipeline_mode=pl.Buffered(1))
    return pl.pallas_call(
        mlp_kernel,
        out_shape=(
            jax.ShapeDtypeStruct((rows, width), jnp.bfloat16),
            jax.ShapeDtypeStruct((width, depth), jnp.bfloat16),
            jax.ShapeDtypeStruct((2, depth, width), jnp.bfloat16),
            jax.ShapeDtypeStruct((rows, depth), jnp.bfloat16),
        ),
        grid=(width // WIDE,),
        in_specs=[
            whole,
            pl.BlockSpec((2, depth, WIDE), lambda j: (0, 0, j)),
            pl.BlockSpec((rows, WIDE), lambda j: (0, j)),
            whole,
        ],
        out_specs=(
            pl.BlockSpec((rows, WIDE), lambda j: (0, j)),
            pl.BlockSpec((WIDE, depth), lambda j: (j, 0)),
            pl.BlockSpec((2, depth, WIDE), lambda j: (0, 0, j)),
            pl.BlockSpec((rows, depth), lambda j: (0, 0)),
        ),
        scratch_shapes=[
            pltpu.VMEM((depth, rows), jnp.bfloat16), pltpu.VMEM((rows, depth), jnp.float32),
        ],
        compiler_params=pltpu.CompilerParams(vmem_limit_bytes=60 * 2**20),
        cost_estimate=pl.CostEstimate(
            flops=14 * rows * depth * width, bytes_accessed=80 * 2**20, transcendentals=rows * width
        ),
        name="mlp",
    )(normed, weight, hidden_grad, cotangent)


def projection_back_kernel(
    normed_ref, weight_ref, dq_ref, dk_ref, dv_ref, mixed_ref, middle_ref, grad_ref, back_ref,
    turned, total,
):
    step = pl.program_id(0)

    @pl.when(step == 0)
    def _():
        turned[...] = normed_ref[...].T

    for at, ref in enumerate((dq_ref, dk_ref, dv_ref)):

        @pl.when(step == at)
        def _():
            term = dot(ref[...], weight_ref[0], (1, 1))
            if at == 0:
                total[...] = term
            elif at == 1:
                total[...] += term
            else:
                back_ref[...] = (total[...] + term).astype(jnp.bfloat16)
            grad_ref[0] = dot(turned[...], ref[...], (1, 0)).astype(jnp.bfloat16)

    @pl.when(step == 3)
    def _():
        turned[...] = middle_ref[...].T
        grad_ref[0] = dot(turned[...], mixed_ref[...], (1, 0)).astype(jnp.bfloat16)


def projection_back(normed, weight, dq, dk, dv, mixed, middle):
    rows, depth = normed.shape
    width = dq.shape[1]
    whole = lambda w: pl.BlockSpec((rows, w), lambda j: (0, 0), pipeline_mode=pl.Buffered(1))
    return pl.pallas_call(
        projection_back_kernel,
        out_shape=(
            jax.ShapeDtypeStruct((4, depth, width), jnp.bfloat16),
            jax.ShapeDtypeStruct((rows, depth), jnp.bfloat16),
        ),
        grid=(4,),
        in_specs=[
            whole(depth),
            pl.BlockSpec((1, depth, width), lambda j: (jnp.minimum(j, 2), 0, 0)),
            whole(width), whole(width), whole(width), whole(width), whole(depth),
        ],
        out_specs=(
            pl.BlockSpec((1, depth, width), lambda j: (j, 0, 0)),
            pl.BlockSpec((rows, depth), lambda j: (0, 0)),
        ),
        scratch_shapes=[
            pltpu.VMEM((depth, rows), jnp.bfloat16), pltpu.VMEM((rows, depth), jnp.float32),
        ],
        compiler_params=pltpu.CompilerParams(vmem_limit_bytes=60 * 2**20),
        cost_estimate=pl.CostEstimate(
            flops=14 * rows * depth * width, bytes_accessed=40 * 2**20, transcendentals=0
        ),
        name="projection_back",
    )(normed, weight, dq, dk, dv, mixed, middle)


def scatter_low(grad, axis=1):
    return lax.psum_scatter(
        grad.astype(jnp.bfloat16), ("shard", "ctx"), scatter_dimension=axis, tiled=True
    ).astype(jnp.float32)


def after(array, *others):
    return lax.optimization_barrier((array, *others))[0]


def adam_update(weight, first, second, grad, decay):
    first_new = beta_one * first + (1.0 - beta_one) * grad
    second_new = beta_two * second + (1.0 - beta_two) * grad * grad
    first_hat = first_new / (1.0 - beta_one**step_count)
    second_hat = second_new / (1.0 - beta_two**step_count)
    update = learn_rate * (first_hat / (jnp.sqrt(second_hat) + adam_eps) + decay * weight)
    return (update, first_new, second_new)


def body(
    tokens,
    cotangent,
    lengths,
    qkv_weight,
    out_weight,
    gate_up_weight,
    down_weight,
    norm_gains,
    qkv_first,
    out_first,
    gate_up_first,
    down_first,
    gains_first,
    qkv_second,
    out_second,
    gate_up_second,
    down_second,
    gains_second,
):
    row_count = tokens.shape[0]
    count = lax.axis_size("tp")
    offset = lax.axis_index("ctx") * row_count
    query_index = offset + jnp.arange(row_count, dtype=jnp.int32)
    qkv_low = qkv_weight.astype(jnp.bfloat16)
    out_low = out_weight.astype(jnp.bfloat16)
    gate_up_low = gate_up_weight.astype(jnp.bfloat16)
    down_low = down_weight.astype(jnp.bfloat16)
    gains_low = norm_gains.astype(jnp.bfloat16).astype(jnp.float32)
    gains_low = jnp.concatenate([gains_low] * 4, 0)
    gather = lambda a: lax.all_gather(a, ("shard", "ctx"), axis=1, tiled=True)
    qkv_full = gather(qkv_low)
    both_full = gather(after(jnp.concatenate([out_low, down_low], 0), qkv_full))
    cosine, sine = rotation(query_index, HEAD)
    cosine, sine = (jnp.concatenate([c[:, 0]] * 4, 1) for c in (cosine, sine))
    normed_one, query, keys, values, keys_prev, values_prev, mixed_low, totals, gains_full = layer_front(
        lengths, tokens, qkv_full, gains_low, cosine, sine
    )
    gain_one, gain_two = gains_full[0:1], gains_full[1:2]
    gate_up_full = gather(after(gate_up_low, both_full, totals))
    normed_two, middle, hidden_grad = sum_middle(
        mixed_low, both_full, tokens, gain_two, cotangent, count
    )
    hidden, down_grad_local, gate_up_grad_local, mlp_back_part = mlp(
        normed_two, gate_up_full, hidden_grad, cotangent
    )
    gate_up_grad = scatter_low(gate_up_grad_local)
    middle_low, middle_grad, gain_two_grad, out_part = sum_middle_back(
        mlp_back_part, middle, cotangent, gain_two, hidden, both_full, count
    )
    down_grad = scatter_low(after(down_grad_local, gate_up_grad, middle_low))
    mixed_grad = back_dot(middle_low, both_full[: mixed_low.shape[1]]).astype(jnp.bfloat16)
    query_low, key_low, value_low, out_tokens = attend_back(
        lengths,
        [query, keys, values, keys_prev, values_prev, mixed_low, mixed_grad, totals],
        cosine, sine, out_part, middle, count,
    )
    qkv_grad_local, attn_back_part = projection_back(
        normed_one, qkv_full, query_low, key_low, value_low, mixed_low, middle_low
    )
    attn_back_part, qkv_grad_local, _ = lax.optimization_barrier(
        (attn_back_part, qkv_grad_local, down_grad)
    )
    qkv_grad = scatter_low(qkv_grad_local)
    out_grad = qkv_grad[3].T
    qkv_grad = qkv_grad[:3]
    input_grad, gains_grad = sum_input_back(
        attn_back_part, tokens, middle_grad, gain_one, gain_two_grad, norm_gains.shape[1], count
    )
    qkv_step, qkv_first_new, qkv_second_new = adam_update(
        qkv_weight, qkv_first, qkv_second, qkv_grad, decay_rate
    )
    out_step, out_first_new, out_second_new = adam_update(
        out_weight, out_first, out_second, out_grad, decay_rate
    )
    gate_up_step, gate_up_first_new, gate_up_second_new = adam_update(
        gate_up_weight, gate_up_first, gate_up_second, gate_up_grad, decay_rate
    )
    down_step, down_first_new, down_second_new = adam_update(
        down_weight, down_first, down_second, down_grad, decay_rate
    )
    gains_step, gains_first_new, gains_second_new = adam_update(
        norm_gains, gains_first, gains_second, gains_grad, 0.0
    )
    qkv_new = qkv_weight - qkv_step
    gate_up_new = gate_up_weight - gate_up_step
    down_new = down_weight - down_step
    return (
        out_tokens,
        input_grad,
        qkv_grad,
        out_grad,
        gate_up_grad,
        down_grad,
        gains_grad,
        qkv_new,
        out_step,
        gate_up_new,
        down_new,
        gains_step,
        qkv_first_new,
        out_first_new,
        gate_up_first_new,
        down_first_new,
        gains_first_new,
        qkv_second_new,
        out_second_new,
        gate_up_second_new,
        down_second_new,
        gains_second_new,
    )


def solution(mesh):
    return jax.shard_map(
        body,
        mesh=mesh,
        in_specs=(
            P(("shard", "ctx"), None),
            P(("shard", "ctx"), None),
            P("shard"),
            P(None, ("shard", "ctx"), "tp"),
            P("tp", ("shard", "ctx")),
            P(None, ("shard", "ctx"), "tp"),
            P("tp", ("shard", "ctx")),
            P(None, ("shard", "ctx")),
            P(None, ("shard", "ctx"), "tp"),
            P("tp", ("shard", "ctx")),
            P(None, ("shard", "ctx"), "tp"),
            P("tp", ("shard", "ctx")),
            P(None, ("shard", "ctx")),
            P(None, ("shard", "ctx"), "tp"),
            P("tp", ("shard", "ctx")),
            P(None, ("shard", "ctx"), "tp"),
            P("tp", ("shard", "ctx")),
            P(None, ("shard", "ctx")),
        ),
        out_specs=(
            P(("shard", "ctx"), None),
            P(("shard", "ctx"), None),
            P(None, ("shard", "ctx"), "tp"),
            P("tp", ("shard", "ctx")),
            P(None, ("shard", "ctx"), "tp"),
            P("tp", ("shard", "ctx")),
            P(None, ("shard", "ctx")),
            P(None, ("shard", "ctx"), "tp"),
            P("tp", ("shard", "ctx")),
            P(None, ("shard", "ctx"), "tp"),
            P("tp", ("shard", "ctx")),
            P(None, ("shard", "ctx")),
            P(None, ("shard", "ctx"), "tp"),
            P("tp", ("shard", "ctx")),
            P(None, ("shard", "ctx"), "tp"),
            P("tp", ("shard", "ctx")),
            P(None, ("shard", "ctx")),
            P(None, ("shard", "ctx"), "tp"),
            P("tp", ("shard", "ctx")),
            P(None, ("shard", "ctx"), "tp"),
            P("tp", ("shard", "ctx")),
            P(None, ("shard", "ctx")),
        ),
        check_vma=False,
    )
```

```python
import functools
import jax
import jax.numpy as jnp
from jax import lax
from jax.experimental import pallas as pl
from jax.experimental.pallas import tpu as pltpu
from jax.sharding import PartitionSpec as P

HEAD = 64
PAIR = 128
BLOCK = 256
CHUNK = 16
LAG = 2
BACK_CHUNK = 32
BACK_LAG = 3
WIDE = 256
SPACING = 5
LEAD = 1
MLP_WIDE = 256
MASKED = -1e30
MESH = pl.DeviceIdType.MESH
VMEM_SPEC = pl.BlockSpec(memory_space=pltpu.VMEM)
SMEM_SPEC = pl.BlockSpec(memory_space=pltpu.SMEM)
HBM_SPEC = pl.BlockSpec(memory_space=pl.ANY)


norm_eps = 1e-05
rope_base = 130000.0
beta_one = 0.9
beta_two = 0.95
learn_rate = 0.02
decay_rate = 0.1
adam_eps = 1e-08
step_count = 4.0


def rotation(position, head_size):
    half = head_size // 2
    freqs = rope_base ** (-(jnp.arange(half, dtype=jnp.float32) * 2.0) / head_size)
    angle = position.astype(jnp.float32)[:, None] * freqs[None, :]
    return (jnp.cos(angle)[:, None, :], jnp.sin(angle)[:, None, :])


def dot(left, right, contract):
    return lax.dot_general(
        left, right, ((contract[:1], contract[1:]), ((), ())), preferred_element_type=jnp.float32
    )


def one_head(values, head):
    lane = lax.broadcasted_iota(jnp.int32, values.shape, 1)
    return jnp.where((lane < HEAD) == (head == 0), values, jnp.zeros_like(values))


def causal(scores):
    key = lax.broadcasted_iota(jnp.int32, scores.shape, 0)
    query = lax.broadcasted_iota(jnp.int32, scores.shape, 1)
    return jnp.where(key <= query, scores, MASKED)


def rotate_lanes(values, cosine, sine):
    lane = lax.broadcasted_iota(jnp.int32, values.shape, 1) % HEAD
    width = values.shape[1]
    ahead = pltpu.roll(values, width - HEAD // 2, 1)
    behind = pltpu.roll(values, HEAD // 2, 1)
    return values * cosine + jnp.where(lane < HEAD // 2, -ahead, behind) * sine


def greet(me, count, more=0, more_ends=0):
    barrier = pltpu.get_barrier_semaphore()

    @pl.when(me > 0)
    def _():
        pl.semaphore_signal(barrier, inc=1, device_id={"tp": me - 1}, device_id_type=MESH)

    @pl.when(me < count - 1)
    def _():
        pl.semaphore_signal(barrier, inc=1, device_id={"tp": me + 1}, device_id_type=MESH)

    @pl.when((me > 0) & (me < count - 1))
    def _():
        pl.semaphore_wait(barrier, 2 + more)

    @pl.when((me == 0) | (me == count - 1))
    def _():
        pl.semaphore_wait(barrier, 1 + more + more_ends)


def chain_parts(count, part_ref, out_ref, slots, send, recv, finish, size, lag=1, land=None, stored=None):
    me = lax.axis_index("tp")
    apart = land is not None
    land = land if apart else out_ref
    half = out_ref.shape[0] // 2
    chunks = half // size

    def copy(stream, at, source, target, device):
        return pltpu.make_async_remote_copy(
            src_ref=source, dst_ref=target, send_sem=send.at[stream, at],
            recv_sem=recv.at[stream, at], device_id={"tp": device}, device_id_type=MESH,
        )

    def ends(way):
        place = me if way == 1 else count - 1 - me
        return place, me + way

    def reduce_copy(way, at, device):
        index = 0 if way == 1 else 1
        rows = pl.ds(pl.multiple_of(at * size, size), size)
        return copy(index, at, slots.at[index, rows], slots.at[index, rows], device)

    def spread_copy(way, at, device):
        base = 0 if way == 1 else half
        rows = pl.ds(pl.multiple_of(base + at * size, size), size)
        return copy(2 if way == 1 else 3, at, land.at[rows], land.at[rows], device)

    def store_copy(index, at):
        rows = pl.ds(pl.multiple_of(index * half + at * size, size), size)
        return pltpu.make_async_copy(land.at[rows], out_ref.at[rows], stored.at[index, at])

    def reduce_step(way, tick):
        place, ahead = ends(way)
        index = 0 if way == 1 else 1
        base = half if way == 1 else 0
        at = tick - lag * place

        @pl.when((at >= 0) & (at < chunks))
        def _():
            local = pl.ds(pl.multiple_of(at * size, size), size)
            rows = pl.ds(pl.multiple_of(base + at * size, size), size)

            @pl.when(place == 0)
            def _():
                slots[index, local] = part_ref[rows]

            @pl.when(place > 0)
            def _():
                reduce_copy(way, at, ahead).wait_recv()

            @pl.when((place > 0) & (place < count - 1))
            def _():
                slots[index, local] = (
                    slots[index, local].astype(jnp.float32) + part_ref[rows].astype(jnp.float32)
                ).astype(jnp.bfloat16)

            @pl.when(place < count - 1)
            def _():
                reduce_copy(way, at, ahead).start()

            @pl.when(place == count - 1)
            def _():
                total = slots[index, local].astype(jnp.float32) + part_ref[rows].astype(jnp.float32)
                land[rows] = finish(rows, local, total, at)
                if apart:
                    store_copy(1 if way == 1 else 0, at).start()
                spread_copy(-way, at, me - way).start()

    def spread_step(way, tick):
        place, ahead = ends(way)
        at = tick - lag * (count - 1) - lag * place

        @pl.when((at >= 0) & (at < chunks) & (place > 0))
        def _():
            spread_copy(way, at, ahead).wait_recv()

            @pl.when(place < count - 1)
            def _():
                spread_copy(way, at, ahead).start()

            if apart:
                store_copy(0 if way == 1 else 1, at).start()

    def step(tick):
        for way in (1, -1):
            reduce_step(way, tick)
        for way in (1, -1):
            spread_step(way, tick)

    def drain():
        @pl.loop(0, chunks)
        def _(at):
            if apart:
                for index in range(2):
                    store_copy(index, at).wait()

            for way in (1, -1):
                place, ahead = ends(way)

                @pl.when(place < count - 1)
                def _():
                    reduce_copy(way, at, ahead).wait_send()
                    spread_copy(way, at, ahead).wait_send()

    return step, drain, chunks + 2 * lag * (count - 1)


def run_ticks(parts, start, wait, finally_drain):
    step, drain, ticks = parts
    tick = pl.program_id(0)
    pl.when(tick == 0)(start)
    pl.when(tick == SPACING - 2)(wait)
    step(tick)

    @pl.when(tick == ticks - 1)
    def _():
        drain()
        finally_drain()

    return tick


def tick_count(rows, count):
    return rows // 2 // CHUNK + 2 * LAG * (count - 1)


def unit_scale(stream):
    return lax.rsqrt(jnp.mean(stream * stream, axis=-1, keepdims=True) + norm_eps)


def fold(values):
    return values.reshape(-1, 8, values.shape[1]).sum(0)


def norm_back(stream, gain, upstream):
    scale = unit_scale(stream)
    gain_grad = fold(upstream * stream * scale)
    inner = jnp.sum(upstream * gain * stream, axis=-1, keepdims=True)
    grad = scale * gain * upstream - stream * (scale * scale * scale / stream.shape[-1]) * inner
    return grad, gain_grad


def loads_of(pairs, sems):
    copies = [
        pltpu.make_async_copy(source, target, sems.at[at])
        for at, (source, target) in enumerate(pairs)
    ]

    def start():
        for copy in copies:
            copy.start()

    def wait():
        for copy in copies:
            copy.wait()

    return start, wait


def half_store(source, target, sems, count):
    chunks = source.shape[0] // CHUNK
    me = lax.axis_index("tp")

    def copy(at):
        rows = pl.ds(pl.multiple_of(at * CHUNK, CHUNK), CHUNK)
        return pltpu.make_async_copy(source.at[rows], target.at[rows], sems.at[at])

    def drain():
        @pl.when((me == 0) | (me == count - 1))
        def _():
            @pl.loop(0, chunks)
            def _(at):
                copy(at).wait()

    return copy, drain


def middle_kernel(
    count, blocks, mixed_ref, weight_ref, tokens_hbm, gain_ref, cotangent_hbm, down_ref,
    out_ref, middle_ref, hidden_grad_ref,
    slots, land, send, recv, stored, part_ref, tokens_ref, cotangent_ref, middle, load_sem, half_sem,
):
    load, wait = loads_of([(tokens_hbm, tokens_ref), (cotangent_hbm, cotangent_ref)], load_sem)
    half_copy, half_drain = half_store(middle, middle_ref, half_sem, count)

    def start():
        load()
        greet(lax.axis_index("tp"), count)

        @pl.loop(0, part_ref.shape[0] // BLOCK)
        def _(at):
            here = pl.ds(pl.multiple_of(at * BLOCK, BLOCK), BLOCK)
            part_ref[here] = dot(mixed_ref[here], weight_ref[...], (1, 0)).astype(jnp.bfloat16)

    def finish(rows, local, total, at):
        value = tokens_ref[rows].astype(jnp.float32) + total
        middle[local] = value
        half_copy(at).start()
        return (value * unit_scale(value) * gain_ref[...]).astype(jnp.bfloat16)

    parts = chain_parts(
        count, part_ref, out_ref, slots, send, recv, finish, CHUNK, LAG, land, stored
    )
    tick = run_ticks(parts, start, wait, half_drain)

    @pl.when((tick % SPACING == SPACING - 1) & (tick < blocks * SPACING))
    def _():
        hidden_grad_ref[...] = dot(cotangent_ref[...], down_ref[...], (1, 1))


def middle_back_kernel(
    count, part_ref, middle_hbm, cotangent_hbm, gain_ref, hidden_hbm, down_ref,
    out_ref, grad_ref, gain_grad_ref, layer_ref,
    slots, land, send, recv, stored, middle_ref, cotangent_ref, hidden_ref, grad, load_sem, half_sem,
):
    load, wait = loads_of(
        [(middle_hbm, middle_ref), (cotangent_hbm, cotangent_ref), (hidden_hbm, hidden_ref)],
        load_sem,
    )
    half_copy, half_drain = half_store(grad, grad_ref, half_sem, count)

    def start():
        load()
        greet(lax.axis_index("tp"), count)
        gain_grad_ref[...] = jnp.zeros_like(gain_grad_ref)

    def finish(rows, local, total, at):
        value, gain_grad = norm_back(middle_ref[local], gain_ref[...], total)
        gain_grad_ref[...] += gain_grad
        value = cotangent_ref[rows].astype(jnp.float32) + value
        grad[local] = value
        half_copy(at).start()
        return value.astype(jnp.bfloat16)

    parts = chain_parts(
        count, part_ref, out_ref, slots, send, recv, finish, CHUNK, LAG, land, stored
    )
    tick = run_ticks(parts, start, wait, half_drain)

    @pl.when((tick % SPACING == SPACING - 1) & (tick < part_ref.shape[1] // WIDE * SPACING))
    def _():
        skip = down_ref.shape[0] - hidden_ref.shape[1]
        layer_ref[...] = dot(hidden_ref[...], down_ref[skip:], (1, 0)).astype(jnp.bfloat16)


def input_back_kernel(
    count, part_ref, tokens_hbm, grad_hbm, gain_ref, other_ref, out_ref, gains_ref,
    slots, land, send, recv, stored, tokens_ref, grad_ref, local, landed, along,
    load_sem, plane_send, plane_recv, line_send, line_recv,
):
    load, wait = loads_of([(tokens_hbm, tokens_ref), (grad_hbm, grad_ref)], load_sem)

    me = lax.axis_index("tp")
    size, index, peer = plane_peers()
    width = gains_ref.shape[1]
    last = (me == 0) | (me == count - 1)

    def start():
        load()

        @pl.when(last)
        def _():
            greet_plane(size, peer)

        greet(me, count, 0, size - 1)
        local[0:8] = jnp.zeros((8, local.shape[1]), jnp.float32)
        local[8:16] = other_ref[...]

    def finish(rows, part, total, at):
        grad, gain_grad = norm_back(tokens_ref[rows].astype(jnp.float32), gain_ref[...], total)
        local[0:8] += gain_grad
        return (grad_ref[part] + grad).astype(jnp.bfloat16)

    step, drain, ticks = chain_parts(
        count, part_ref, out_ref, slots, send, recv, finish, CHUNK, LAG, land, stored
    )

    def columns(at):
        return pl.ds(pl.multiple_of(at * width, width), width)

    def plane_copy(distance):
        at, device = peer(distance)
        return pltpu.make_async_remote_copy(
            src_ref=local.at[:, columns(at)], dst_ref=landed.at[distance],
            send_sem=plane_send.at[distance], recv_sem=plane_recv.at[distance],
            device_id=device, device_id_type=MESH,
        )

    def line_copy(way):
        which = 0 if way == 1 else 1
        return pltpu.make_async_remote_copy(
            src_ref=along.at[which], dst_ref=along.at[which],
            send_sem=line_send.at[which], recv_sem=line_recv.at[which],
            device_id={"tp": me + way}, device_id_type=MESH,
        )

    done = out_ref.shape[0] // 2 // CHUNK + LAG * (count - 1)

    tick = pl.program_id(0)
    pl.when(tick == 0)(start)
    pl.when(tick == SPACING - 2)(wait)
    step(tick)

    @pl.when(last & (tick == done - 1))
    def _():
        for distance in range(1, size):
            plane_copy(distance).start()

    @pl.when(last & (tick == done + LAG))
    def _():
        total = local[:, columns(index)]
        for distance in range(1, size):
            plane_copy(distance).wait()
            total = total + landed[distance]

        @pl.when(me == 0)
        def _():
            along[0] = total
            line_copy(1).start()

        @pl.when(me == count - 1)
        def _():
            along[1] = total
            line_copy(-1).start()

    for way in (1, -1):
        place = me if way == 1 else count - 1 - me

        @pl.when((place > 0) & (tick == jnp.minimum(done + LAG + place, ticks - 1)))
        def _():
            line_copy(way).wait_recv()

            @pl.when(place < count - 1)
            def _():
                line_copy(way).start()

    @pl.when(tick == ticks - 1)
    def _():
        for way in (1, -1):
            place = me if way == 1 else count - 1 - me

            @pl.when(place < count - 1)
            def _():
                line_copy(way).wait_send()

        sums = along[0] + along[1]
        gains_ref[0:1] = sums[0:8].sum(0, keepdims=True)
        gains_ref[1:2] = sums[8:16].sum(0, keepdims=True)
        drain()


def chain_call(kernel, name, number, count, shape, inputs, outs, scratch):
    rows, width = shape
    chunks = rows // 2 // CHUNK
    arrays, in_specs = zip(*inputs)
    out_shape, out_specs = zip(*outs)
    return pl.pallas_call(
        kernel,
        out_shape=out_shape,
        grid=(tick_count(rows, count),),
        in_specs=in_specs,
        out_specs=out_specs,
        scratch_shapes=[
            pltpu.VMEM((2, rows // 2, width), jnp.bfloat16),
            pltpu.VMEM((rows, width), jnp.bfloat16),
            pltpu.SemaphoreType.DMA((4, chunks)),
            pltpu.SemaphoreType.DMA((4, chunks)),
            pltpu.SemaphoreType.DMA((2, chunks)),
            *scratch,
        ],
        compiler_params=pltpu.CompilerParams(
            collective_id=number, has_side_effects=True, vmem_limit_bytes=60 * 2**20
        ),
        cost_estimate=pl.CostEstimate(
            flops=100 * 10**9, bytes_accessed=12 * rows * width, transcendentals=0
        ),
        name=name,
    )(*arrays)


def far(shape, dtype):
    return jax.ShapeDtypeStruct(shape, dtype), HBM_SPEC


def kept(shape, dtype):
    return jax.ShapeDtypeStruct(shape, dtype), VMEM_SPEC


def sum_middle(mixed, both, tokens, gain, cotangent, count):
    rows, width = tokens.shape
    inner = mixed.shape[1]
    hidden = both.shape[0] - inner
    last = hidden // WIDE - 1
    at = lambda i: jnp.minimum(i // SPACING, last)
    return chain_call(
        functools.partial(middle_kernel, count, last + 1), "sum_middle", 1, count, tokens.shape,
        [
            (mixed, VMEM_SPEC),
            (both, pl.BlockSpec((inner, width), lambda i: (0, 0), pipeline_mode=pl.Buffered(1))),
            (tokens, HBM_SPEC), (gain, VMEM_SPEC), (cotangent, HBM_SPEC),
            (both, pl.BlockSpec((WIDE, width), lambda i: (inner // WIDE + at(i), 0))),
        ],
        [
            far(tokens.shape, jnp.bfloat16),
            far((rows // 2, width), jnp.float32),
            (
                jax.ShapeDtypeStruct((rows, hidden), jnp.float32),
                pl.BlockSpec((rows, WIDE), lambda i: (0, at(i))),
            ),
        ],
        [
            *[pltpu.VMEM(tokens.shape, jnp.bfloat16)] * 3,
            pltpu.VMEM((rows // 2, width), jnp.float32),
            pltpu.SemaphoreType.DMA((2,)),
            pltpu.SemaphoreType.DMA((rows // 2 // CHUNK,)),
        ],
    )


def sum_middle_back(part, middle, cotangent, gain, hidden, both, count):
    rows, width = part.shape
    last = width // WIDE - 1
    at = lambda i: jnp.minimum(i // SPACING, last)
    return chain_call(
        functools.partial(middle_back_kernel, count), "sum_middle_back", 2, count, part.shape,
        [
            (part, VMEM_SPEC), (middle, HBM_SPEC), (cotangent, HBM_SPEC), (gain, VMEM_SPEC),
            (hidden, HBM_SPEC), (both, pl.BlockSpec((both.shape[0], WIDE), lambda i: (0, at(i)))),
        ],
        [
            far(part.shape, jnp.bfloat16),
            far((rows // 2, width), jnp.float32),
            kept((8, width), jnp.float32),
            (
                jax.ShapeDtypeStruct(part.shape, jnp.bfloat16),
                pl.BlockSpec((rows, WIDE), lambda i: (0, at(i))),
            ),
        ],
        [
            pltpu.VMEM((rows // 2, width), jnp.float32),
            pltpu.VMEM(part.shape, jnp.bfloat16),
            pltpu.VMEM(hidden.shape, jnp.bfloat16),
            pltpu.VMEM((rows // 2, width), jnp.float32),
            pltpu.SemaphoreType.DMA((3,)),
            pltpu.SemaphoreType.DMA((rows // 2 // CHUNK,)),
        ],
    )


def sum_input_back(part, tokens, grad, gain, other, size, count):
    width = part.shape[1]
    plane = width // size
    return chain_call(
        functools.partial(input_back_kernel, count), "sum_input_back", 3, count, part.shape,
        [
            (part, VMEM_SPEC), (tokens, HBM_SPEC), (grad, HBM_SPEC), (gain, VMEM_SPEC),
            (other, VMEM_SPEC),
        ],
        [far(part.shape, jnp.bfloat16), kept((2, size), jnp.float32)],
        [
            pltpu.VMEM(part.shape, jnp.bfloat16),
            pltpu.VMEM(grad.shape, jnp.float32),
            pltpu.VMEM((16, width), jnp.float32),
            pltpu.VMEM((plane, 16, size), jnp.float32),
            pltpu.VMEM((2, 16, size), jnp.float32),
            pltpu.SemaphoreType.DMA((2,)),
            pltpu.SemaphoreType.DMA((plane,)),
            pltpu.SemaphoreType.DMA((plane,)),
            pltpu.SemaphoreType.DMA((2,)),
            pltpu.SemaphoreType.DMA((2,)),
        ],
    )


def rotate_pairs(values, cosine, sine):
    parts = [
        rotate_lanes(values[:, at : at + PAIR], cosine, sine)
        for at in range(0, values.shape[1], PAIR)
    ]
    return jnp.concatenate(parts, 1)


def plane_peers():
    ctx = lax.axis_size("ctx")
    size = lax.axis_size("shard") * ctx
    mine = lax.axis_index("shard") * ctx + lax.axis_index("ctx")

    def peer(distance):
        index = lax.rem(mine + distance, size)
        return index, {"shard": index // ctx, "ctx": lax.rem(index, ctx)}

    return size, mine, peer


def greet_plane(size, peer):
    barrier = pltpu.get_barrier_semaphore()
    for distance in range(1, size):
        pl.semaphore_signal(barrier, inc=1, device_id=peer(distance)[1], device_id_type=MESH)


def front_kernel(
    live_ref, tokens_ref, weight_ref, own_gain_ref, cos_ref, sin_ref,
    h_ref, q_ref, k_ref, v_ref, kp_ref, vp_ref, o_ref, l_ref, gain_ref,
    send, recv, gain_send, gain_recv,
):
    late = lax.axis_index("ctx")
    rows, width = q_ref.shape
    block = min(BLOCK, rows)
    blocks = rows // block
    pairs = width // PAIR
    size, index, peer = plane_peers()
    part = own_gain_ref.shape[1]
    greet_plane(size, peer)
    pl.semaphore_wait(pltpu.get_barrier_semaphore(), size - 1)
    mine = pl.ds(pl.multiple_of(index * part, part), part)
    gain_ref[:, mine] = own_gain_ref[...]

    def gain_copy(distance):
        return pltpu.make_async_remote_copy(
            src_ref=own_gain_ref, dst_ref=gain_ref.at[:, mine],
            send_sem=gain_send.at[distance], recv_sem=gain_recv.at[distance],
            device_id=peer(distance)[1], device_id_type=MESH,
        )

    for distance in range(1, size):
        gain_copy(distance).start()
    for distance in range(1, size):
        gain_copy(distance).wait()

    def here(at):
        return pl.ds(pl.multiple_of(at * block, block), block)

    def lanes(pair):
        return pl.ds(pl.multiple_of(pair * PAIR, PAIR), PAIR)

    @pl.loop(0, blocks)
    def _(at):
        stream = tokens_ref[here(at)].astype(jnp.float32)
        normed = (stream * unit_scale(stream) * gain_ref[0:1]).astype(jnp.bfloat16)
        h_ref[here(at)] = normed
        keys = dot(normed, weight_ref[1], (1, 0))
        k_ref[here(at)] = rotate_pairs(keys, cos_ref[here(at)], sin_ref[here(at)]).astype(jnp.bfloat16)
        v_ref[here(at)] = dot(normed, weight_ref[2], (1, 0)).astype(jnp.bfloat16)

    def exchange(pair):
        return [
            pltpu.make_async_remote_copy(
                src_ref=own.at[:, lanes(pair)], dst_ref=prev.at[:, lanes(pair)],
                send_sem=send.at[which, pair], recv_sem=recv.at[which, pair],
                device_id={"ctx": 1 - late}, device_id_type=MESH,
            )
            for which, own, prev in ((0, k_ref, kp_ref), (1, v_ref, vp_ref))
        ]

    @pl.when(late == 0)
    def _():
        @pl.loop(0, pairs)
        def _(pair):
            for copy in exchange(pair):
                copy.start()

    @pl.loop(0, blocks)
    def _(at):
        query = dot(h_ref[here(at)], weight_ref[0], (1, 0))
        query = rotate_pairs(query, cos_ref[here(at)], sin_ref[here(at)]) * 0.125
        q_ref[here(at)] = query.astype(jnp.bfloat16)

    def attend(pair, own, with_prev):
        column = lanes(pair)
        mine = slice(own * block, (own + 1) * block)
        query = q_ref[mine, column]
        mixed = []
        for head in range(2):
            queries = one_head(query, head)
            parts = []
            if with_prev:
                parts.append((dot(kp_ref[:, column], queries, (1, 1)), vp_ref[:, column]))
            if own:
                before = slice(0, own * block)
                parts.append((dot(k_ref[before, column], queries, (1, 1)), v_ref[before, column]))
            parts.append((causal(dot(k_ref[mine, column], queries, (1, 1))), v_ref[mine, column]))
            peak = parts[0][0].max(0, keepdims=True)
            for scores, _ in parts[1:]:
                peak = jnp.maximum(peak, scores.max(0, keepdims=True))
            expo = [jnp.exp(scores - peak) for scores, _ in parts]
            denom = expo[0].sum(0, keepdims=True)
            for e in expo[1:]:
                denom = denom + e.sum(0, keepdims=True)
            inverse = 1.0 / denom
            total = None
            for e, (_, value) in zip(expo, parts):
                term = dot(value, (e * inverse).astype(jnp.bfloat16), (0, 0))
                total = term if total is None else total + term
            mixed.append(total[head * HEAD : (head + 1) * HEAD])
            index = late * rows + own * block + lax.broadcasted_iota(jnp.int32, peak.shape, 1)
            l_ref[pair, head : head + 1, mine] = jnp.where(
                index < live_ref[0], peak + jnp.log(denom), -MASKED
            )
        result = jnp.concatenate(mixed, 0).T
        index = late * rows + own * block + lax.broadcasted_iota(jnp.int32, result.shape, 0)
        own_value = v_ref[mine, column].astype(jnp.float32)
        o_ref[mine, column] = jnp.where(index < live_ref[0], result, own_value).astype(jnp.bfloat16)

    @pl.loop(0, pairs)
    def _(pair):
        @pl.when(late == 0)
        def _():
            for own in range(blocks):
                attend(pair, own, False)

        @pl.when(late == 1)
        def _():
            for copy in exchange(pair):
                copy.wait_recv()
            for own in range(blocks):
                attend(pair, own, True)

    @pl.when(late == 0)
    def _():
        @pl.loop(0, pairs)
        def _(pair):
            for copy in exchange(pair):
                copy.wait_send()


def layer_front(live, tokens, weight, gain, cosine, sine):
    rows, depth = tokens.shape
    width = weight.shape[2]
    pairs = width // PAIR
    part = jax.ShapeDtypeStruct((rows, width), jnp.bfloat16)
    outs = (
        jax.ShapeDtypeStruct((rows, depth), jnp.bfloat16), part, part, part, part, part, part,
        jax.ShapeDtypeStruct((pairs, 2, rows), jnp.float32),
        jax.ShapeDtypeStruct((8, depth), jnp.float32),
    )
    size = lax.axis_size("shard") * lax.axis_size("ctx")
    return pl.pallas_call(
        front_kernel,
        out_shape=outs,
        in_specs=[SMEM_SPEC] + [VMEM_SPEC] * 5,
        out_specs=(VMEM_SPEC,) * len(outs),
        scratch_shapes=[pltpu.SemaphoreType.DMA((2, pairs))] * 2
        + [pltpu.SemaphoreType.DMA((size,))] * 2,
        compiler_params=pltpu.CompilerParams(
            collective_id=4, has_side_effects=True, vmem_limit_bytes=56 * 2**20
        ),
        cost_estimate=pl.CostEstimate(
            flops=80 * 10**9, bytes_accessed=40 * 2**20, transcendentals=0
        ),
        name="layer_front",
    )(live, tokens, weight, gain, cosine, sine)


def attend_back_kernel(
    count, live_ref, q_ref, k_ref, v_ref, kp_ref, vp_ref, o_ref, l_ref, cos_ref, sin_ref,
    part_ref, middle_ref, grad_ref, weight_ref, dq_ref, dk_ref, dv_ref, out_ref,
    do_ref, dq_acc, dk_acc, dv_acc, dkp_acc, dvp_acc, leave, arrive, slots, send, recv, chain_send, chain_recv,
):
    late = lax.axis_index("ctx")
    me = lax.axis_index("tp")
    rows, width = q_ref.shape
    block = min(BLOCK, rows)
    blocks = rows // block
    pairs = width // PAIR
    barrier = pltpu.get_barrier_semaphore()
    pl.semaphore_signal(barrier, inc=1, device_id={"ctx": 1 - late}, device_id_type=MESH)
    greet(me, count, 1)
    tick, drain, ticks = chain_parts(
        count, part_ref, out_ref, slots, chain_send, chain_recv,
        lambda rows, part, total, at: (middle_ref[part] + total).astype(jnp.bfloat16), BACK_CHUNK, BACK_LAG,
    )

    def here(at):
        return pl.ds(pl.multiple_of(at * block, block), block)

    def lanes(pair):
        return pl.ds(pl.multiple_of(pair * PAIR, PAIR), PAIR)

    def prepare(pair, step):
        column = lanes(pair)
        query = q_ref[here(step), column]
        upstream = do_ref[here(step), column]
        product = (upstream.astype(jnp.float32) * o_ref[here(step), column].astype(jnp.float32)).T
        queries = [one_head(query, head) for head in range(2)]
        upstreams = [one_head(upstream, head) for head in range(2)]
        inner = [
            product[head * HEAD : (head + 1) * HEAD].sum(0, keepdims=True) for head in range(2)
        ]
        totals = [l_ref[pair, head : head + 1, here(step)] for head in range(2)]
        query_both = jnp.concatenate(queries, 0)
        upstream_both = jnp.concatenate(upstreams, 0)

        def tile(keys, values, masked):
            grads, probs_all, out = [], [], []
            for head in range(2):
                scores = dot(keys, queries[head], (1, 1))
                if masked:
                    scores = causal(scores)
                probs = jnp.exp(scores - totals[head])
                prob_grad = dot(values, upstreams[head], (1, 1))
                score_grad = (probs * (prob_grad - inner[head])).astype(jnp.bfloat16)
                probs_all.append(probs.astype(jnp.bfloat16))
                grads.append(score_grad)
                out.append(dot(keys, score_grad, (0, 0))[head * HEAD : (head + 1) * HEAD])
            key_grad = dot(jnp.concatenate(grads, 1), query_both, (1, 0))
            value_grad = dot(jnp.concatenate(probs_all, 1), upstream_both, (1, 0))
            return jnp.concatenate(out, 0), key_grad, value_grad

        return tile, upstream

    def exchange(pair):
        return pltpu.make_async_remote_copy(
            src_ref=leave.at[pair], dst_ref=arrive.at[pair], send_sem=send.at[pair],
            recv_sem=recv.at[pair], device_id={"ctx": 1 - late}, device_id_type=MESH,
        )

    def prev_step(pair, step):
        column = lanes(pair)
        tile, _ = prepare(pair, step)

        @pl.when(step == 0)
        def _():
            dkp_acc[...] = jnp.zeros_like(dkp_acc)
            dvp_acc[...] = jnp.zeros_like(dvp_acc)

        query_grad = None
        for at in range(blocks):
            mine = slice(at * block, (at + 1) * block)
            more, key_grad, value_grad = tile(kp_ref[mine, column], vp_ref[mine, column], False)
            query_grad = more if query_grad is None else query_grad + more
            dkp_acc[mine] += key_grad
            dvp_acc[mine] += value_grad
        dq_acc[pair, :, here(step)] = query_grad

        @pl.when(step == blocks - 1)
        def _():
            leave[pair, 0] = dkp_acc[...].astype(jnp.bfloat16)
            leave[pair, 1] = dvp_acc[...].astype(jnp.bfloat16)
            exchange(pair).start()

    def own_step(pair, step):
        column = lanes(pair)
        tile, upstream = prepare(pair, step)
        query_grad, key_grad, value_grad = tile(k_ref[here(step), column], v_ref[here(step), column], True)
        index = late * rows + step * block + lax.broadcasted_iota(jnp.int32, upstream.shape, 0)
        dk_acc[here(step), column] = key_grad
        dv_acc[here(step), column] = value_grad + jnp.where(
            index < live_ref[0], 0.0, upstream.astype(jnp.float32)
        )
        dq_acc[pair, :, here(step)] += query_grad

        @pl.loop(0, step)
        def _(at):
            more, key_grad, value_grad = tile(k_ref[here(at), column], v_ref[here(at), column], False)
            dk_acc[here(at), column] += key_grad
            dv_acc[here(at), column] += value_grad
            dq_acc[pair, :, here(step)] += more

        grad = dq_acc[pair, :, here(step)].T * 0.125
        grad = rotate_lanes(grad, cos_ref[here(step)], -sin_ref[here(step)])
        dq_ref[here(step), column] = grad.astype(jnp.bfloat16)

    @pl.when(late == 0)
    def _():
        dq_acc[...] = jnp.zeros_like(dq_acc)

    @pl.loop(0, blocks)
    def _(at):
        for more in range(LEAD):
            tick(at * LEAD + more)
        do_ref[here(at)] = dot(grad_ref[here(at)], weight_ref[...], (1, 1)).astype(jnp.bfloat16)

    steps = pairs * blocks
    lead = blocks * LEAD

    @pl.loop(0, 2 * steps)
    def _(at):
        @pl.when(lead + at < ticks)
        def _():
            tick(lead + at)

        @pl.when((late == 1) & (at < steps))
        def _():
            prev_step(at // blocks, at % blocks)

        @pl.when(at >= steps)
        def _():
            own_step((at - steps) // blocks, at % blocks)

    if ticks > lead + 2 * steps:
        pl.loop(lead + 2 * steps, ticks)(tick)

    @pl.loop(0, pairs)
    def _(pair):
        column = lanes(pair)

        @pl.when(late == 0)
        def _():
            exchange(pair).wait_recv()
            dk_acc[:, column] += arrive[pair, 0].astype(jnp.float32)
            dv_acc[:, column] += arrive[pair, 1].astype(jnp.float32)

        @pl.when(late == 1)
        def _():
            exchange(pair).wait_send()

        dk_ref[:, column] = rotate_lanes(dk_acc[:, column], cos_ref[...], -sin_ref[...]).astype(
            jnp.bfloat16
        )
        dv_ref[:, column] = dv_acc[:, column].astype(jnp.bfloat16)

    drain()


def attend_back(live, arrays, cosine, sine, out_part, middle, grad, both, count):
    rows, width = arrays[0].shape
    pairs = width // PAIR
    part = jax.ShapeDtypeStruct((rows, width), jnp.bfloat16)
    outs = (
        part, part, part, jax.ShapeDtypeStruct(out_part.shape, jnp.bfloat16),
    )
    chunks = rows // 2 // BACK_CHUNK
    return pl.pallas_call(
        functools.partial(attend_back_kernel, count),
        out_shape=outs,
        in_specs=[SMEM_SPEC] + [VMEM_SPEC] * 13,
        out_specs=(VMEM_SPEC,) * len(outs),
        scratch_shapes=[
            pltpu.VMEM((rows, width), jnp.bfloat16),
            pltpu.VMEM((pairs, PAIR, rows), jnp.float32),
            pltpu.VMEM((rows, width), jnp.float32),
            pltpu.VMEM((rows, width), jnp.float32),
            pltpu.VMEM((rows, PAIR), jnp.float32),
            pltpu.VMEM((rows, PAIR), jnp.float32),
            pltpu.VMEM((pairs, 2, rows, PAIR), jnp.bfloat16),
            pltpu.VMEM((pairs, 2, rows, PAIR), jnp.bfloat16),
            pltpu.VMEM((2, rows // 2, out_part.shape[1]), jnp.bfloat16),
            pltpu.SemaphoreType.DMA((pairs,)),
            pltpu.SemaphoreType.DMA((pairs,)),
            pltpu.SemaphoreType.DMA((4, chunks)),
            pltpu.SemaphoreType.DMA((4, chunks)),
        ],
        compiler_params=pltpu.CompilerParams(
            collective_id=5, has_side_effects=True, vmem_limit_bytes=58 * 2**20
        ),
        cost_estimate=pl.CostEstimate(
            flops=100 * 10**9, bytes_accessed=40 * 2**20, transcendentals=0
        ),
        name="attend_back",
    )(live, *arrays, cosine, sine, out_part, middle, grad, both)


def narrow_kernel(out_ref, down_ref, gate_up_ref, both_ref, low_ref):
    split = out_ref.shape[0]
    both_ref[:split] = out_ref[...].astype(jnp.bfloat16)
    both_ref[split:] = down_ref[...].astype(jnp.bfloat16)
    low_ref[...] = gate_up_ref[...].astype(jnp.bfloat16)


def narrow(out_weight, down_weight, gate_up_weight):
    return pl.pallas_call(
        narrow_kernel,
        out_shape=(
            jax.ShapeDtypeStruct(
                (out_weight.shape[0] + down_weight.shape[0], out_weight.shape[1]), jnp.bfloat16
            ),
            jax.ShapeDtypeStruct(gate_up_weight.shape, jnp.bfloat16),
        ),
        in_specs=[VMEM_SPEC] * 3,
        out_specs=(VMEM_SPEC,) * 2,
        compiler_params=pltpu.CompilerParams(vmem_limit_bytes=40 * 2**20),
        cost_estimate=pl.CostEstimate(flops=40 * 10**9, bytes_accessed=2**24, transcendentals=0),
        name="narrow",
    )(out_weight, down_weight, gate_up_weight)


def mlp_kernel(
    normed_ref, weight_ref, hidden_grad_ref, cotangent_ref,
    hidden_ref, down_grad_ref, gate_up_grad_ref, back_ref, turned, total,
):
    step = pl.program_id(0)

    @pl.when(step == 0)
    def _():
        turned[...] = normed_ref[...].T
        total[...] = jnp.zeros_like(total)

    gate = dot(normed_ref[...], weight_ref[0], (1, 0))
    upward = dot(normed_ref[...], weight_ref[1], (1, 0))
    hidden_grad = hidden_grad_ref[...]
    sigma = jax.nn.sigmoid(gate)
    swish = gate * sigma
    hidden = (swish * upward).astype(jnp.bfloat16)
    hidden_ref[...] = hidden
    gate_grad = (hidden_grad * upward * sigma * (1.0 + gate * (1.0 - sigma))).astype(jnp.bfloat16)
    upward_grad = (hidden_grad * swish).astype(jnp.bfloat16)
    both = jnp.concatenate([gate_grad, upward_grad], 1)
    weights = jnp.concatenate([weight_ref[0], weight_ref[1]], 1)
    total[...] += dot(both, weights, (1, 1))
    gate_up_grad_ref[0] = dot(turned[...], gate_grad, (1, 0)).astype(jnp.bfloat16)
    gate_up_grad_ref[1] = dot(turned[...], upward_grad, (1, 0)).astype(jnp.bfloat16)
    down_grad_ref[...] = dot(hidden.T, cotangent_ref[...], (1, 0)).astype(jnp.bfloat16)

    @pl.when(step == pl.num_programs(0) - 1)
    def _():
        back_ref[...] = total[...].astype(jnp.bfloat16)


def mlp(normed, weight, hidden_grad, cotangent):
    rows, depth = normed.shape
    width = weight.shape[2]
    whole = pl.BlockSpec((rows, depth), lambda j: (0, 0), pipeline_mode=pl.Buffered(1))
    return pl.pallas_call(
        mlp_kernel,
        out_shape=(
            jax.ShapeDtypeStruct((rows, width), jnp.bfloat16),
            jax.ShapeDtypeStruct((width, depth), jnp.bfloat16),
            jax.ShapeDtypeStruct((2, depth, width), jnp.bfloat16),
            jax.ShapeDtypeStruct((rows, depth), jnp.bfloat16),
        ),
        grid=(width // MLP_WIDE,),
        in_specs=[
            whole,
            pl.BlockSpec((2, depth, MLP_WIDE), lambda j: (0, 0, j)),
            pl.BlockSpec((rows, MLP_WIDE), lambda j: (0, j)),
            whole,
        ],
        out_specs=(
            pl.BlockSpec((rows, MLP_WIDE), lambda j: (0, j)),
            pl.BlockSpec((MLP_WIDE, depth), lambda j: (j, 0)),
            pl.BlockSpec((2, depth, MLP_WIDE), lambda j: (0, 0, j)),
            pl.BlockSpec((rows, depth), lambda j: (0, 0)),
        ),
        scratch_shapes=[
            pltpu.VMEM((depth, rows), jnp.bfloat16), pltpu.VMEM((rows, depth), jnp.float32),
        ],
        compiler_params=pltpu.CompilerParams(vmem_limit_bytes=60 * 2**20),
        cost_estimate=pl.CostEstimate(
            flops=14 * rows * depth * width, bytes_accessed=80 * 2**20, transcendentals=rows * width
        ),
        name="mlp",
    )(normed, weight, hidden_grad, cotangent)


def projection_back_kernel(
    normed_ref, weight_ref, dq_ref, dk_ref, dv_ref, mixed_ref, middle_ref, grad_ref, back_ref,
    turned, total,
):
    step = pl.program_id(0)

    @pl.when(step == 0)
    def _():
        turned[...] = normed_ref[...].T

    for at, ref in enumerate((dq_ref, dk_ref, dv_ref)):

        @pl.when(step == at)
        def _():
            term = dot(ref[...], weight_ref[0], (1, 1))
            if at == 0:
                total[...] = term
            elif at == 1:
                total[...] += term
            else:
                back_ref[...] = (total[...] + term).astype(jnp.bfloat16)
            grad_ref[0] = dot(turned[...], ref[...], (1, 0)).astype(jnp.bfloat16)

    @pl.when(step == 3)
    def _():
        turned[...] = middle_ref[...].T
        grad_ref[0] = dot(turned[...], mixed_ref[...], (1, 0)).astype(jnp.bfloat16)


def projection_back(normed, weight, dq, dk, dv, mixed, middle):
    rows, depth = normed.shape
    width = dq.shape[1]
    whole = lambda w: pl.BlockSpec((rows, w), lambda j: (0, 0), pipeline_mode=pl.Buffered(1))
    return pl.pallas_call(
        projection_back_kernel,
        out_shape=(
            jax.ShapeDtypeStruct((4, depth, width), jnp.bfloat16),
            jax.ShapeDtypeStruct((rows, depth), jnp.bfloat16),
        ),
        grid=(4,),
        in_specs=[
            whole(depth),
            pl.BlockSpec((1, depth, width), lambda j: (jnp.minimum(j, 2), 0, 0)),
            whole(width), whole(width), whole(width), whole(width), whole(depth),
        ],
        out_specs=(
            pl.BlockSpec((1, depth, width), lambda j: (j, 0, 0)),
            pl.BlockSpec((rows, depth), lambda j: (0, 0)),
        ),
        scratch_shapes=[
            pltpu.VMEM((depth, rows), jnp.bfloat16), pltpu.VMEM((rows, depth), jnp.float32),
        ],
        compiler_params=pltpu.CompilerParams(vmem_limit_bytes=60 * 2**20),
        cost_estimate=pl.CostEstimate(
            flops=14 * rows * depth * width, bytes_accessed=40 * 2**20, transcendentals=0
        ),
        name="projection_back",
    )(normed, weight, dq, dk, dv, mixed, middle)


def scatter_low(grad, axis=1):
    return lax.psum_scatter(
        grad.astype(jnp.bfloat16), ("shard", "ctx"), scatter_dimension=axis, tiled=True
    ).astype(jnp.float32)


def after(array, *others):
    return lax.optimization_barrier((array, *others))[0]


def adam_update(weight, first, second, grad, decay):
    first_new = beta_one * first + (1.0 - beta_one) * grad
    second_new = beta_two * second + (1.0 - beta_two) * grad * grad
    first_hat = first_new / (1.0 - beta_one**step_count)
    second_hat = second_new / (1.0 - beta_two**step_count)
    update = learn_rate * (first_hat / (jnp.sqrt(second_hat) + adam_eps) + decay * weight)
    return (update, first_new, second_new)


def body(
    tokens,
    cotangent,
    lengths,
    qkv_weight,
    out_weight,
    gate_up_weight,
    down_weight,
    norm_gains,
    qkv_first,
    out_first,
    gate_up_first,
    down_first,
    gains_first,
    qkv_second,
    out_second,
    gate_up_second,
    down_second,
    gains_second,
):
    row_count = tokens.shape[0]
    count = lax.axis_size("tp")
    offset = lax.axis_index("ctx") * row_count
    query_index = offset + jnp.arange(row_count, dtype=jnp.int32)
    qkv_low = qkv_weight.astype(jnp.bfloat16)
    both_low, gate_up_low = narrow(out_weight, down_weight, gate_up_weight)
    gains_low = norm_gains.astype(jnp.bfloat16).astype(jnp.float32)
    gains_low = jnp.concatenate([gains_low] * 4, 0)
    gather = lambda a: lax.all_gather(a, ("shard", "ctx"), axis=1, tiled=True)
    qkv_full = gather(qkv_low)
    both_full = gather(after(both_low, qkv_full))
    cosine, sine = rotation(query_index, HEAD)
    cosine, sine = (jnp.concatenate([c[:, 0]] * 4, 1) for c in (cosine, sine))
    normed_one, query, keys, values, keys_prev, values_prev, mixed_low, totals, gains_full = layer_front(
        lengths, tokens, qkv_full, gains_low, cosine, sine
    )
    gain_one, gain_two = gains_full[0:1], gains_full[1:2]
    gate_up_full = gather(after(gate_up_low, both_full, totals))
    normed_two, middle, hidden_grad = sum_middle(
        mixed_low, both_full, tokens, gain_two, cotangent, count
    )
    hidden, down_grad_local, gate_up_grad_local, mlp_back_part = mlp(
        normed_two, gate_up_full, hidden_grad, cotangent
    )
    gate_up_grad = scatter_low(gate_up_grad_local)
    middle_low, middle_grad, gain_two_grad, out_part = sum_middle_back(
        mlp_back_part, middle, cotangent, gain_two, hidden, both_full, count
    )
    down_grad = scatter_low(after(down_grad_local, gate_up_grad, middle_low))
    query_low, key_low, value_low, out_tokens = attend_back(
        lengths,
        [query, keys, values, keys_prev, values_prev, mixed_low, totals],
        cosine, sine, out_part, middle, middle_low, both_full[: mixed_low.shape[1]], count,
    )
    qkv_grad_local, attn_back_part = projection_back(
        normed_one, qkv_full, query_low, key_low, value_low, mixed_low, middle_low
    )
    attn_back_part, qkv_grad_local, _ = lax.optimization_barrier(
        (attn_back_part, qkv_grad_local, down_grad)
    )
    qkv_grad = scatter_low(qkv_grad_local)
    out_grad = lax.optimization_barrier(qkv_grad[3].T)
    qkv_grad = qkv_grad[:3]
    input_grad, gains_grad = sum_input_back(
        attn_back_part, tokens, middle_grad, gain_one, gain_two_grad, norm_gains.shape[1], count
    )
    qkv_step, qkv_first_new, qkv_second_new = adam_update(
        qkv_weight, qkv_first, qkv_second, qkv_grad, decay_rate
    )
    out_step, out_first_new, out_second_new = adam_update(
        out_weight, out_first, out_second, out_grad, decay_rate
    )
    gate_up_step, gate_up_first_new, gate_up_second_new = adam_update(
        gate_up_weight, gate_up_first, gate_up_second, gate_up_grad, decay_rate
    )
    down_step, down_first_new, down_second_new = adam_update(
        down_weight, down_first, down_second, down_grad, decay_rate
    )
    gains_step, gains_first_new, gains_second_new = adam_update(
        norm_gains, gains_first, gains_second, gains_grad, 0.0
    )
    qkv_new = qkv_weight - qkv_step
    gate_up_new = gate_up_weight - gate_up_step
    down_new = down_weight - down_step
    return (
        out_tokens,
        input_grad,
        qkv_grad,
        out_grad,
        gate_up_grad,
        down_grad,
        gains_grad,
        qkv_new,
        out_step,
        gate_up_new,
        down_new,
        gains_step,
        qkv_first_new,
        out_first_new,
        gate_up_first_new,
        down_first_new,
        gains_first_new,
        qkv_second_new,
        out_second_new,
        gate_up_second_new,
        down_second_new,
        gains_second_new,
    )


def solution(mesh):
    return jax.shard_map(
        body,
        mesh=mesh,
        in_specs=(
            P(("shard", "ctx"), None),
            P(("shard", "ctx"), None),
            P("shard"),
            P(None, ("shard", "ctx"), "tp"),
            P("tp", ("shard", "ctx")),
            P(None, ("shard", "ctx"), "tp"),
            P("tp", ("shard", "ctx")),
            P(None, ("shard", "ctx")),
            P(None, ("shard", "ctx"), "tp"),
            P("tp", ("shard", "ctx")),
            P(None, ("shard", "ctx"), "tp"),
            P("tp", ("shard", "ctx")),
            P(None, ("shard", "ctx")),
            P(None, ("shard", "ctx"), "tp"),
            P("tp", ("shard", "ctx")),
            P(None, ("shard", "ctx"), "tp"),
            P("tp", ("shard", "ctx")),
            P(None, ("shard", "ctx")),
        ),
        out_specs=(
            P(("shard", "ctx"), None),
            P(("shard", "ctx"), None),
            P(None, ("shard", "ctx"), "tp"),
            P("tp", ("shard", "ctx")),
            P(None, ("shard", "ctx"), "tp"),
            P("tp", ("shard", "ctx")),
            P(None, ("shard", "ctx")),
            P(None, ("shard", "ctx"), "tp"),
            P("tp", ("shard", "ctx")),
            P(None, ("shard", "ctx"), "tp"),
            P("tp", ("shard", "ctx")),
            P(None, ("shard", "ctx")),
            P(None, ("shard", "ctx"), "tp"),
            P("tp", ("shard", "ctx")),
            P(None, ("shard", "ctx"), "tp"),
            P("tp", ("shard", "ctx")),
            P(None, ("shard", "ctx")),
            P(None, ("shard", "ctx"), "tp"),
            P("tp", ("shard", "ctx")),
            P(None, ("shard", "ctx"), "tp"),
            P("tp", ("shard", "ctx")),
            P(None, ("shard", "ctx")),
        ),
        check_vma=False,
    )
```

```python
import functools
import jax
import jax.numpy as jnp
from jax import lax
from jax.experimental import pallas as pl
from jax.experimental.pallas import tpu as pltpu
from jax.sharding import PartitionSpec as P

HEAD = 64
PAIR = 128
BLOCK = 256
CHUNK = 16
LAG = 2
BACK_CHUNK = 32
BACK_LAG = 3
WIDE = 256
SPACING = 5
LEAD = 1
MLP_WIDE = 256
MASKED = -1e30
MESH = pl.DeviceIdType.MESH
VMEM_SPEC = pl.BlockSpec(memory_space=pltpu.VMEM)
SMEM_SPEC = pl.BlockSpec(memory_space=pltpu.SMEM)
HBM_SPEC = pl.BlockSpec(memory_space=pl.ANY)


norm_eps = 1e-05
rope_base = 130000.0
beta_one = 0.9
beta_two = 0.95
learn_rate = 0.02
decay_rate = 0.1
adam_eps = 1e-08
step_count = 4.0


def rotation(position, head_size):
    half = head_size // 2
    freqs = rope_base ** (-(jnp.arange(half, dtype=jnp.float32) * 2.0) / head_size)
    angle = position.astype(jnp.float32)[:, None] * freqs[None, :]
    return (jnp.cos(angle)[:, None, :], jnp.sin(angle)[:, None, :])


def dot(left, right, contract):
    return lax.dot_general(
        left, right, ((contract[:1], contract[1:]), ((), ())), preferred_element_type=jnp.float32
    )


def one_head(values, head):
    lane = lax.broadcasted_iota(jnp.int32, values.shape, 1)
    return jnp.where((lane < HEAD) == (head == 0), values, jnp.zeros_like(values))


def causal(scores):
    key = lax.broadcasted_iota(jnp.int32, scores.shape, 0)
    query = lax.broadcasted_iota(jnp.int32, scores.shape, 1)
    return jnp.where(key <= query, scores, MASKED)


def rotate_lanes(values, cosine, sine):
    lane = lax.broadcasted_iota(jnp.int32, values.shape, 1) % HEAD
    width = values.shape[1]
    ahead = pltpu.roll(values, width - HEAD // 2, 1)
    behind = pltpu.roll(values, HEAD // 2, 1)
    return values * cosine + jnp.where(lane < HEAD // 2, -ahead, behind) * sine


def greet(me, count, more=0, more_ends=0):
    barrier = pltpu.get_barrier_semaphore()

    @pl.when(me > 0)
    def _():
        pl.semaphore_signal(barrier, inc=1, device_id={"tp": me - 1}, device_id_type=MESH)

    @pl.when(me < count - 1)
    def _():
        pl.semaphore_signal(barrier, inc=1, device_id={"tp": me + 1}, device_id_type=MESH)

    @pl.when((me > 0) & (me < count - 1))
    def _():
        pl.semaphore_wait(barrier, 2 + more)

    @pl.when((me == 0) | (me == count - 1))
    def _():
        pl.semaphore_wait(barrier, 1 + more + more_ends)


def chain_parts(count, part_ref, out_ref, slots, send, recv, finish, size, lag=1, land=None, stored=None):
    me = lax.axis_index("tp")
    apart = land is not None
    land = land if apart else out_ref
    half = out_ref.shape[0] // 2
    chunks = half // size

    def copy(stream, at, source, target, device):
        return pltpu.make_async_remote_copy(
            src_ref=source, dst_ref=target, send_sem=send.at[stream, at],
            recv_sem=recv.at[stream, at], device_id={"tp": device}, device_id_type=MESH,
        )

    def ends(way):
        place = me if way == 1 else count - 1 - me
        return place, me + way

    def reduce_copy(way, at, device):
        index = 0 if way == 1 else 1
        rows = pl.ds(pl.multiple_of(at * size, size), size)
        return copy(index, at, slots.at[index, rows], slots.at[index, rows], device)

    def spread_copy(way, at, device):
        base = 0 if way == 1 else half
        rows = pl.ds(pl.multiple_of(base + at * size, size), size)
        return copy(2 if way == 1 else 3, at, land.at[rows], land.at[rows], device)

    def store_copy(index, at):
        rows = pl.ds(pl.multiple_of(index * half + at * size, size), size)
        return pltpu.make_async_copy(land.at[rows], out_ref.at[rows], stored.at[index, at])

    def reduce_step(way, tick):
        place, ahead = ends(way)
        index = 0 if way == 1 else 1
        base = half if way == 1 else 0
        at = tick - lag * place

        @pl.when((at >= 0) & (at < chunks))
        def _():
            local = pl.ds(pl.multiple_of(at * size, size), size)
            rows = pl.ds(pl.multiple_of(base + at * size, size), size)

            @pl.when(place == 0)
            def _():
                slots[index, local] = part_ref[rows]

            @pl.when(place > 0)
            def _():
                reduce_copy(way, at, ahead).wait_recv()

            @pl.when((place > 0) & (place < count - 1))
            def _():
                slots[index, local] = (
                    slots[index, local].astype(jnp.float32) + part_ref[rows].astype(jnp.float32)
                ).astype(jnp.bfloat16)

            @pl.when(place < count - 1)
            def _():
                reduce_copy(way, at, ahead).start()

            @pl.when(place == count - 1)
            def _():
                total = slots[index, local].astype(jnp.float32) + part_ref[rows].astype(jnp.float32)
                land[rows] = finish(rows, local, total, at)
                if apart:
                    store_copy(1 if way == 1 else 0, at).start()
                spread_copy(-way, at, me - way).start()

    def spread_step(way, tick):
        place, ahead = ends(way)
        at = tick - lag * (count - 1) - lag * place

        @pl.when((at >= 0) & (at < chunks) & (place > 0))
        def _():
            spread_copy(way, at, ahead).wait_recv()

            @pl.when(place < count - 1)
            def _():
                spread_copy(way, at, ahead).start()

            if apart:
                store_copy(0 if way == 1 else 1, at).start()

    def step(tick):
        for way in (1, -1):
            reduce_step(way, tick)
        for way in (1, -1):
            spread_step(way, tick)

    def drain():
        @pl.loop(0, chunks)
        def _(at):
            if apart:
                for index in range(2):
                    store_copy(index, at).wait()

            for way in (1, -1):
                place, ahead = ends(way)

                @pl.when(place < count - 1)
                def _():
                    reduce_copy(way, at, ahead).wait_send()
                    spread_copy(way, at, ahead).wait_send()

    return step, drain, chunks + 2 * lag * (count - 1)


def run_ticks(parts, start, wait, finally_drain):
    step, drain, ticks = parts
    tick = pl.program_id(0)
    pl.when(tick == 0)(start)
    pl.when(tick == SPACING - 2)(wait)
    step(tick)

    @pl.when(tick == ticks - 1)
    def _():
        drain()
        finally_drain()

    return tick


def tick_count(rows, count):
    return rows // 2 // CHUNK + 2 * LAG * (count - 1)


def unit_scale(stream):
    return lax.rsqrt(jnp.mean(stream * stream, axis=-1, keepdims=True) + norm_eps)


def fold(values):
    return values.reshape(-1, 8, values.shape[1]).sum(0)


def norm_back(stream, gain, upstream):
    scale = unit_scale(stream)
    gain_grad = fold(upstream * stream * scale)
    inner = jnp.sum(upstream * gain * stream, axis=-1, keepdims=True)
    grad = scale * gain * upstream - stream * (scale * scale * scale / stream.shape[-1]) * inner
    return grad, gain_grad


def loads_of(pairs, sems):
    copies = [
        pltpu.make_async_copy(source, target, sems.at[at])
        for at, (source, target) in enumerate(pairs)
    ]

    def start():
        for copy in copies:
            copy.start()

    def wait():
        for copy in copies:
            copy.wait()

    return start, wait


def half_store(source, target, sems, count):
    chunks = source.shape[0] // CHUNK
    me = lax.axis_index("tp")

    def copy(at):
        rows = pl.ds(pl.multiple_of(at * CHUNK, CHUNK), CHUNK)
        return pltpu.make_async_copy(source.at[rows], target.at[rows], sems.at[at])

    def drain():
        @pl.when((me == 0) | (me == count - 1))
        def _():
            @pl.loop(0, chunks)
            def _(at):
                copy(at).wait()

    return copy, drain


def middle_kernel(
    count, blocks, mixed_ref, weight_ref, tokens_hbm, gain_ref, cotangent_hbm, down_ref,
    out_ref, middle_ref, hidden_grad_ref,
    slots, land, send, recv, stored, part_ref, tokens_ref, cotangent_ref, middle, load_sem, half_sem,
):
    load, wait = loads_of([(tokens_hbm, tokens_ref), (cotangent_hbm, cotangent_ref)], load_sem)
    half_copy, half_drain = half_store(middle, middle_ref, half_sem, count)

    def start():
        load()
        greet(lax.axis_index("tp"), count)

        @pl.loop(0, part_ref.shape[0] // BLOCK)
        def _(at):
            here = pl.ds(pl.multiple_of(at * BLOCK, BLOCK), BLOCK)
            part_ref[here] = dot(mixed_ref[here], weight_ref[...], (1, 0)).astype(jnp.bfloat16)

    def finish(rows, local, total, at):
        value = tokens_ref[rows].astype(jnp.float32) + total
        middle[local] = value
        half_copy(at).start()
        return (value * unit_scale(value) * gain_ref[...]).astype(jnp.bfloat16)

    parts = chain_parts(
        count, part_ref, out_ref, slots, send, recv, finish, CHUNK, LAG, land, stored
    )
    tick = run_ticks(parts, start, wait, half_drain)

    @pl.when((tick % SPACING == SPACING - 1) & (tick < blocks * SPACING))
    def _():
        hidden_grad_ref[...] = dot(cotangent_ref[...], down_ref[...], (1, 1))


def middle_back_kernel(
    count, part_ref, middle_hbm, cotangent_hbm, gain_ref, hidden_hbm, down_ref,
    out_ref, grad_ref, gain_grad_ref, layer_ref,
    slots, land, send, recv, stored, middle_ref, cotangent_ref, hidden_ref, grad, load_sem, half_sem,
):
    load, wait = loads_of(
        [(middle_hbm, middle_ref), (cotangent_hbm, cotangent_ref), (hidden_hbm, hidden_ref)],
        load_sem,
    )
    half_copy, half_drain = half_store(grad, grad_ref, half_sem, count)

    def start():
        load()
        greet(lax.axis_index("tp"), count)
        gain_grad_ref[...] = jnp.zeros_like(gain_grad_ref)

    def finish(rows, local, total, at):
        value, gain_grad = norm_back(middle_ref[local], gain_ref[...], total)
        gain_grad_ref[...] += gain_grad
        value = cotangent_ref[rows].astype(jnp.float32) + value
        grad[local] = value
        half_copy(at).start()
        return value.astype(jnp.bfloat16)

    parts = chain_parts(
        count, part_ref, out_ref, slots, send, recv, finish, CHUNK, LAG, land, stored
    )
    tick = run_ticks(parts, start, wait, half_drain)

    @pl.when((tick % SPACING == SPACING - 1) & (tick < part_ref.shape[1] // WIDE * SPACING))
    def _():
        skip = down_ref.shape[0] - hidden_ref.shape[1]
        layer_ref[...] = dot(hidden_ref[...], down_ref[skip:], (1, 0)).astype(jnp.bfloat16)


def input_back_kernel(
    count, part_ref, tokens_hbm, grad_hbm, gain_ref, other_ref, out_ref, gains_ref,
    slots, land, send, recv, stored, tokens_ref, grad_ref, local, landed, along,
    load_sem, plane_send, plane_recv, line_send, line_recv,
):
    load, wait = loads_of([(tokens_hbm, tokens_ref), (grad_hbm, grad_ref)], load_sem)

    me = lax.axis_index("tp")
    size, index, peer = plane_peers()
    width = gains_ref.shape[1]
    last = (me == 0) | (me == count - 1)

    def start():
        load()

        @pl.when(last)
        def _():
            greet_plane(size, peer)

        greet(me, count, 0, size - 1)
        local[0:8] = jnp.zeros((8, local.shape[1]), jnp.float32)
        local[8:16] = other_ref[...]

    def finish(rows, part, total, at):
        grad, gain_grad = norm_back(tokens_ref[rows].astype(jnp.float32), gain_ref[...], total)
        local[0:8] += gain_grad
        return (grad_ref[part] + grad).astype(jnp.bfloat16)

    step, drain, ticks = chain_parts(
        count, part_ref, out_ref, slots, send, recv, finish, CHUNK, LAG, land, stored
    )

    def columns(at):
        return pl.ds(pl.multiple_of(at * width, width), width)

    def plane_copy(distance):
        at, device = peer(distance)
        return pltpu.make_async_remote_copy(
            src_ref=local.at[:, columns(at)], dst_ref=landed.at[distance],
            send_sem=plane_send.at[distance], recv_sem=plane_recv.at[distance],
            device_id=device, device_id_type=MESH,
        )

    def line_copy(way):
        which = 0 if way == 1 else 1
        return pltpu.make_async_remote_copy(
            src_ref=along.at[which], dst_ref=along.at[which],
            send_sem=line_send.at[which], recv_sem=line_recv.at[which],
            device_id={"tp": me + way}, device_id_type=MESH,
        )

    done = out_ref.shape[0] // 2 // CHUNK + LAG * (count - 1)

    tick = pl.program_id(0)
    pl.when(tick == 0)(start)
    pl.when(tick == SPACING - 2)(wait)
    step(tick)

    @pl.when(last & (tick == done - 1))
    def _():
        for distance in range(1, size):
            plane_copy(distance).start()

    @pl.when(last & (tick == done + LAG))
    def _():
        total = local[:, columns(index)]
        for distance in range(1, size):
            plane_copy(distance).wait()
            total = total + landed[distance]

        @pl.when(me == 0)
        def _():
            along[0] = total
            line_copy(1).start()

        @pl.when(me == count - 1)
        def _():
            along[1] = total
            line_copy(-1).start()

    for way in (1, -1):
        place = me if way == 1 else count - 1 - me

        @pl.when((place > 0) & (tick == jnp.minimum(done + LAG + place, ticks - 1)))
        def _():
            line_copy(way).wait_recv()

            @pl.when(place < count - 1)
            def _():
                line_copy(way).start()

    @pl.when(tick == ticks - 1)
    def _():
        for way in (1, -1):
            place = me if way == 1 else count - 1 - me

            @pl.when(place < count - 1)
            def _():
                line_copy(way).wait_send()

        sums = along[0] + along[1]
        gains_ref[0:1] = sums[0:8].sum(0, keepdims=True)
        gains_ref[1:2] = sums[8:16].sum(0, keepdims=True)
        drain()


def chain_call(kernel, name, number, count, shape, inputs, outs, scratch):
    rows, width = shape
    chunks = rows // 2 // CHUNK
    arrays, in_specs = zip(*inputs)
    out_shape, out_specs = zip(*outs)
    return pl.pallas_call(
        kernel,
        out_shape=out_shape,
        grid=(tick_count(rows, count),),
        in_specs=in_specs,
        out_specs=out_specs,
        scratch_shapes=[
            pltpu.VMEM((2, rows // 2, width), jnp.bfloat16),
            pltpu.VMEM((rows, width), jnp.bfloat16),
            pltpu.SemaphoreType.DMA((4, chunks)),
            pltpu.SemaphoreType.DMA((4, chunks)),
            pltpu.SemaphoreType.DMA((2, chunks)),
            *scratch,
        ],
        compiler_params=pltpu.CompilerParams(
            collective_id=number, has_side_effects=True, vmem_limit_bytes=60 * 2**20
        ),
        cost_estimate=pl.CostEstimate(
            flops=100 * 10**9, bytes_accessed=12 * rows * width, transcendentals=0
        ),
        name=name,
    )(*arrays)


def far(shape, dtype):
    return jax.ShapeDtypeStruct(shape, dtype), HBM_SPEC


def kept(shape, dtype):
    return jax.ShapeDtypeStruct(shape, dtype), VMEM_SPEC


def sum_middle(mixed, both, tokens, gain, cotangent, count):
    rows, width = tokens.shape
    inner = mixed.shape[1]
    hidden = both.shape[0] - inner
    last = hidden // WIDE - 1
    at = lambda i: jnp.minimum(i // SPACING, last)
    return chain_call(
        functools.partial(middle_kernel, count, last + 1), "sum_middle", 1, count, tokens.shape,
        [
            (mixed, VMEM_SPEC),
            (both, pl.BlockSpec((inner, width), lambda i: (0, 0), pipeline_mode=pl.Buffered(1))),
            (tokens, HBM_SPEC), (gain, VMEM_SPEC), (cotangent, HBM_SPEC),
            (both, pl.BlockSpec((WIDE, width), lambda i: (inner // WIDE + at(i), 0))),
        ],
        [
            far(tokens.shape, jnp.bfloat16),
            far((rows // 2, width), jnp.float32),
            (
                jax.ShapeDtypeStruct((rows, hidden), jnp.float32),
                pl.BlockSpec((rows, WIDE), lambda i: (0, at(i))),
            ),
        ],
        [
            *[pltpu.VMEM(tokens.shape, jnp.bfloat16)] * 3,
            pltpu.VMEM((rows // 2, width), jnp.float32),
            pltpu.SemaphoreType.DMA((2,)),
            pltpu.SemaphoreType.DMA((rows // 2 // CHUNK,)),
        ],
    )


def sum_middle_back(part, middle, cotangent, gain, hidden, both, count):
    rows, width = part.shape
    last = width // WIDE - 1
    at = lambda i: jnp.minimum(i // SPACING, last)
    return chain_call(
        functools.partial(middle_back_kernel, count), "sum_middle_back", 2, count, part.shape,
        [
            (part, VMEM_SPEC), (middle, HBM_SPEC), (cotangent, HBM_SPEC), (gain, VMEM_SPEC),
            (hidden, HBM_SPEC), (both, pl.BlockSpec((both.shape[0], WIDE), lambda i: (0, at(i)))),
        ],
        [
            far(part.shape, jnp.bfloat16),
            far((rows // 2, width), jnp.float32),
            kept((8, width), jnp.float32),
            (
                jax.ShapeDtypeStruct(part.shape, jnp.bfloat16),
                pl.BlockSpec((rows, WIDE), lambda i: (0, at(i))),
            ),
        ],
        [
            pltpu.VMEM((rows // 2, width), jnp.float32),
            pltpu.VMEM(part.shape, jnp.bfloat16),
            pltpu.VMEM(hidden.shape, jnp.bfloat16),
            pltpu.VMEM((rows // 2, width), jnp.float32),
            pltpu.SemaphoreType.DMA((3,)),
            pltpu.SemaphoreType.DMA((rows // 2 // CHUNK,)),
        ],
    )


def sum_input_back(part, tokens, grad, gain, other, size, count):
    width = part.shape[1]
    plane = width // size
    return chain_call(
        functools.partial(input_back_kernel, count), "sum_input_back", 3, count, part.shape,
        [
            (part, VMEM_SPEC), (tokens, HBM_SPEC), (grad, HBM_SPEC), (gain, VMEM_SPEC),
            (other, VMEM_SPEC),
        ],
        [far(part.shape, jnp.bfloat16), kept((2, size), jnp.float32)],
        [
            pltpu.VMEM(part.shape, jnp.bfloat16),
            pltpu.VMEM(grad.shape, jnp.float32),
            pltpu.VMEM((16, width), jnp.float32),
            pltpu.VMEM((plane, 16, size), jnp.float32),
            pltpu.VMEM((2, 16, size), jnp.float32),
            pltpu.SemaphoreType.DMA((2,)),
            pltpu.SemaphoreType.DMA((plane,)),
            pltpu.SemaphoreType.DMA((plane,)),
            pltpu.SemaphoreType.DMA((2,)),
            pltpu.SemaphoreType.DMA((2,)),
        ],
    )


def rotate_pairs(values, cosine, sine):
    parts = [
        rotate_lanes(values[:, at : at + PAIR], cosine, sine)
        for at in range(0, values.shape[1], PAIR)
    ]
    return jnp.concatenate(parts, 1)


def plane_peers():
    ctx = lax.axis_size("ctx")
    size = lax.axis_size("shard") * ctx
    mine = lax.axis_index("shard") * ctx + lax.axis_index("ctx")

    def peer(distance):
        index = lax.rem(mine + distance, size)
        return index, {"shard": index // ctx, "ctx": lax.rem(index, ctx)}

    return size, mine, peer


def greet_plane(size, peer):
    barrier = pltpu.get_barrier_semaphore()
    for distance in range(1, size):
        pl.semaphore_signal(barrier, inc=1, device_id=peer(distance)[1], device_id_type=MESH)


def front_kernel(
    live_ref, tokens_ref, weight_ref, own_gain_ref, cos_ref, sin_ref,
    h_ref, q_ref, k_ref, v_ref, kp_ref, vp_ref, o_ref, l_ref, gain_ref,
    send, recv, gain_send, gain_recv,
):
    late = lax.axis_index("ctx")
    rows, width = q_ref.shape
    block = min(BLOCK, rows)
    blocks = rows // block
    pairs = width // PAIR
    size, index, peer = plane_peers()
    part = own_gain_ref.shape[1]
    greet_plane(size, peer)
    pl.semaphore_wait(pltpu.get_barrier_semaphore(), size - 1)
    mine = pl.ds(pl.multiple_of(index * part, part), part)
    gain_ref[:, mine] = own_gain_ref[...]

    def gain_copy(distance):
        return pltpu.make_async_remote_copy(
            src_ref=own_gain_ref, dst_ref=gain_ref.at[:, mine],
            send_sem=gain_send.at[distance], recv_sem=gain_recv.at[distance],
            device_id=peer(distance)[1], device_id_type=MESH,
        )

    for distance in range(1, size):
        gain_copy(distance).start()
    for distance in range(1, size):
        gain_copy(distance).wait()

    def here(at):
        return pl.ds(pl.multiple_of(at * block, block), block)

    def lanes(pair):
        return pl.ds(pl.multiple_of(pair * PAIR, PAIR), PAIR)

    @pl.loop(0, blocks)
    def _(at):
        stream = tokens_ref[here(at)].astype(jnp.float32)
        normed = (stream * unit_scale(stream) * gain_ref[0:1]).astype(jnp.bfloat16)
        h_ref[here(at)] = normed
        keys = dot(normed, weight_ref[1], (1, 0))
        k_ref[here(at)] = rotate_pairs(keys, cos_ref[here(at)], sin_ref[here(at)]).astype(jnp.bfloat16)
        v_ref[here(at)] = dot(normed, weight_ref[2], (1, 0)).astype(jnp.bfloat16)

    def exchange(pair):
        return [
            pltpu.make_async_remote_copy(
                src_ref=own.at[:, lanes(pair)], dst_ref=prev.at[:, lanes(pair)],
                send_sem=send.at[which, pair], recv_sem=recv.at[which, pair],
                device_id={"ctx": 1 - late}, device_id_type=MESH,
            )
            for which, own, prev in ((0, k_ref, kp_ref), (1, v_ref, vp_ref))
        ]

    @pl.when(late == 0)
    def _():
        @pl.loop(0, pairs)
        def _(pair):
            for copy in exchange(pair):
                copy.start()

    @pl.loop(0, blocks)
    def _(at):
        query = dot(h_ref[here(at)], weight_ref[0], (1, 0))
        query = rotate_pairs(query, cos_ref[here(at)], sin_ref[here(at)]) * 0.125
        q_ref[here(at)] = query.astype(jnp.bfloat16)

    def attend(pair, own, with_prev):
        column = lanes(pair)
        mine = slice(own * block, (own + 1) * block)
        query = q_ref[mine, column]
        mixed = []
        for head in range(2):
            queries = one_head(query, head)
            parts = []
            if with_prev:
                parts.append((dot(kp_ref[:, column], queries, (1, 1)), vp_ref[:, column]))
            if own:
                before = slice(0, own * block)
                parts.append((dot(k_ref[before, column], queries, (1, 1)), v_ref[before, column]))
            parts.append((causal(dot(k_ref[mine, column], queries, (1, 1))), v_ref[mine, column]))
            peak = parts[0][0].max(0, keepdims=True)
            for scores, _ in parts[1:]:
                peak = jnp.maximum(peak, scores.max(0, keepdims=True))
            expo = [jnp.exp(scores - peak) for scores, _ in parts]
            denom = expo[0].sum(0, keepdims=True)
            for e in expo[1:]:
                denom = denom + e.sum(0, keepdims=True)
            inverse = 1.0 / denom
            total = None
            for e, (_, value) in zip(expo, parts):
                term = dot(value, (e * inverse).astype(jnp.bfloat16), (0, 0))
                total = term if total is None else total + term
            mixed.append(total[head * HEAD : (head + 1) * HEAD])
            index = late * rows + own * block + lax.broadcasted_iota(jnp.int32, peak.shape, 1)
            l_ref[pair, head : head + 1, mine] = jnp.where(
                index < live_ref[0], peak + jnp.log(denom), -MASKED
            )
        result = jnp.concatenate(mixed, 0).T
        index = late * rows + own * block + lax.broadcasted_iota(jnp.int32, result.shape, 0)
        own_value = v_ref[mine, column].astype(jnp.float32)
        o_ref[mine, column] = jnp.where(index < live_ref[0], result, own_value).astype(jnp.bfloat16)

    @pl.loop(0, pairs)
    def _(pair):
        @pl.when(late == 0)
        def _():
            for own in range(blocks):
                attend(pair, own, False)

        @pl.when(late == 1)
        def _():
            for copy in exchange(pair):
                copy.wait_recv()
            for own in range(blocks):
                attend(pair, own, True)

    @pl.when(late == 0)
    def _():
        @pl.loop(0, pairs)
        def _(pair):
            for copy in exchange(pair):
                copy.wait_send()


def layer_front(live, tokens, weight, gain, cosine, sine):
    rows, depth = tokens.shape
    width = weight.shape[2]
    pairs = width // PAIR
    part = jax.ShapeDtypeStruct((rows, width), jnp.bfloat16)
    outs = (
        jax.ShapeDtypeStruct((rows, depth), jnp.bfloat16), part, part, part, part, part, part,
        jax.ShapeDtypeStruct((pairs, 2, rows), jnp.float32),
        jax.ShapeDtypeStruct((8, depth), jnp.float32),
    )
    size = lax.axis_size("shard") * lax.axis_size("ctx")
    return pl.pallas_call(
        front_kernel,
        out_shape=outs,
        in_specs=[SMEM_SPEC] + [VMEM_SPEC] * 5,
        out_specs=(VMEM_SPEC,) * len(outs),
        scratch_shapes=[pltpu.SemaphoreType.DMA((2, pairs))] * 2
        + [pltpu.SemaphoreType.DMA((size,))] * 2,
        compiler_params=pltpu.CompilerParams(
            collective_id=4, has_side_effects=True, vmem_limit_bytes=56 * 2**20
        ),
        cost_estimate=pl.CostEstimate(
            flops=80 * 10**9, bytes_accessed=40 * 2**20, transcendentals=0
        ),
        name="layer_front",
    )(live, tokens, weight, gain, cosine, sine)


def attend_back_kernel(
    count, live_ref, q_hbm, k_hbm, v_hbm, kp_hbm, vp_hbm, o_hbm, l_ref, cos_ref, sin_ref,
    part_ref, middle_hbm, grad_ref, both_hbm, dq_ref, dk_ref, dv_ref, out_ref,
    q_ref, k_ref, v_ref, kp_ref, vp_ref, o_ref, do_ref, weight_ref, middle_ref, early_sem, late_sem,
    dq_acc, dk_acc, dv_acc, dkp_acc, dvp_acc, leave, arrive, slots, send, recv, chain_send, chain_recv,
):
    late = lax.axis_index("ctx")
    me = lax.axis_index("tp")
    rows, width = q_ref.shape
    block = min(BLOCK, rows)
    blocks = rows // block
    pairs = width // PAIR
    load_early, wait_early = loads_of(
        [(both_hbm.at[pl.ds(0, width)], weight_ref), (middle_hbm, middle_ref)], early_sem
    )
    load_late, wait_late = loads_of(
        [
            (o_hbm, o_ref), (q_hbm, q_ref), (kp_hbm, kp_ref), (vp_hbm, vp_ref), (k_hbm, k_ref),
            (v_hbm, v_ref),
        ],
        late_sem,
    )
    load_early()
    load_late()
    barrier = pltpu.get_barrier_semaphore()
    pl.semaphore_signal(barrier, inc=1, device_id={"ctx": 1 - late}, device_id_type=MESH)
    greet(me, count, 1)
    tick, drain, ticks = chain_parts(
        count, part_ref, out_ref, slots, chain_send, chain_recv,
        lambda rows, part, total, at: (middle_ref[part] + total).astype(jnp.bfloat16), BACK_CHUNK, BACK_LAG,
    )

    def here(at):
        return pl.ds(pl.multiple_of(at * block, block), block)

    def lanes(pair):
        return pl.ds(pl.multiple_of(pair * PAIR, PAIR), PAIR)

    def prepare(pair, step):
        column = lanes(pair)
        query = q_ref[here(step), column]
        upstream = do_ref[here(step), column]
        product = (upstream.astype(jnp.float32) * o_ref[here(step), column].astype(jnp.float32)).T
        queries = [one_head(query, head) for head in range(2)]
        upstreams = [one_head(upstream, head) for head in range(2)]
        inner = [
            product[head * HEAD : (head + 1) * HEAD].sum(0, keepdims=True) for head in range(2)
        ]
        totals = [l_ref[pair, head : head + 1, here(step)] for head in range(2)]
        query_both = jnp.concatenate(queries, 0)
        upstream_both = jnp.concatenate(upstreams, 0)

        def tile(keys, values, masked):
            grads, probs_all, out = [], [], []
            for head in range(2):
                scores = dot(keys, queries[head], (1, 1))
                if masked:
                    scores = causal(scores)
                probs = jnp.exp(scores - totals[head])
                prob_grad = dot(values, upstreams[head], (1, 1))
                score_grad = (probs * (prob_grad - inner[head])).astype(jnp.bfloat16)
                probs_all.append(probs.astype(jnp.bfloat16))
                grads.append(score_grad)
                out.append(dot(keys, score_grad, (0, 0))[head * HEAD : (head + 1) * HEAD])
            key_grad = dot(jnp.concatenate(grads, 1), query_both, (1, 0))
            value_grad = dot(jnp.concatenate(probs_all, 1), upstream_both, (1, 0))
            return jnp.concatenate(out, 0), key_grad, value_grad

        return tile, upstream

    def exchange(pair):
        return pltpu.make_async_remote_copy(
            src_ref=leave.at[pair], dst_ref=arrive.at[pair], send_sem=send.at[pair],
            recv_sem=recv.at[pair], device_id={"ctx": 1 - late}, device_id_type=MESH,
        )

    def prev_step(pair, step):
        column = lanes(pair)
        tile, _ = prepare(pair, step)

        @pl.when(step == 0)
        def _():
            dkp_acc[...] = jnp.zeros_like(dkp_acc)
            dvp_acc[...] = jnp.zeros_like(dvp_acc)

        query_grad = None
        for at in range(blocks):
            mine = slice(at * block, (at + 1) * block)
            more, key_grad, value_grad = tile(kp_ref[mine, column], vp_ref[mine, column], False)
            query_grad = more if query_grad is None else query_grad + more
            dkp_acc[mine] += key_grad
            dvp_acc[mine] += value_grad
        dq_acc[pair, :, here(step)] = query_grad

        @pl.when(step == blocks - 1)
        def _():
            leave[pair, 0] = dkp_acc[...].astype(jnp.bfloat16)
            leave[pair, 1] = dvp_acc[...].astype(jnp.bfloat16)
            exchange(pair).start()

    def own_step(pair, step):
        column = lanes(pair)
        tile, upstream = prepare(pair, step)
        query_grad, key_grad, value_grad = tile(k_ref[here(step), column], v_ref[here(step), column], True)
        index = late * rows + step * block + lax.broadcasted_iota(jnp.int32, upstream.shape, 0)
        dk_acc[here(step), column] = key_grad
        dv_acc[here(step), column] = value_grad + jnp.where(
            index < live_ref[0], 0.0, upstream.astype(jnp.float32)
        )
        dq_acc[pair, :, here(step)] += query_grad

        @pl.loop(0, step)
        def _(at):
            more, key_grad, value_grad = tile(k_ref[here(at), column], v_ref[here(at), column], False)
            dk_acc[here(at), column] += key_grad
            dv_acc[here(at), column] += value_grad
            dq_acc[pair, :, here(step)] += more

        grad = dq_acc[pair, :, here(step)].T * 0.125
        grad = rotate_lanes(grad, cos_ref[here(step)], -sin_ref[here(step)])
        dq_ref[here(step), column] = grad.astype(jnp.bfloat16)

    @pl.when(late == 0)
    def _():
        dq_acc[...] = jnp.zeros_like(dq_acc)

    wait_early()

    @pl.loop(0, blocks)
    def _(at):
        for more in range(LEAD):
            tick(at * LEAD + more)
        do_ref[here(at)] = dot(grad_ref[here(at)], weight_ref[...], (1, 1)).astype(jnp.bfloat16)

    wait_late()
    steps = pairs * blocks
    lead = blocks * LEAD

    @pl.loop(0, 2 * steps)
    def _(at):
        @pl.when(lead + at < ticks)
        def _():
            tick(lead + at)

        @pl.when((late == 1) & (at < steps))
        def _():
            prev_step(at // blocks, at % blocks)

        @pl.when(at >= steps)
        def _():
            own_step((at - steps) // blocks, at % blocks)

    if ticks > lead + 2 * steps:
        pl.loop(lead + 2 * steps, ticks)(tick)

    @pl.loop(0, pairs)
    def _(pair):
        column = lanes(pair)

        @pl.when(late == 0)
        def _():
            exchange(pair).wait_recv()
            dk_acc[:, column] += arrive[pair, 0].astype(jnp.float32)
            dv_acc[:, column] += arrive[pair, 1].astype(jnp.float32)

        @pl.when(late == 1)
        def _():
            exchange(pair).wait_send()

        dk_ref[:, column] = rotate_lanes(dk_acc[:, column], cos_ref[...], -sin_ref[...]).astype(
            jnp.bfloat16
        )
        dv_ref[:, column] = dv_acc[:, column].astype(jnp.bfloat16)

    drain()


def attend_back(live, arrays, cosine, sine, out_part, middle, grad, both, count):
    rows, width = arrays[0].shape
    pairs = width // PAIR
    part = jax.ShapeDtypeStruct((rows, width), jnp.bfloat16)
    outs = (
        part, part, part, jax.ShapeDtypeStruct(out_part.shape, jnp.bfloat16),
    )
    chunks = rows // 2 // BACK_CHUNK
    return pl.pallas_call(
        functools.partial(attend_back_kernel, count),
        out_shape=outs,
        in_specs=[SMEM_SPEC] + [HBM_SPEC] * 6 + [VMEM_SPEC] * 4 + [HBM_SPEC, VMEM_SPEC, HBM_SPEC],
        out_specs=(VMEM_SPEC,) * len(outs),
        scratch_shapes=[
            *[pltpu.VMEM((rows, width), jnp.bfloat16)] * 7,
            pltpu.VMEM((width, middle.shape[1]), jnp.bfloat16),
            pltpu.VMEM(middle.shape, jnp.float32),
            pltpu.SemaphoreType.DMA((2,)),
            pltpu.SemaphoreType.DMA((6,)),
            pltpu.VMEM((pairs, PAIR, rows), jnp.float32),
            pltpu.VMEM((rows, width), jnp.float32),
            pltpu.VMEM((rows, width), jnp.float32),
            pltpu.VMEM((rows, PAIR), jnp.float32),
            pltpu.VMEM((rows, PAIR), jnp.float32),
            pltpu.VMEM((pairs, 2, rows, PAIR), jnp.bfloat16),
            pltpu.VMEM((pairs, 2, rows, PAIR), jnp.bfloat16),
            pltpu.VMEM((2, rows // 2, out_part.shape[1]), jnp.bfloat16),
            pltpu.SemaphoreType.DMA((pairs,)),
            pltpu.SemaphoreType.DMA((pairs,)),
            pltpu.SemaphoreType.DMA((4, chunks)),
            pltpu.SemaphoreType.DMA((4, chunks)),
        ],
        compiler_params=pltpu.CompilerParams(
            collective_id=5, has_side_effects=True, vmem_limit_bytes=58 * 2**20
        ),
        cost_estimate=pl.CostEstimate(
            flops=100 * 10**9, bytes_accessed=40 * 2**20, transcendentals=0
        ),
        name="attend_back",
    )(live, *arrays, cosine, sine, out_part, middle, grad, both)


def narrow_kernel(out_ref, down_ref, gate_up_ref, both_ref, low_ref):
    split = out_ref.shape[0]
    both_ref[:split] = out_ref[...].astype(jnp.bfloat16)
    both_ref[split:] = down_ref[...].astype(jnp.bfloat16)
    low_ref[...] = gate_up_ref[...].astype(jnp.bfloat16)


def narrow(out_weight, down_weight, gate_up_weight):
    return pl.pallas_call(
        narrow_kernel,
        out_shape=(
            jax.ShapeDtypeStruct(
                (out_weight.shape[0] + down_weight.shape[0], out_weight.shape[1]), jnp.bfloat16
            ),
            jax.ShapeDtypeStruct(gate_up_weight.shape, jnp.bfloat16),
        ),
        in_specs=[VMEM_SPEC] * 3,
        out_specs=(VMEM_SPEC,) * 2,
        compiler_params=pltpu.CompilerParams(vmem_limit_bytes=40 * 2**20),
        cost_estimate=pl.CostEstimate(flops=40 * 10**9, bytes_accessed=2**24, transcendentals=0),
        name="narrow",
    )(out_weight, down_weight, gate_up_weight)


def mlp_kernel(
    normed_ref, weight_ref, hidden_grad_ref, cotangent_ref,
    hidden_ref, down_grad_ref, gate_up_grad_ref, back_ref, turned, total,
):
    step = pl.program_id(0)

    @pl.when(step == 0)
    def _():
        turned[...] = normed_ref[...].T
        total[...] = jnp.zeros_like(total)

    gate = dot(normed_ref[...], weight_ref[0], (1, 0))
    upward = dot(normed_ref[...], weight_ref[1], (1, 0))
    hidden_grad = hidden_grad_ref[...]
    sigma = jax.nn.sigmoid(gate)
    swish = gate * sigma
    hidden = (swish * upward).astype(jnp.bfloat16)
    hidden_ref[...] = hidden
    gate_grad = (hidden_grad * upward * sigma * (1.0 + gate * (1.0 - sigma))).astype(jnp.bfloat16)
    upward_grad = (hidden_grad * swish).astype(jnp.bfloat16)
    both = jnp.concatenate([gate_grad, upward_grad], 1)
    weights = jnp.concatenate([weight_ref[0], weight_ref[1]], 1)
    total[...] += dot(both, weights, (1, 1))
    gate_up_grad_ref[0] = dot(turned[...], gate_grad, (1, 0)).astype(jnp.bfloat16)
    gate_up_grad_ref[1] = dot(turned[...], upward_grad, (1, 0)).astype(jnp.bfloat16)
    down_grad_ref[...] = dot(hidden.T, cotangent_ref[...], (1, 0)).astype(jnp.bfloat16)

    @pl.when(step == pl.num_programs(0) - 1)
    def _():
        back_ref[...] = total[...].astype(jnp.bfloat16)


def mlp(normed, weight, hidden_grad, cotangent):
    rows, depth = normed.shape
    width = weight.shape[2]
    whole = pl.BlockSpec((rows, depth), lambda j: (0, 0), pipeline_mode=pl.Buffered(1))
    return pl.pallas_call(
        mlp_kernel,
        out_shape=(
            jax.ShapeDtypeStruct((rows, width), jnp.bfloat16),
            jax.ShapeDtypeStruct((width, depth), jnp.bfloat16),
            jax.ShapeDtypeStruct((2, depth, width), jnp.bfloat16),
            jax.ShapeDtypeStruct((rows, depth), jnp.bfloat16),
        ),
        grid=(width // MLP_WIDE,),
        in_specs=[
            whole,
            pl.BlockSpec((2, depth, MLP_WIDE), lambda j: (0, 0, j)),
            pl.BlockSpec((rows, MLP_WIDE), lambda j: (0, j)),
            whole,
        ],
        out_specs=(
            pl.BlockSpec((rows, MLP_WIDE), lambda j: (0, j)),
            pl.BlockSpec((MLP_WIDE, depth), lambda j: (j, 0)),
            pl.BlockSpec((2, depth, MLP_WIDE), lambda j: (0, 0, j)),
            pl.BlockSpec((rows, depth), lambda j: (0, 0)),
        ),
        scratch_shapes=[
            pltpu.VMEM((depth, rows), jnp.bfloat16), pltpu.VMEM((rows, depth), jnp.float32),
        ],
        compiler_params=pltpu.CompilerParams(vmem_limit_bytes=60 * 2**20),
        cost_estimate=pl.CostEstimate(
            flops=14 * rows * depth * width, bytes_accessed=80 * 2**20, transcendentals=rows * width
        ),
        name="mlp",
    )(normed, weight, hidden_grad, cotangent)


def projection_back_kernel(
    normed_ref, weight_ref, dq_ref, dk_ref, dv_ref, mixed_ref, middle_ref, grad_ref, back_ref,
    turned, total,
):
    step = pl.program_id(0)

    @pl.when(step == 0)
    def _():
        turned[...] = normed_ref[...].T

    for at, ref in enumerate((dq_ref, dk_ref, dv_ref)):

        @pl.when(step == at)
        def _():
            term = dot(ref[...], weight_ref[0], (1, 1))
            if at == 0:
                total[...] = term
            elif at == 1:
                total[...] += term
            else:
                back_ref[...] = (total[...] + term).astype(jnp.bfloat16)
            grad_ref[0] = dot(turned[...], ref[...], (1, 0)).astype(jnp.bfloat16)

    @pl.when(step == 3)
    def _():
        turned[...] = middle_ref[...].T
        grad_ref[0] = dot(turned[...], mixed_ref[...], (1, 0)).astype(jnp.bfloat16)


def projection_back(normed, weight, dq, dk, dv, mixed, middle):
    rows, depth = normed.shape
    width = dq.shape[1]
    whole = lambda w: pl.BlockSpec((rows, w), lambda j: (0, 0), pipeline_mode=pl.Buffered(1))
    return pl.pallas_call(
        projection_back_kernel,
        out_shape=(
            jax.ShapeDtypeStruct((4, depth, width), jnp.bfloat16),
            jax.ShapeDtypeStruct((rows, depth), jnp.bfloat16),
        ),
        grid=(4,),
        in_specs=[
            whole(depth),
            pl.BlockSpec((1, depth, width), lambda j: (jnp.minimum(j, 2), 0, 0)),
            whole(width), whole(width), whole(width), whole(width), whole(depth),
        ],
        out_specs=(
            pl.BlockSpec((1, depth, width), lambda j: (j, 0, 0)),
            pl.BlockSpec((rows, depth), lambda j: (0, 0)),
        ),
        scratch_shapes=[
            pltpu.VMEM((depth, rows), jnp.bfloat16), pltpu.VMEM((rows, depth), jnp.float32),
        ],
        compiler_params=pltpu.CompilerParams(vmem_limit_bytes=60 * 2**20),
        cost_estimate=pl.CostEstimate(
            flops=14 * rows * depth * width, bytes_accessed=40 * 2**20, transcendentals=0
        ),
        name="projection_back",
    )(normed, weight, dq, dk, dv, mixed, middle)


def tail_kernel(
    grad_ref, out_grad_ref, w_ref, m_ref, s_ref, ow_ref, om_ref, os_ref,
    g_out, w_out, m_out, s_out, og_out, step_out, om_out, os_out,
):
    grad = grad_ref[0:3].astype(jnp.float32)
    update, first, second = adam_update(w_ref[...], m_ref[...], s_ref[...], grad, decay_rate)
    g_out[...] = grad
    w_out[...] = w_ref[...] - update
    m_out[...] = first
    s_out[...] = second
    grad = out_grad_ref[0].astype(jnp.float32).T
    update, first, second = adam_update(ow_ref[...], om_ref[...], os_ref[...], grad, decay_rate)
    og_out[...] = grad
    step_out[...] = update
    om_out[...] = first
    os_out[...] = second


def adam_tail(grads, qkv, out):
    planes, rows, width = qkv[0].shape
    steps = width // PAIR
    mine = pl.BlockSpec((planes, rows // steps, width), lambda i: (0, i, 0))
    other = pl.BlockSpec((PAIR, rows), lambda i: (i, 0))
    shapes = [jax.ShapeDtypeStruct(qkv[0].shape, jnp.float32)] * 4
    shapes += [jax.ShapeDtypeStruct(out[0].shape, jnp.float32)] * 4
    results = pl.pallas_call(
        tail_kernel,
        out_shape=tuple(shapes),
        grid=(steps,),
        in_specs=[
            pl.BlockSpec((planes + 1, rows // steps, width), lambda i: (0, i, 0)),
            pl.BlockSpec((1, rows, PAIR), lambda i: (planes, 0, i)),
            mine, mine, mine, other, other, other,
        ],
        out_specs=(mine,) * 4 + (other,) * 4,
        compiler_params=pltpu.CompilerParams(vmem_limit_bytes=40 * 2**20),
        cost_estimate=pl.CostEstimate(
            flops=10**7, bytes_accessed=16 * 2**20, transcendentals=0
        ),
        name="adam_tail",
    )(grads, grads, *qkv, *out)
    return results[:4], results[4:]


def scatter_low(grad, axis=1):
    return lax.psum_scatter(
        grad.astype(jnp.bfloat16), ("shard", "ctx"), scatter_dimension=axis, tiled=True
    ).astype(jnp.float32)


def after(array, *others):
    return lax.optimization_barrier((array, *others))[0]


def adam_update(weight, first, second, grad, decay):
    first_new = beta_one * first + (1.0 - beta_one) * grad
    second_new = beta_two * second + (1.0 - beta_two) * grad * grad
    first_hat = first_new / (1.0 - beta_one**step_count)
    second_hat = second_new / (1.0 - beta_two**step_count)
    update = learn_rate * (first_hat / (jnp.sqrt(second_hat) + adam_eps) + decay * weight)
    return (update, first_new, second_new)


def body(
    tokens,
    cotangent,
    lengths,
    qkv_weight,
    out_weight,
    gate_up_weight,
    down_weight,
    norm_gains,
    qkv_first,
    out_first,
    gate_up_first,
    down_first,
    gains_first,
    qkv_second,
    out_second,
    gate_up_second,
    down_second,
    gains_second,
):
    row_count = tokens.shape[0]
    count = lax.axis_size("tp")
    offset = lax.axis_index("ctx") * row_count
    query_index = offset + jnp.arange(row_count, dtype=jnp.int32)
    qkv_low = qkv_weight.astype(jnp.bfloat16)
    both_low, gate_up_low = narrow(out_weight, down_weight, gate_up_weight)
    gains_low = norm_gains.astype(jnp.bfloat16).astype(jnp.float32)
    gains_low = jnp.concatenate([gains_low] * 4, 0)
    gather = lambda a: lax.all_gather(a, ("shard", "ctx"), axis=1, tiled=True)
    qkv_full = gather(qkv_low)
    both_full = gather(after(both_low, qkv_full))
    cosine, sine = rotation(query_index, HEAD)
    cosine, sine = (jnp.concatenate([c[:, 0]] * 4, 1) for c in (cosine, sine))
    normed_one, query, keys, values, keys_prev, values_prev, mixed_low, totals, gains_full = layer_front(
        lengths, tokens, qkv_full, gains_low, cosine, sine
    )
    gain_one, gain_two = gains_full[0:1], gains_full[1:2]
    gate_up_full = gather(after(gate_up_low, both_full, totals))
    normed_two, middle, hidden_grad = sum_middle(
        mixed_low, both_full, tokens, gain_two, cotangent, count
    )
    hidden, down_grad_local, gate_up_grad_local, mlp_back_part = mlp(
        normed_two, gate_up_full, hidden_grad, cotangent
    )
    down_grad = scatter_low(down_grad_local)
    middle_low, middle_grad, gain_two_grad, out_part = sum_middle_back(
        mlp_back_part, middle, cotangent, gain_two, hidden, both_full, count
    )
    gate_up_grad = scatter_low(after(gate_up_grad_local, down_grad, middle_low))
    query_low, key_low, value_low, out_tokens = attend_back(
        lengths,
        [query, keys, values, keys_prev, values_prev, mixed_low, totals],
        cosine, sine, out_part, middle, middle_low, both_full, count,
    )
    qkv_grad_local, attn_back_part = projection_back(
        normed_one, qkv_full, query_low, key_low, value_low, mixed_low, middle_low
    )
    attn_back_part, qkv_grad_local, _ = lax.optimization_barrier(
        (attn_back_part, qkv_grad_local, gate_up_grad)
    )
    tail_grads = lax.psum_scatter(
        qkv_grad_local, ("shard", "ctx"), scatter_dimension=1, tiled=True
    )
    input_grad, gains_grad = sum_input_back(
        attn_back_part, tokens, middle_grad, gain_one, gain_two_grad, norm_gains.shape[1], count
    )
    tail_grads, _ = lax.optimization_barrier((tail_grads, gains_grad))
    (qkv_grad, qkv_new, qkv_first_new, qkv_second_new), (
        out_grad, out_step, out_first_new, out_second_new,
    ) = adam_tail(
        tail_grads,
        (qkv_weight, qkv_first, qkv_second),
        (out_weight, out_first, out_second),
    )
    gate_up_step, gate_up_first_new, gate_up_second_new = adam_update(
        gate_up_weight, gate_up_first, gate_up_second, gate_up_grad, decay_rate
    )
    down_step, down_first_new, down_second_new = adam_update(
        down_weight, down_first, down_second, down_grad, decay_rate
    )
    gains_step, gains_first_new, gains_second_new = adam_update(
        norm_gains, gains_first, gains_second, gains_grad, 0.0
    )
    gate_up_new = gate_up_weight - gate_up_step
    down_new = down_weight - down_step
    return (
        out_tokens,
        input_grad,
        qkv_grad,
        out_grad,
        gate_up_grad,
        down_grad,
        gains_grad,
        qkv_new,
        out_step,
        gate_up_new,
        down_new,
        gains_step,
        qkv_first_new,
        out_first_new,
        gate_up_first_new,
        down_first_new,
        gains_first_new,
        qkv_second_new,
        out_second_new,
        gate_up_second_new,
        down_second_new,
        gains_second_new,
    )


def solution(mesh):
    return jax.shard_map(
        body,
        mesh=mesh,
        in_specs=(
            P(("shard", "ctx"), None),
            P(("shard", "ctx"), None),
            P("shard"),
            P(None, ("shard", "ctx"), "tp"),
            P("tp", ("shard", "ctx")),
            P(None, ("shard", "ctx"), "tp"),
            P("tp", ("shard", "ctx")),
            P(None, ("shard", "ctx")),
            P(None, ("shard", "ctx"), "tp"),
            P("tp", ("shard", "ctx")),
            P(None, ("shard", "ctx"), "tp"),
            P("tp", ("shard", "ctx")),
            P(None, ("shard", "ctx")),
            P(None, ("shard", "ctx"), "tp"),
            P("tp", ("shard", "ctx")),
            P(None, ("shard", "ctx"), "tp"),
            P("tp", ("shard", "ctx")),
            P(None, ("shard", "ctx")),
        ),
        out_specs=(
            P(("shard", "ctx"), None),
            P(("shard", "ctx"), None),
            P(None, ("shard", "ctx"), "tp"),
            P("tp", ("shard", "ctx")),
            P(None, ("shard", "ctx"), "tp"),
            P("tp", ("shard", "ctx")),
            P(None, ("shard", "ctx")),
            P(None, ("shard", "ctx"), "tp"),
            P("tp", ("shard", "ctx")),
            P(None, ("shard", "ctx"), "tp"),
            P("tp", ("shard", "ctx")),
            P(None, ("shard", "ctx")),
            P(None, ("shard", "ctx"), "tp"),
            P("tp", ("shard", "ctx")),
            P(None, ("shard", "ctx"), "tp"),
            P("tp", ("shard", "ctx")),
            P(None, ("shard", "ctx")),
            P(None, ("shard", "ctx"), "tp"),
            P("tp", ("shard", "ctx")),
            P(None, ("shard", "ctx"), "tp"),
            P("tp", ("shard", "ctx")),
            P(None, ("shard", "ctx")),
        ),
        check_vma=False,
    )
```

```python
import functools
import jax
import jax.numpy as jnp
from jax import lax
from jax.experimental import pallas as pl
from jax.experimental.pallas import tpu as pltpu
from jax.sharding import PartitionSpec as P

HEAD = 64
PAIR = 128
BLOCK = 256
CHUNK = 16
LAG = 2
BACK_CHUNK = 32
BACK_LAG = 3
WIDE = 256
SPACING = 5
LEAD = 1
MLP_WIDE = 256
MASKED = -1e30
MESH = pl.DeviceIdType.MESH
VMEM_SPEC = pl.BlockSpec(memory_space=pltpu.VMEM)
SMEM_SPEC = pl.BlockSpec(memory_space=pltpu.SMEM)
HBM_SPEC = pl.BlockSpec(memory_space=pl.ANY)


norm_eps = 1e-05
rope_base = 130000.0
beta_one = 0.9
beta_two = 0.95
learn_rate = 0.02
decay_rate = 0.1
adam_eps = 1e-08
step_count = 4.0


def rotation(position, head_size):
    half = head_size // 2
    freqs = rope_base ** (-(jnp.arange(half, dtype=jnp.float32) * 2.0) / head_size)
    angle = position.astype(jnp.float32)[:, None] * freqs[None, :]
    return (jnp.cos(angle)[:, None, :], jnp.sin(angle)[:, None, :])


def dot(left, right, contract):
    return lax.dot_general(
        left, right, ((contract[:1], contract[1:]), ((), ())), preferred_element_type=jnp.float32
    )


def one_head(values, head):
    lane = lax.broadcasted_iota(jnp.int32, values.shape, 1)
    return jnp.where((lane < HEAD) == (head == 0), values, jnp.zeros_like(values))


def causal(scores):
    key = lax.broadcasted_iota(jnp.int32, scores.shape, 0)
    query = lax.broadcasted_iota(jnp.int32, scores.shape, 1)
    return jnp.where(key <= query, scores, MASKED)


def rotate_lanes(values, cosine, sine):
    lane = lax.broadcasted_iota(jnp.int32, values.shape, 1) % HEAD
    width = values.shape[1]
    ahead = pltpu.roll(values, width - HEAD // 2, 1)
    behind = pltpu.roll(values, HEAD // 2, 1)
    return values * cosine + jnp.where(lane < HEAD // 2, -ahead, behind) * sine


def greet(me, count, more=0, more_ends=0):
    barrier = pltpu.get_barrier_semaphore()

    @pl.when(me > 0)
    def _():
        pl.semaphore_signal(barrier, inc=1, device_id={"tp": me - 1}, device_id_type=MESH)

    @pl.when(me < count - 1)
    def _():
        pl.semaphore_signal(barrier, inc=1, device_id={"tp": me + 1}, device_id_type=MESH)

    @pl.when((me > 0) & (me < count - 1))
    def _():
        pl.semaphore_wait(barrier, 2 + more)

    @pl.when((me == 0) | (me == count - 1))
    def _():
        pl.semaphore_wait(barrier, 1 + more + more_ends)


def chain_parts(count, part_ref, out_ref, slots, send, recv, finish, size, lag=1, land=None, stored=None):
    me = lax.axis_index("tp")
    apart = land is not None
    land = land if apart else out_ref
    half = out_ref.shape[0] // 2
    chunks = half // size

    def copy(stream, at, source, target, device):
        return pltpu.make_async_remote_copy(
            src_ref=source, dst_ref=target, send_sem=send.at[stream, at],
            recv_sem=recv.at[stream, at], device_id={"tp": device}, device_id_type=MESH,
        )

    def ends(way):
        place = me if way == 1 else count - 1 - me
        return place, me + way

    def reduce_copy(way, at, device):
        index = 0 if way == 1 else 1
        rows = pl.ds(pl.multiple_of(at * size, size), size)
        return copy(index, at, slots.at[index, rows], slots.at[index, rows], device)

    def spread_copy(way, at, device):
        base = 0 if way == 1 else half
        rows = pl.ds(pl.multiple_of(base + at * size, size), size)
        return copy(2 if way == 1 else 3, at, land.at[rows], land.at[rows], device)

    def store_copy(index, at):
        rows = pl.ds(pl.multiple_of(index * half + at * size, size), size)
        return pltpu.make_async_copy(land.at[rows], out_ref.at[rows], stored.at[index, at])

    def reduce_step(way, tick):
        place, ahead = ends(way)
        index = 0 if way == 1 else 1
        base = half if way == 1 else 0
        at = tick - lag * place

        @pl.when((at >= 0) & (at < chunks))
        def _():
            local = pl.ds(pl.multiple_of(at * size, size), size)
            rows = pl.ds(pl.multiple_of(base + at * size, size), size)

            @pl.when(place == 0)
            def _():
                slots[index, local] = part_ref[rows]

            @pl.when(place > 0)
            def _():
                reduce_copy(way, at, ahead).wait_recv()

            @pl.when((place > 0) & (place < count - 1))
            def _():
                slots[index, local] = (
                    slots[index, local].astype(jnp.float32) + part_ref[rows].astype(jnp.float32)
                ).astype(jnp.bfloat16)

            @pl.when(place < count - 1)
            def _():
                reduce_copy(way, at, ahead).start()

            @pl.when(place == count - 1)
            def _():
                total = slots[index, local].astype(jnp.float32) + part_ref[rows].astype(jnp.float32)
                land[rows] = finish(rows, local, total, at)
                if apart:
                    store_copy(1 if way == 1 else 0, at).start()
                spread_copy(-way, at, me - way).start()

    def spread_step(way, tick):
        place, ahead = ends(way)
        at = tick - lag * (count - 1) - lag * place

        @pl.when((at >= 0) & (at < chunks) & (place > 0))
        def _():
            spread_copy(way, at, ahead).wait_recv()

            @pl.when(place < count - 1)
            def _():
                spread_copy(way, at, ahead).start()

            if apart:
                store_copy(0 if way == 1 else 1, at).start()

    def step(tick):
        for way in (1, -1):
            reduce_step(way, tick)
        for way in (1, -1):
            spread_step(way, tick)

    def drain():
        @pl.loop(0, chunks)
        def _(at):
            if apart:
                for index in range(2):
                    store_copy(index, at).wait()

            for way in (1, -1):
                place, ahead = ends(way)

                @pl.when(place < count - 1)
                def _():
                    reduce_copy(way, at, ahead).wait_send()
                    spread_copy(way, at, ahead).wait_send()

    return step, drain, chunks + 2 * lag * (count - 1)


def run_ticks(parts, start, wait, finally_drain):
    step, drain, ticks = parts
    tick = pl.program_id(0)
    pl.when(tick == 0)(start)
    pl.when(tick == SPACING - 2)(wait)
    step(tick)

    @pl.when(tick == ticks - 1)
    def _():
        drain()
        finally_drain()

    return tick


def tick_count(rows, count):
    return rows // 2 // CHUNK + 2 * LAG * (count - 1)


def unit_scale(stream):
    return lax.rsqrt(jnp.mean(stream * stream, axis=-1, keepdims=True) + norm_eps)


def fold(values):
    return values.reshape(-1, 8, values.shape[1]).sum(0)


def norm_back(stream, gain, upstream):
    scale = unit_scale(stream)
    gain_grad = fold(upstream * stream * scale)
    inner = jnp.sum(upstream * gain * stream, axis=-1, keepdims=True)
    grad = scale * gain * upstream - stream * (scale * scale * scale / stream.shape[-1]) * inner
    return grad, gain_grad


def loads_of(pairs, sems):
    copies = [
        pltpu.make_async_copy(source, target, sems.at[at])
        for at, (source, target) in enumerate(pairs)
    ]

    def start():
        for copy in copies:
            copy.start()

    def wait():
        for copy in copies:
            copy.wait()

    return start, wait


def half_store(source, target, sems, count):
    chunks = source.shape[0] // CHUNK
    me = lax.axis_index("tp")

    def copy(at):
        rows = pl.ds(pl.multiple_of(at * CHUNK, CHUNK), CHUNK)
        return pltpu.make_async_copy(source.at[rows], target.at[rows], sems.at[at])

    def drain():
        @pl.when((me == 0) | (me == count - 1))
        def _():
            @pl.loop(0, chunks)
            def _(at):
                copy(at).wait()

    return copy, drain


def middle_kernel(
    count, blocks, mixed_ref, weight_ref, tokens_hbm, gain_ref, cotangent_hbm, down_ref,
    out_ref, middle_ref, hidden_grad_ref,
    slots, land, send, recv, stored, part_ref, tokens_ref, cotangent_ref, middle, load_sem, half_sem,
):
    load, wait = loads_of([(tokens_hbm, tokens_ref), (cotangent_hbm, cotangent_ref)], load_sem)
    half_copy, half_drain = half_store(middle, middle_ref, half_sem, count)

    def start():
        load()
        greet(lax.axis_index("tp"), count)

        project(0)

    half_blocks = part_ref.shape[0] // 2 // BLOCK

    def project(at):
        for half in range(2):
            here = pl.ds(pl.multiple_of((half * half_blocks + at) * BLOCK, BLOCK), BLOCK)
            part_ref[here] = dot(mixed_ref[here], weight_ref[...], (1, 0)).astype(jnp.bfloat16)

    def finish(rows, local, total, at):
        value = tokens_ref[rows].astype(jnp.float32) + total
        middle[local] = value
        half_copy(at).start()
        return (value * unit_scale(value) * gain_ref[1:2]).astype(jnp.bfloat16)

    parts = chain_parts(
        count, part_ref, out_ref, slots, send, recv, finish, CHUNK, LAG, land, stored
    )
    tick = run_ticks(parts, start, wait, half_drain)

    @pl.when((tick >= 1) & (tick < half_blocks))
    def _():
        project(tick)

    @pl.when((tick % SPACING == SPACING - 1) & (tick < blocks * SPACING))
    def _():
        hidden_grad_ref[...] = dot(cotangent_ref[...], down_ref[...], (1, 1))


def middle_back_kernel(
    count, part_ref, middle_hbm, cotangent_hbm, gain_ref, hidden_hbm, down_ref,
    out_ref, grad_ref, gain_grad_ref, layer_ref,
    slots, land, send, recv, stored, middle_ref, cotangent_ref, hidden_ref, grad, load_sem, half_sem,
):
    load, wait = loads_of(
        [(middle_hbm, middle_ref), (cotangent_hbm, cotangent_ref), (hidden_hbm, hidden_ref)],
        load_sem,
    )
    half_copy, half_drain = half_store(grad, grad_ref, half_sem, count)

    def start():
        load()
        greet(lax.axis_index("tp"), count)
        gain_grad_ref[...] = jnp.zeros_like(gain_grad_ref)

    def finish(rows, local, total, at):
        value, gain_grad = norm_back(middle_ref[local], gain_ref[1:2], total)
        gain_grad_ref[...] += gain_grad
        value = cotangent_ref[rows].astype(jnp.float32) + value
        grad[local] = value
        half_copy(at).start()
        return value.astype(jnp.bfloat16)

    parts = chain_parts(
        count, part_ref, out_ref, slots, send, recv, finish, CHUNK, LAG, land, stored
    )
    tick = run_ticks(parts, start, wait, half_drain)

    @pl.when((tick % SPACING == SPACING - 1) & (tick < part_ref.shape[1] // WIDE * SPACING))
    def _():
        skip = down_ref.shape[0] - hidden_ref.shape[1]
        layer_ref[...] = dot(hidden_ref[...], down_ref[skip:], (1, 0)).astype(jnp.bfloat16)


def input_back_kernel(
    count, part_ref, tokens_hbm, grad_hbm, gain_ref, other_ref, out_ref, gains_ref,
    slots, land, send, recv, stored, tokens_ref, grad_ref, local, landed, along,
    load_sem, plane_send, plane_recv, line_send, line_recv,
):
    load, wait = loads_of([(tokens_hbm, tokens_ref), (grad_hbm, grad_ref)], load_sem)

    me = lax.axis_index("tp")
    size, index, peer = plane_peers()
    width = gains_ref.shape[1]
    last = (me == 0) | (me == count - 1)

    def start():
        load()

        @pl.when(last)
        def _():
            greet_plane(size, peer)

        greet(me, count, 0, size - 1)
        local[0:8] = jnp.zeros((8, local.shape[1]), jnp.float32)
        local[8:16] = other_ref[...]

    def finish(rows, part, total, at):
        grad, gain_grad = norm_back(tokens_ref[rows].astype(jnp.float32), gain_ref[0:1], total)
        local[0:8] += gain_grad
        return (grad_ref[part] + grad).astype(jnp.bfloat16)

    step, drain, ticks = chain_parts(
        count, part_ref, out_ref, slots, send, recv, finish, CHUNK, LAG, land, stored
    )

    def columns(at):
        return pl.ds(pl.multiple_of(at * width, width), width)

    def plane_copy(distance):
        at, device = peer(distance)
        return pltpu.make_async_remote_copy(
            src_ref=local.at[:, columns(at)], dst_ref=landed.at[distance],
            send_sem=plane_send.at[distance], recv_sem=plane_recv.at[distance],
            device_id=device, device_id_type=MESH,
        )

    def line_copy(way):
        which = 0 if way == 1 else 1
        return pltpu.make_async_remote_copy(
            src_ref=along.at[which], dst_ref=along.at[which],
            send_sem=line_send.at[which], recv_sem=line_recv.at[which],
            device_id={"tp": me + way}, device_id_type=MESH,
        )

    done = out_ref.shape[0] // 2 // CHUNK + LAG * (count - 1)

    tick = pl.program_id(0)
    pl.when(tick == 0)(start)
    pl.when(tick == SPACING - 2)(wait)
    step(tick)

    @pl.when(last & (tick == done - 1))
    def _():
        for distance in range(1, size):
            plane_copy(distance).start()

    @pl.when(last & (tick == done + LAG))
    def _():
        total = local[:, columns(index)]
        for distance in range(1, size):
            plane_copy(distance).wait()
            total = total + landed[distance]

        @pl.when(me == 0)
        def _():
            along[0] = total
            line_copy(1).start()

        @pl.when(me == count - 1)
        def _():
            along[1] = total
            line_copy(-1).start()

    for way in (1, -1):
        place = me if way == 1 else count - 1 - me

        @pl.when((place > 0) & (tick == jnp.minimum(done + LAG + place, ticks - 1)))
        def _():
            line_copy(way).wait_recv()

            @pl.when(place < count - 1)
            def _():
                line_copy(way).start()

    @pl.when(tick == ticks - 1)
    def _():
        for way in (1, -1):
            place = me if way == 1 else count - 1 - me

            @pl.when(place < count - 1)
            def _():
                line_copy(way).wait_send()

        sums = along[0] + along[1]
        gains_ref[0:1] = sums[0:8].sum(0, keepdims=True)
        gains_ref[1:2] = sums[8:16].sum(0, keepdims=True)
        drain()


def chain_call(kernel, name, number, count, shape, inputs, outs, scratch):
    rows, width = shape
    chunks = rows // 2 // CHUNK
    arrays, in_specs = zip(*inputs)
    out_shape, out_specs = zip(*outs)
    return pl.pallas_call(
        kernel,
        out_shape=out_shape,
        grid=(tick_count(rows, count),),
        in_specs=in_specs,
        out_specs=out_specs,
        scratch_shapes=[
            pltpu.VMEM((2, rows // 2, width), jnp.bfloat16),
            pltpu.VMEM((rows, width), jnp.bfloat16),
            pltpu.SemaphoreType.DMA((4, chunks)),
            pltpu.SemaphoreType.DMA((4, chunks)),
            pltpu.SemaphoreType.DMA((2, chunks)),
            *scratch,
        ],
        compiler_params=pltpu.CompilerParams(
            collective_id=number, has_side_effects=True, vmem_limit_bytes=60 * 2**20
        ),
        cost_estimate=pl.CostEstimate(
            flops=100 * 10**9, bytes_accessed=12 * rows * width, transcendentals=0
        ),
        name=name,
    )(*arrays)


def far(shape, dtype):
    return jax.ShapeDtypeStruct(shape, dtype), HBM_SPEC


def kept(shape, dtype):
    return jax.ShapeDtypeStruct(shape, dtype), VMEM_SPEC


def sum_middle(mixed, both, tokens, gain, cotangent, count):
    rows, width = tokens.shape
    inner = mixed.shape[1]
    hidden = both.shape[0] - inner
    last = hidden // WIDE - 1
    at = lambda i: jnp.minimum(i // SPACING, last)
    return chain_call(
        functools.partial(middle_kernel, count, last + 1), "sum_middle", 1, count, tokens.shape,
        [
            (mixed, VMEM_SPEC),
            (both, pl.BlockSpec((inner, width), lambda i: (0, 0), pipeline_mode=pl.Buffered(1))),
            (tokens, HBM_SPEC), (gain, VMEM_SPEC), (cotangent, HBM_SPEC),
            (both, pl.BlockSpec((WIDE, width), lambda i: (inner // WIDE + at(i), 0))),
        ],
        [
            far(tokens.shape, jnp.bfloat16),
            far((rows // 2, width), jnp.float32),
            (
                jax.ShapeDtypeStruct((rows, hidden), jnp.float32),
                pl.BlockSpec((rows, WIDE), lambda i: (0, at(i))),
            ),
        ],
        [
            *[pltpu.VMEM(tokens.shape, jnp.bfloat16)] * 3,
            pltpu.VMEM((rows // 2, width), jnp.float32),
            pltpu.SemaphoreType.DMA((2,)),
            pltpu.SemaphoreType.DMA((rows // 2 // CHUNK,)),
        ],
    )


def sum_middle_back(part, middle, cotangent, gain, hidden, both, count):
    rows, width = part.shape
    last = width // WIDE - 1
    at = lambda i: jnp.minimum(i // SPACING, last)
    return chain_call(
        functools.partial(middle_back_kernel, count), "sum_middle_back", 2, count, part.shape,
        [
            (part, VMEM_SPEC), (middle, HBM_SPEC), (cotangent, HBM_SPEC), (gain, VMEM_SPEC),
            (hidden, HBM_SPEC), (both, pl.BlockSpec((both.shape[0], WIDE), lambda i: (0, at(i)))),
        ],
        [
            far(part.shape, jnp.bfloat16),
            far((rows // 2, width), jnp.float32),
            kept((8, width), jnp.float32),
            (
                jax.ShapeDtypeStruct(part.shape, jnp.bfloat16),
                pl.BlockSpec((rows, WIDE), lambda i: (0, at(i))),
            ),
        ],
        [
            pltpu.VMEM((rows // 2, width), jnp.float32),
            pltpu.VMEM(part.shape, jnp.bfloat16),
            pltpu.VMEM(hidden.shape, jnp.bfloat16),
            pltpu.VMEM((rows // 2, width), jnp.float32),
            pltpu.SemaphoreType.DMA((3,)),
            pltpu.SemaphoreType.DMA((rows // 2 // CHUNK,)),
        ],
    )


def sum_input_back(part, tokens, grad, gain, other, size, count):
    width = part.shape[1]
    plane = width // size
    return chain_call(
        functools.partial(input_back_kernel, count), "sum_input_back", 3, count, part.shape,
        [
            (part, VMEM_SPEC), (tokens, HBM_SPEC), (grad, HBM_SPEC), (gain, VMEM_SPEC),
            (other, VMEM_SPEC),
        ],
        [far(part.shape, jnp.bfloat16), kept((2, size), jnp.float32)],
        [
            pltpu.VMEM(part.shape, jnp.bfloat16),
            pltpu.VMEM(grad.shape, jnp.float32),
            pltpu.VMEM((16, width), jnp.float32),
            pltpu.VMEM((plane, 16, size), jnp.float32),
            pltpu.VMEM((2, 16, size), jnp.float32),
            pltpu.SemaphoreType.DMA((2,)),
            pltpu.SemaphoreType.DMA((plane,)),
            pltpu.SemaphoreType.DMA((plane,)),
            pltpu.SemaphoreType.DMA((2,)),
            pltpu.SemaphoreType.DMA((2,)),
        ],
    )


def rotate_pairs(values, cosine, sine):
    parts = [
        rotate_lanes(values[:, at : at + PAIR], cosine, sine)
        for at in range(0, values.shape[1], PAIR)
    ]
    return jnp.concatenate(parts, 1)


def plane_peers():
    ctx = lax.axis_size("ctx")
    size = lax.axis_size("shard") * ctx
    mine = lax.axis_index("shard") * ctx + lax.axis_index("ctx")

    def peer(distance):
        index = lax.rem(mine + distance, size)
        return index, {"shard": index // ctx, "ctx": lax.rem(index, ctx)}

    return size, mine, peer


def greet_plane(size, peer):
    barrier = pltpu.get_barrier_semaphore()
    for distance in range(1, size):
        pl.semaphore_signal(barrier, inc=1, device_id=peer(distance)[1], device_id_type=MESH)


def front_kernel(
    live_ref, tokens_ref, weight_ref, own_gain_ref, cos_ref, sin_ref,
    h_ref, q_ref, k_ref, v_ref, kp_ref, vp_ref, o_ref, l_ref, gain_ref,
    send, recv, gain_send, gain_recv,
):
    late = lax.axis_index("ctx")
    rows, width = q_ref.shape
    block = min(BLOCK, rows)
    blocks = rows // block
    pairs = width // PAIR
    size, index, peer = plane_peers()
    part = own_gain_ref.shape[1]
    greet_plane(size, peer)
    pl.semaphore_wait(pltpu.get_barrier_semaphore(), size - 1)
    mine = pl.ds(pl.multiple_of(index * part, part), part)
    gain_ref[:, mine] = own_gain_ref[...]

    def gain_copy(distance):
        return pltpu.make_async_remote_copy(
            src_ref=own_gain_ref, dst_ref=gain_ref.at[:, mine],
            send_sem=gain_send.at[distance], recv_sem=gain_recv.at[distance],
            device_id=peer(distance)[1], device_id_type=MESH,
        )

    for distance in range(1, size):
        gain_copy(distance).start()
    for distance in range(1, size):
        gain_copy(distance).wait()

    def here(at):
        return pl.ds(pl.multiple_of(at * block, block), block)

    def lanes(pair):
        return pl.ds(pl.multiple_of(pair * PAIR, PAIR), PAIR)

    @pl.loop(0, blocks)
    def _(at):
        stream = tokens_ref[here(at)].astype(jnp.float32)
        normed = (stream * unit_scale(stream) * gain_ref[0:1]).astype(jnp.bfloat16)
        h_ref[here(at)] = normed
        keys = dot(normed, weight_ref[1], (1, 0))
        k_ref[here(at)] = rotate_pairs(keys, cos_ref[here(at)], sin_ref[here(at)]).astype(jnp.bfloat16)
        v_ref[here(at)] = dot(normed, weight_ref[2], (1, 0)).astype(jnp.bfloat16)

    def exchange(pair):
        return [
            pltpu.make_async_remote_copy(
                src_ref=own.at[:, lanes(pair)], dst_ref=prev.at[:, lanes(pair)],
                send_sem=send.at[which, pair], recv_sem=recv.at[which, pair],
                device_id={"ctx": 1 - late}, device_id_type=MESH,
            )
            for which, own, prev in ((0, k_ref, kp_ref), (1, v_ref, vp_ref))
        ]

    @pl.when(late == 0)
    def _():
        @pl.loop(0, pairs)
        def _(pair):
            for copy in exchange(pair):
                copy.start()

    @pl.loop(0, blocks)
    def _(at):
        query = dot(h_ref[here(at)], weight_ref[0], (1, 0))
        query = rotate_pairs(query, cos_ref[here(at)], sin_ref[here(at)]) * 0.125
        q_ref[here(at)] = query.astype(jnp.bfloat16)

    def attend(pair, own, with_prev):
        column = lanes(pair)
        mine = slice(own * block, (own + 1) * block)
        query = q_ref[mine, column]
        mixed = []
        for head in range(2):
            queries = one_head(query, head)
            parts = []
            if with_prev:
                parts.append((dot(kp_ref[:, column], queries, (1, 1)), vp_ref[:, column]))
            if own:
                before = slice(0, own * block)
                parts.append((dot(k_ref[before, column], queries, (1, 1)), v_ref[before, column]))
            parts.append((causal(dot(k_ref[mine, column], queries, (1, 1))), v_ref[mine, column]))
            peak = parts[0][0].max(0, keepdims=True)
            for scores, _ in parts[1:]:
                peak = jnp.maximum(peak, scores.max(0, keepdims=True))
            expo = [jnp.exp(scores - peak) for scores, _ in parts]
            denom = expo[0].sum(0, keepdims=True)
            for e in expo[1:]:
                denom = denom + e.sum(0, keepdims=True)
            inverse = 1.0 / denom
            total = None
            for e, (_, value) in zip(expo, parts):
                term = dot(value, (e * inverse).astype(jnp.bfloat16), (0, 0))
                total = term if total is None else total + term
            mixed.append(total[head * HEAD : (head + 1) * HEAD])
            index = late * rows + own * block + lax.broadcasted_iota(jnp.int32, peak.shape, 1)
            l_ref[pair, head : head + 1, mine] = jnp.where(
                index < live_ref[0], peak + jnp.log(denom), -MASKED
            )
        result = jnp.concatenate(mixed, 0).T
        index = late * rows + own * block + lax.broadcasted_iota(jnp.int32, result.shape, 0)
        own_value = v_ref[mine, column].astype(jnp.float32)
        o_ref[mine, column] = jnp.where(index < live_ref[0], result, own_value).astype(jnp.bfloat16)

    @pl.loop(0, pairs)
    def _(pair):
        @pl.when(late == 0)
        def _():
            for own in range(blocks):
                attend(pair, own, False)

        @pl.when(late == 1)
        def _():
            for copy in exchange(pair):
                copy.wait_recv()
            for own in range(blocks):
                attend(pair, own, True)

    @pl.when(late == 0)
    def _():
        @pl.loop(0, pairs)
        def _(pair):
            for copy in exchange(pair):
                copy.wait_send()


def layer_front(live, tokens, weight, gain, cosine, sine):
    rows, depth = tokens.shape
    width = weight.shape[2]
    pairs = width // PAIR
    part = jax.ShapeDtypeStruct((rows, width), jnp.bfloat16)
    outs = (
        jax.ShapeDtypeStruct((rows, depth), jnp.bfloat16), part, part, part, part, part, part,
        jax.ShapeDtypeStruct((pairs, 2, rows), jnp.float32),
        jax.ShapeDtypeStruct((8, depth), jnp.float32),
    )
    size = lax.axis_size("shard") * lax.axis_size("ctx")
    return pl.pallas_call(
        front_kernel,
        out_shape=outs,
        in_specs=[SMEM_SPEC] + [VMEM_SPEC] * 5,
        out_specs=(VMEM_SPEC,) * len(outs),
        scratch_shapes=[pltpu.SemaphoreType.DMA((2, pairs))] * 2
        + [pltpu.SemaphoreType.DMA((size,))] * 2,
        compiler_params=pltpu.CompilerParams(
            collective_id=4, has_side_effects=True, vmem_limit_bytes=56 * 2**20
        ),
        cost_estimate=pl.CostEstimate(
            flops=80 * 10**9, bytes_accessed=40 * 2**20, transcendentals=0
        ),
        name="layer_front",
    )(live, tokens, weight, gain, cosine, sine)


def attend_back_kernel(
    count, live_ref, q_hbm, k_hbm, v_hbm, kp_hbm, vp_hbm, o_hbm, l_ref, cos_ref, sin_ref,
    part_ref, middle_hbm, grad_ref, both_hbm, dq_ref, dk_ref, dv_ref, out_ref,
    q_ref, k_ref, v_ref, kp_ref, vp_ref, o_ref, do_ref, weight_ref, middle_ref, early_sem, late_sem,
    dq_acc, dk_acc, dv_acc, dkp_acc, dvp_acc, leave, arrive, slots, send, recv, chain_send, chain_recv,
):
    late = lax.axis_index("ctx")
    me = lax.axis_index("tp")
    rows, width = q_ref.shape
    block = min(BLOCK, rows)
    blocks = rows // block
    pairs = width // PAIR
    load_early, wait_early = loads_of(
        [(both_hbm.at[pl.ds(0, width)], weight_ref), (middle_hbm, middle_ref)], early_sem
    )
    load_late, wait_late = loads_of(
        [
            (o_hbm, o_ref), (q_hbm, q_ref), (kp_hbm, kp_ref), (vp_hbm, vp_ref), (k_hbm, k_ref),
            (v_hbm, v_ref),
        ],
        late_sem,
    )
    load_early()
    load_late()
    barrier = pltpu.get_barrier_semaphore()
    pl.semaphore_signal(barrier, inc=1, device_id={"ctx": 1 - late}, device_id_type=MESH)
    greet(me, count, 1)
    tick, drain, ticks = chain_parts(
        count, part_ref, out_ref, slots, chain_send, chain_recv,
        lambda rows, part, total, at: (middle_ref[part] + total).astype(jnp.bfloat16), BACK_CHUNK, BACK_LAG,
    )

    def here(at):
        return pl.ds(pl.multiple_of(at * block, block), block)

    def lanes(pair):
        return pl.ds(pl.multiple_of(pair * PAIR, PAIR), PAIR)

    def prepare(pair, step):
        column = lanes(pair)
        query = q_ref[here(step), column]
        upstream = do_ref[here(step), column]
        product = (upstream.astype(jnp.float32) * o_ref[here(step), column].astype(jnp.float32)).T
        queries = [one_head(query, head) for head in range(2)]
        upstreams = [one_head(upstream, head) for head in range(2)]
        inner = [
            product[head * HEAD : (head + 1) * HEAD].sum(0, keepdims=True) for head in range(2)
        ]
        totals = [l_ref[pair, head : head + 1, here(step)] for head in range(2)]
        query_both = jnp.concatenate(queries, 0)
        upstream_both = jnp.concatenate(upstreams, 0)

        def tile(keys, values, masked):
            grads, probs_all, out = [], [], []
            for head in range(2):
                scores = dot(keys, queries[head], (1, 1))
                if masked:
                    scores = causal(scores)
                probs = jnp.exp(scores - totals[head])
                prob_grad = dot(values, upstreams[head], (1, 1))
                score_grad = (probs * (prob_grad - inner[head])).astype(jnp.bfloat16)
                probs_all.append(probs.astype(jnp.bfloat16))
                grads.append(score_grad)
                out.append(dot(keys, score_grad, (0, 0))[head * HEAD : (head + 1) * HEAD])
            key_grad = dot(jnp.concatenate(grads, 1), query_both, (1, 0))
            value_grad = dot(jnp.concatenate(probs_all, 1), upstream_both, (1, 0))
            return jnp.concatenate(out, 0), key_grad, value_grad

        return tile, upstream

    def exchange(pair):
        return pltpu.make_async_remote_copy(
            src_ref=leave.at[pair], dst_ref=arrive.at[pair], send_sem=send.at[pair],
            recv_sem=recv.at[pair], device_id={"ctx": 1 - late}, device_id_type=MESH,
        )

    def prev_step(pair, step):
        column = lanes(pair)
        tile, _ = prepare(pair, step)

        @pl.when(step == 0)
        def _():
            dkp_acc[...] = jnp.zeros_like(dkp_acc)
            dvp_acc[...] = jnp.zeros_like(dvp_acc)

        query_grad = None
        for at in range(blocks):
            mine = slice(at * block, (at + 1) * block)
            more, key_grad, value_grad = tile(kp_ref[mine, column], vp_ref[mine, column], False)
            query_grad = more if query_grad is None else query_grad + more
            dkp_acc[mine] += key_grad
            dvp_acc[mine] += value_grad
        dq_acc[pair, :, here(step)] = query_grad

        @pl.when(step == blocks - 1)
        def _():
            leave[pair, 0] = dkp_acc[...].astype(jnp.bfloat16)
            leave[pair, 1] = dvp_acc[...].astype(jnp.bfloat16)
            exchange(pair).start()

    def own_step(pair, step):
        column = lanes(pair)
        tile, upstream = prepare(pair, step)
        query_grad, key_grad, value_grad = tile(k_ref[here(step), column], v_ref[here(step), column], True)
        index = late * rows + step * block + lax.broadcasted_iota(jnp.int32, upstream.shape, 0)
        dk_acc[here(step), column] = key_grad
        dv_acc[here(step), column] = value_grad + jnp.where(
            index < live_ref[0], 0.0, upstream.astype(jnp.float32)
        )
        dq_acc[pair, :, here(step)] += query_grad

        @pl.loop(0, step)
        def _(at):
            more, key_grad, value_grad = tile(k_ref[here(at), column], v_ref[here(at), column], False)
            dk_acc[here(at), column] += key_grad
            dv_acc[here(at), column] += value_grad
            dq_acc[pair, :, here(step)] += more

        grad = dq_acc[pair, :, here(step)].T * 0.125
        grad = rotate_lanes(grad, cos_ref[here(step)], -sin_ref[here(step)])
        dq_ref[here(step), column] = grad.astype(jnp.bfloat16)

    @pl.when(late == 0)
    def _():
        dq_acc[...] = jnp.zeros_like(dq_acc)

    wait_early()

    @pl.loop(0, blocks)
    def _(at):
        for more in range(LEAD):
            tick(at * LEAD + more)
        do_ref[here(at)] = dot(grad_ref[here(at)], weight_ref[...], (1, 1)).astype(jnp.bfloat16)

    wait_late()
    steps = pairs * blocks
    lead = blocks * LEAD

    @pl.loop(0, 2 * steps)
    def _(at):
        @pl.when(lead + at < ticks)
        def _():
            tick(lead + at)

        @pl.when((late == 1) & (at < steps))
        def _():
            prev_step(at // blocks, at % blocks)

        @pl.when(at >= steps)
        def _():
            own_step((at - steps) // blocks, at % blocks)

    if ticks > lead + 2 * steps:
        pl.loop(lead + 2 * steps, ticks)(tick)

    @pl.loop(0, pairs)
    def _(pair):
        column = lanes(pair)

        @pl.when(late == 0)
        def _():
            exchange(pair).wait_recv()
            dk_acc[:, column] += arrive[pair, 0].astype(jnp.float32)
            dv_acc[:, column] += arrive[pair, 1].astype(jnp.float32)

        @pl.when(late == 1)
        def _():
            exchange(pair).wait_send()

        dk_ref[:, column] = rotate_lanes(dk_acc[:, column], cos_ref[...], -sin_ref[...]).astype(
            jnp.bfloat16
        )
        dv_ref[:, column] = dv_acc[:, column].astype(jnp.bfloat16)

    drain()


def attend_back(live, arrays, cosine, sine, out_part, middle, grad, both, count):
    rows, width = arrays[0].shape
    pairs = width // PAIR
    part = jax.ShapeDtypeStruct((rows, width), jnp.bfloat16)
    outs = (
        part, part, part, jax.ShapeDtypeStruct(out_part.shape, jnp.bfloat16),
    )
    chunks = rows // 2 // BACK_CHUNK
    return pl.pallas_call(
        functools.partial(attend_back_kernel, count),
        out_shape=outs,
        in_specs=[SMEM_SPEC] + [HBM_SPEC] * 6 + [VMEM_SPEC] * 4 + [HBM_SPEC, VMEM_SPEC, HBM_SPEC],
        out_specs=(VMEM_SPEC,) * len(outs),
        scratch_shapes=[
            *[pltpu.VMEM((rows, width), jnp.bfloat16)] * 7,
            pltpu.VMEM((width, middle.shape[1]), jnp.bfloat16),
            pltpu.VMEM(middle.shape, jnp.float32),
            pltpu.SemaphoreType.DMA((2,)),
            pltpu.SemaphoreType.DMA((6,)),
            pltpu.VMEM((pairs, PAIR, rows), jnp.float32),
            pltpu.VMEM((rows, width), jnp.float32),
            pltpu.VMEM((rows, width), jnp.float32),
            pltpu.VMEM((rows, PAIR), jnp.float32),
            pltpu.VMEM((rows, PAIR), jnp.float32),
            pltpu.VMEM((pairs, 2, rows, PAIR), jnp.bfloat16),
            pltpu.VMEM((pairs, 2, rows, PAIR), jnp.bfloat16),
            pltpu.VMEM((2, rows // 2, out_part.shape[1]), jnp.bfloat16),
            pltpu.SemaphoreType.DMA((pairs,)),
            pltpu.SemaphoreType.DMA((pairs,)),
            pltpu.SemaphoreType.DMA((4, chunks)),
            pltpu.SemaphoreType.DMA((4, chunks)),
        ],
        compiler_params=pltpu.CompilerParams(
            collective_id=5, has_side_effects=True, vmem_limit_bytes=58 * 2**20
        ),
        cost_estimate=pl.CostEstimate(
            flops=100 * 10**9, bytes_accessed=40 * 2**20, transcendentals=0
        ),
        name="attend_back",
    )(live, *arrays, cosine, sine, out_part, middle, grad, both)


def narrow_kernel(
    out_ref, down_ref, gate_up_ref, cos_in, sin_in, both_ref, low_ref, cos_ref, sin_ref
):
    cos_ref[...] = cos_in[...]
    sin_ref[...] = sin_in[...]
    split = out_ref.shape[0]
    both_ref[:split] = out_ref[...].astype(jnp.bfloat16)
    both_ref[split:] = down_ref[...].astype(jnp.bfloat16)
    low_ref[...] = gate_up_ref[...].astype(jnp.bfloat16)


def narrow(out_weight, down_weight, gate_up_weight, cosine, sine):
    return pl.pallas_call(
        narrow_kernel,
        out_shape=(
            jax.ShapeDtypeStruct(
                (out_weight.shape[0] + down_weight.shape[0], out_weight.shape[1]), jnp.bfloat16
            ),
            jax.ShapeDtypeStruct(gate_up_weight.shape, jnp.bfloat16),
            jax.ShapeDtypeStruct(cosine.shape, jnp.float32),
            jax.ShapeDtypeStruct(sine.shape, jnp.float32),
        ),
        in_specs=[VMEM_SPEC] * 5,
        out_specs=(VMEM_SPEC,) * 4,
        compiler_params=pltpu.CompilerParams(vmem_limit_bytes=40 * 2**20),
        cost_estimate=pl.CostEstimate(flops=40 * 10**9, bytes_accessed=2**24, transcendentals=0),
        name="narrow",
    )(out_weight, down_weight, gate_up_weight, cosine, sine)


def mlp_kernel(
    normed_ref, weight_ref, hidden_grad_ref, cotangent_ref,
    hidden_ref, down_grad_ref, gate_up_grad_ref, back_ref, turned, total,
):
    step = pl.program_id(0)

    @pl.when(step == 0)
    def _():
        turned[...] = normed_ref[...].T
        total[...] = jnp.zeros_like(total)

    gate = dot(normed_ref[...], weight_ref[0], (1, 0))
    upward = dot(normed_ref[...], weight_ref[1], (1, 0))
    hidden_grad = hidden_grad_ref[...]
    sigma = jax.nn.sigmoid(gate)
    swish = gate * sigma
    hidden = (swish * upward).astype(jnp.bfloat16)
    hidden_ref[...] = hidden
    gate_grad = (hidden_grad * upward * sigma * (1.0 + gate * (1.0 - sigma))).astype(jnp.bfloat16)
    upward_grad = (hidden_grad * swish).astype(jnp.bfloat16)
    both = jnp.concatenate([gate_grad, upward_grad], 1)
    weights = jnp.concatenate([weight_ref[0], weight_ref[1]], 1)
    total[...] += dot(both, weights, (1, 1))
    gate_up_grad_ref[0] = dot(turned[...], gate_grad, (1, 0)).astype(jnp.bfloat16)
    gate_up_grad_ref[1] = dot(turned[...], upward_grad, (1, 0)).astype(jnp.bfloat16)
    down_grad_ref[...] = dot(hidden.T, cotangent_ref[...], (1, 0)).astype(jnp.bfloat16)

    @pl.when(step == pl.num_programs(0) - 1)
    def _():
        back_ref[...] = total[...].astype(jnp.bfloat16)


def mlp(normed, weight, hidden_grad, cotangent):
    rows, depth = normed.shape
    width = weight.shape[2]
    whole = pl.BlockSpec((rows, depth), lambda j: (0, 0), pipeline_mode=pl.Buffered(1))
    return pl.pallas_call(
        mlp_kernel,
        out_shape=(
            jax.ShapeDtypeStruct((rows, width), jnp.bfloat16),
            jax.ShapeDtypeStruct((width, depth), jnp.bfloat16),
            jax.ShapeDtypeStruct((2, depth, width), jnp.bfloat16),
            jax.ShapeDtypeStruct((rows, depth), jnp.bfloat16),
        ),
        grid=(width // MLP_WIDE,),
        in_specs=[
            whole,
            pl.BlockSpec((2, depth, MLP_WIDE), lambda j: (0, 0, j)),
            pl.BlockSpec((rows, MLP_WIDE), lambda j: (0, j)),
            whole,
        ],
        out_specs=(
            pl.BlockSpec((rows, MLP_WIDE), lambda j: (0, j)),
            pl.BlockSpec((MLP_WIDE, depth), lambda j: (j, 0)),
            pl.BlockSpec((2, depth, MLP_WIDE), lambda j: (0, 0, j)),
            pl.BlockSpec((rows, depth), lambda j: (0, 0)),
        ),
        scratch_shapes=[
            pltpu.VMEM((depth, rows), jnp.bfloat16), pltpu.VMEM((rows, depth), jnp.float32),
        ],
        compiler_params=pltpu.CompilerParams(vmem_limit_bytes=60 * 2**20),
        cost_estimate=pl.CostEstimate(
            flops=14 * rows * depth * width, bytes_accessed=80 * 2**20, transcendentals=rows * width
        ),
        name="mlp",
    )(normed, weight, hidden_grad, cotangent)


def projection_back_kernel(
    normed_ref, weight_ref, dq_ref, dk_ref, dv_ref, mixed_ref, middle_ref, grad_ref, back_ref,
    turned, total,
):
    step = pl.program_id(0)

    @pl.when(step == 0)
    def _():
        turned[...] = normed_ref[...].T

    for at, ref in enumerate((dq_ref, dk_ref, dv_ref)):

        @pl.when(step == at)
        def _():
            term = dot(ref[...], weight_ref[0], (1, 1))
            if at == 0:
                total[...] = term
            elif at == 1:
                total[...] += term
            else:
                back_ref[...] = (total[...] + term).astype(jnp.bfloat16)
            grad_ref[0] = dot(turned[...], ref[...], (1, 0)).astype(jnp.bfloat16)

    @pl.when(step == 3)
    def _():
        turned[...] = middle_ref[...].T
        grad_ref[0] = dot(turned[...], mixed_ref[...], (1, 0)).astype(jnp.bfloat16)


def projection_back(normed, weight, dq, dk, dv, mixed, middle):
    rows, depth = normed.shape
    width = dq.shape[1]
    whole = lambda w: pl.BlockSpec((rows, w), lambda j: (0, 0), pipeline_mode=pl.Buffered(1))
    return pl.pallas_call(
        projection_back_kernel,
        out_shape=(
            jax.ShapeDtypeStruct((4, depth, width), jnp.bfloat16),
            jax.ShapeDtypeStruct((rows, depth), jnp.bfloat16),
        ),
        grid=(4,),
        in_specs=[
            whole(depth),
            pl.BlockSpec((1, depth, width), lambda j: (jnp.minimum(j, 2), 0, 0)),
            whole(width), whole(width), whole(width), whole(width), whole(depth),
        ],
        out_specs=(
            pl.BlockSpec((1, depth, width), lambda j: (j, 0, 0)),
            pl.BlockSpec((rows, depth), lambda j: (0, 0)),
        ),
        scratch_shapes=[
            pltpu.VMEM((depth, rows), jnp.bfloat16), pltpu.VMEM((rows, depth), jnp.float32),
        ],
        compiler_params=pltpu.CompilerParams(vmem_limit_bytes=60 * 2**20),
        cost_estimate=pl.CostEstimate(
            flops=14 * rows * depth * width, bytes_accessed=40 * 2**20, transcendentals=0
        ),
        name="projection_back",
    )(normed, weight, dq, dk, dv, mixed, middle)


def tail_kernel(
    grad_ref, out_grad_ref, w_ref, m_ref, s_ref, ow_ref, om_ref, os_ref,
    g_out, w_out, m_out, s_out, og_out, step_out, om_out, os_out,
):
    grad = grad_ref[0:3].astype(jnp.float32)
    update, first, second = adam_update(w_ref[...], m_ref[...], s_ref[...], grad, decay_rate)
    g_out[...] = grad
    w_out[...] = w_ref[...] - update
    m_out[...] = first
    s_out[...] = second
    grad = out_grad_ref[0].astype(jnp.float32).T
    update, first, second = adam_update(ow_ref[...], om_ref[...], os_ref[...], grad, decay_rate)
    og_out[...] = grad
    step_out[...] = update
    om_out[...] = first
    os_out[...] = second


def adam_tail(grads, qkv, out):
    planes, rows, width = qkv[0].shape
    steps = width // PAIR
    mine = pl.BlockSpec((planes, rows // steps, width), lambda i: (0, i, 0))
    other = pl.BlockSpec((PAIR, rows), lambda i: (i, 0))
    shapes = [jax.ShapeDtypeStruct(qkv[0].shape, jnp.float32)] * 4
    shapes += [jax.ShapeDtypeStruct(out[0].shape, jnp.float32)] * 4
    results = pl.pallas_call(
        tail_kernel,
        out_shape=tuple(shapes),
        grid=(steps,),
        in_specs=[
            pl.BlockSpec((planes + 1, rows // steps, width), lambda i: (0, i, 0)),
            pl.BlockSpec((1, rows, PAIR), lambda i: (planes, 0, i)),
            mine, mine, mine, other, other, other,
        ],
        out_specs=(mine,) * 4 + (other,) * 4,
        compiler_params=pltpu.CompilerParams(vmem_limit_bytes=60 * 2**20),
        cost_estimate=pl.CostEstimate(
            flops=10**7, bytes_accessed=16 * 2**20, transcendentals=0
        ),
        name="adam_tail",
    )(grads, grads, *qkv, *out)
    return results[:4], results[4:]


def scatter_low(grad, axis=1):
    return lax.psum_scatter(
        grad.astype(jnp.bfloat16), ("shard", "ctx"), scatter_dimension=axis, tiled=True
    ).astype(jnp.float32)


def after(array, *others):
    return lax.optimization_barrier((array, *others))[0]


def adam_update(weight, first, second, grad, decay):
    first_new = beta_one * first + (1.0 - beta_one) * grad
    second_new = beta_two * second + (1.0 - beta_two) * grad * grad
    first_hat = first_new / (1.0 - beta_one**step_count)
    second_hat = second_new / (1.0 - beta_two**step_count)
    update = learn_rate * (first_hat / (jnp.sqrt(second_hat) + adam_eps) + decay * weight)
    return (update, first_new, second_new)


def body(
    tokens,
    cotangent,
    lengths,
    qkv_weight,
    out_weight,
    gate_up_weight,
    down_weight,
    norm_gains,
    qkv_first,
    out_first,
    gate_up_first,
    down_first,
    gains_first,
    qkv_second,
    out_second,
    gate_up_second,
    down_second,
    gains_second,
):
    row_count = tokens.shape[0]
    count = lax.axis_size("tp")
    offset = lax.axis_index("ctx") * row_count
    query_index = offset + jnp.arange(row_count, dtype=jnp.int32)
    qkv_low = qkv_weight.astype(jnp.bfloat16)
    cosine, sine = rotation(query_index, HEAD)
    cosine, sine = (jnp.concatenate([c[:, 0]] * 4, 1) for c in (cosine, sine))
    both_low, gate_up_low, cosine, sine = narrow(
        out_weight, down_weight, gate_up_weight, cosine, sine
    )
    gains_low = norm_gains.astype(jnp.bfloat16).astype(jnp.float32)
    gains_low = jnp.concatenate([gains_low] * 4, 0)
    gather = lambda a: lax.all_gather(a, ("shard", "ctx"), axis=1, tiled=True)
    qkv_full = gather(qkv_low)
    both_full = gather(after(both_low, qkv_full))
    normed_one, query, keys, values, keys_prev, values_prev, mixed_low, totals, gains_full = layer_front(
        lengths, tokens, qkv_full, gains_low, cosine, sine
    )
    gate_up_full = gather(after(gate_up_low, both_full, totals))
    normed_two, middle, hidden_grad = sum_middle(
        mixed_low, both_full, tokens, gains_full, cotangent, count
    )
    hidden, down_grad_local, gate_up_grad_local, mlp_back_part = mlp(
        normed_two, gate_up_full, hidden_grad, cotangent
    )
    down_grad = scatter_low(down_grad_local)
    middle_low, middle_grad, gain_two_grad, out_part = sum_middle_back(
        mlp_back_part, middle, cotangent, gains_full, hidden, both_full, count
    )
    gate_up_grad = scatter_low(after(gate_up_grad_local, down_grad, middle_low))
    query_low, key_low, value_low, out_tokens = attend_back(
        lengths,
        [query, keys, values, keys_prev, values_prev, mixed_low, totals],
        cosine, sine, out_part, middle, middle_low, both_full, count,
    )
    qkv_grad_local, attn_back_part = projection_back(
        normed_one, qkv_full, query_low, key_low, value_low, mixed_low, middle_low
    )
    attn_back_part, qkv_grad_local, _ = lax.optimization_barrier(
        (attn_back_part, qkv_grad_local, gate_up_grad)
    )
    tail_grads = lax.psum_scatter(
        qkv_grad_local, ("shard", "ctx"), scatter_dimension=1, tiled=True
    )
    input_grad, gains_grad = sum_input_back(
        attn_back_part, tokens, middle_grad, gains_full, gain_two_grad, norm_gains.shape[1], count
    )
    tail_grads, _ = lax.optimization_barrier((tail_grads, gains_grad))
    (qkv_grad, qkv_new, qkv_first_new, qkv_second_new), (
        out_grad, out_step, out_first_new, out_second_new,
    ) = adam_tail(
        tail_grads,
        (qkv_weight, qkv_first, qkv_second),
        (out_weight, out_first, out_second),
    )
    gate_up_step, gate_up_first_new, gate_up_second_new = adam_update(
        gate_up_weight, gate_up_first, gate_up_second, gate_up_grad, decay_rate
    )
    down_step, down_first_new, down_second_new = adam_update(
        down_weight, down_first, down_second, down_grad, decay_rate
    )
    gains_step, gains_first_new, gains_second_new = adam_update(
        norm_gains, gains_first, gains_second, gains_grad, 0.0
    )
    gate_up_new = gate_up_weight - gate_up_step
    down_new = down_weight - down_step
    return (
        out_tokens,
        input_grad,
        qkv_grad,
        out_grad,
        gate_up_grad,
        down_grad,
        gains_grad,
        qkv_new,
        out_step,
        gate_up_new,
        down_new,
        gains_step,
        qkv_first_new,
        out_first_new,
        gate_up_first_new,
        down_first_new,
        gains_first_new,
        qkv_second_new,
        out_second_new,
        gate_up_second_new,
        down_second_new,
        gains_second_new,
    )


def solution(mesh):
    return jax.shard_map(
        body,
        mesh=mesh,
        in_specs=(
            P(("shard", "ctx"), None),
            P(("shard", "ctx"), None),
            P("shard"),
            P(None, ("shard", "ctx"), "tp"),
            P("tp", ("shard", "ctx")),
            P(None, ("shard", "ctx"), "tp"),
            P("tp", ("shard", "ctx")),
            P(None, ("shard", "ctx")),
            P(None, ("shard", "ctx"), "tp"),
            P("tp", ("shard", "ctx")),
            P(None, ("shard", "ctx"), "tp"),
            P("tp", ("shard", "ctx")),
            P(None, ("shard", "ctx")),
            P(None, ("shard", "ctx"), "tp"),
            P("tp", ("shard", "ctx")),
            P(None, ("shard", "ctx"), "tp"),
            P("tp", ("shard", "ctx")),
            P(None, ("shard", "ctx")),
        ),
        out_specs=(
            P(("shard", "ctx"), None),
            P(("shard", "ctx"), None),
            P(None, ("shard", "ctx"), "tp"),
            P("tp", ("shard", "ctx")),
            P(None, ("shard", "ctx"), "tp"),
            P("tp", ("shard", "ctx")),
            P(None, ("shard", "ctx")),
            P(None, ("shard", "ctx"), "tp"),
            P("tp", ("shard", "ctx")),
            P(None, ("shard", "ctx"), "tp"),
            P("tp", ("shard", "ctx")),
            P(None, ("shard", "ctx")),
            P(None, ("shard", "ctx"), "tp"),
            P("tp", ("shard", "ctx")),
            P(None, ("shard", "ctx"), "tp"),
            P("tp", ("shard", "ctx")),
            P(None, ("shard", "ctx")),
            P(None, ("shard", "ctx"), "tp"),
            P("tp", ("shard", "ctx")),
            P(None, ("shard", "ctx"), "tp"),
            P("tp", ("shard", "ctx")),
            P(None, ("shard", "ctx")),
        ),
        check_vma=False,
    )
```

```python
import functools
import jax
import jax.numpy as jnp
from jax import lax
from jax.experimental import pallas as pl
from jax.experimental.pallas import tpu as pltpu
from jax.sharding import PartitionSpec as P

HEAD = 64
PAIR = 128
BLOCK = 256
CHUNK = 16
LAG = 2
BACK_CHUNK = 32
BACK_LAG = 3
WIDE = 256
SPACING = 5
LEAD = 1
MLP_WIDE = 256
MASKED = -1e30
MESH = pl.DeviceIdType.MESH
VMEM_SPEC = pl.BlockSpec(memory_space=pltpu.VMEM)
SMEM_SPEC = pl.BlockSpec(memory_space=pltpu.SMEM)
HBM_SPEC = pl.BlockSpec(memory_space=pl.ANY)


norm_eps = 1e-05
rope_base = 130000.0
beta_one = 0.9
beta_two = 0.95
learn_rate = 0.02
decay_rate = 0.1
adam_eps = 1e-08
step_count = 4.0


def rotation(position, head_size):
    half = head_size // 2
    freqs = rope_base ** (-(jnp.arange(half, dtype=jnp.float32) * 2.0) / head_size)
    angle = position.astype(jnp.float32)[:, None] * freqs[None, :]
    return (jnp.cos(angle)[:, None, :], jnp.sin(angle)[:, None, :])


def dot(left, right, contract):
    return lax.dot_general(
        left, right, ((contract[:1], contract[1:]), ((), ())), preferred_element_type=jnp.float32
    )


def one_head(values, head):
    lane = lax.broadcasted_iota(jnp.int32, values.shape, 1)
    return jnp.where((lane < HEAD) == (head == 0), values, jnp.zeros_like(values))


def causal(scores):
    key = lax.broadcasted_iota(jnp.int32, scores.shape, 0)
    query = lax.broadcasted_iota(jnp.int32, scores.shape, 1)
    return jnp.where(key <= query, scores, MASKED)


def rotate_lanes(values, cosine, sine):
    lane = lax.broadcasted_iota(jnp.int32, values.shape, 1) % HEAD
    width = values.shape[1]
    ahead = pltpu.roll(values, width - HEAD // 2, 1)
    behind = pltpu.roll(values, HEAD // 2, 1)
    return values * cosine + jnp.where(lane < HEAD // 2, -ahead, behind) * sine


def greet(me, count, more=0, more_ends=0):
    barrier = pltpu.get_barrier_semaphore()

    @pl.when(me > 0)
    def _():
        pl.semaphore_signal(barrier, inc=1, device_id={"tp": me - 1}, device_id_type=MESH)

    @pl.when(me < count - 1)
    def _():
        pl.semaphore_signal(barrier, inc=1, device_id={"tp": me + 1}, device_id_type=MESH)

    @pl.when((me > 0) & (me < count - 1))
    def _():
        pl.semaphore_wait(barrier, 2 + more)

    @pl.when((me == 0) | (me == count - 1))
    def _():
        pl.semaphore_wait(barrier, 1 + more + more_ends)


def chain_parts(count, part_ref, out_ref, slots, send, recv, finish, size, lag=1, land=None, stored=None):
    me = lax.axis_index("tp")
    apart = land is not None
    land = land if apart else out_ref
    half = out_ref.shape[0] // 2
    chunks = half // size

    def copy(stream, at, source, target, device):
        return pltpu.make_async_remote_copy(
            src_ref=source, dst_ref=target, send_sem=send.at[stream, at],
            recv_sem=recv.at[stream, at], device_id={"tp": device}, device_id_type=MESH,
        )

    def ends(way):
        place = me if way == 1 else count - 1 - me
        return place, me + way

    def reduce_copy(way, at, device):
        index = 0 if way == 1 else 1
        rows = pl.ds(pl.multiple_of(at * size, size), size)
        return copy(index, at, slots.at[index, rows], slots.at[index, rows], device)

    def spread_copy(way, at, device):
        base = 0 if way == 1 else half
        rows = pl.ds(pl.multiple_of(base + at * size, size), size)
        return copy(2 if way == 1 else 3, at, land.at[rows], land.at[rows], device)

    def store_copy(index, at):
        rows = pl.ds(pl.multiple_of(index * half + at * size, size), size)
        return pltpu.make_async_copy(land.at[rows], out_ref.at[rows], stored.at[index, at])

    def reduce_step(way, tick):
        place, ahead = ends(way)
        index = 0 if way == 1 else 1
        base = half if way == 1 else 0
        at = tick - lag * place

        @pl.when((at >= 0) & (at < chunks))
        def _():
            local = pl.ds(pl.multiple_of(at * size, size), size)
            rows = pl.ds(pl.multiple_of(base + at * size, size), size)

            @pl.when(place == 0)
            def _():
                slots[index, local] = part_ref[rows]

            @pl.when(place > 0)
            def _():
                reduce_copy(way, at, ahead).wait_recv()

            @pl.when((place > 0) & (place < count - 1))
            def _():
                slots[index, local] = (
                    slots[index, local].astype(jnp.float32) + part_ref[rows].astype(jnp.float32)
                ).astype(jnp.bfloat16)

            @pl.when(place < count - 1)
            def _():
                reduce_copy(way, at, ahead).start()

            @pl.when(place == count - 1)
            def _():
                total = slots[index, local].astype(jnp.float32) + part_ref[rows].astype(jnp.float32)
                land[rows] = finish(rows, local, total, at)
                if apart:
                    store_copy(1 if way == 1 else 0, at).start()
                spread_copy(-way, at, me - way).start()

    def spread_step(way, tick):
        place, ahead = ends(way)
        at = tick - lag * (count - 1) - lag * place

        @pl.when((at >= 0) & (at < chunks) & (place > 0))
        def _():
            spread_copy(way, at, ahead).wait_recv()

            @pl.when(place < count - 1)
            def _():
                spread_copy(way, at, ahead).start()

            if apart:
                store_copy(0 if way == 1 else 1, at).start()

    def step(tick):
        for way in (1, -1):
            reduce_step(way, tick)
        for way in (1, -1):
            spread_step(way, tick)

    def drain():
        @pl.loop(0, chunks)
        def _(at):
            if apart:
                for index in range(2):
                    store_copy(index, at).wait()

            for way in (1, -1):
                place, ahead = ends(way)

                @pl.when(place < count - 1)
                def _():
                    reduce_copy(way, at, ahead).wait_send()
                    spread_copy(way, at, ahead).wait_send()

    return step, drain, chunks + 2 * lag * (count - 1)


def run_ticks(parts, start, wait, finally_drain):
    step, drain, ticks = parts
    tick = pl.program_id(0)
    pl.when(tick == 0)(start)
    pl.when(tick == SPACING - 2)(wait)
    step(tick)

    @pl.when(tick == ticks - 1)
    def _():
        drain()
        finally_drain()

    return tick


def tick_count(rows, count):
    return rows // 2 // CHUNK + 2 * LAG * (count - 1)


def unit_scale(stream):
    return lax.rsqrt(jnp.mean(stream * stream, axis=-1, keepdims=True) + norm_eps)


def fold(values):
    return values.reshape(-1, 8, values.shape[1]).sum(0)


def norm_back(stream, gain, upstream):
    scale = unit_scale(stream)
    gain_grad = fold(upstream * stream * scale)
    inner = jnp.sum(upstream * gain * stream, axis=-1, keepdims=True)
    grad = scale * gain * upstream - stream * (scale * scale * scale / stream.shape[-1]) * inner
    return grad, gain_grad


def loads_of(pairs, sems):
    copies = [
        pltpu.make_async_copy(source, target, sems.at[at])
        for at, (source, target) in enumerate(pairs)
    ]

    def start():
        for copy in copies:
            copy.start()

    def wait():
        for copy in copies:
            copy.wait()

    return start, wait


def half_store(source, target, sems, count):
    chunks = source.shape[0] // CHUNK
    me = lax.axis_index("tp")

    def copy(at):
        rows = pl.ds(pl.multiple_of(at * CHUNK, CHUNK), CHUNK)
        return pltpu.make_async_copy(source.at[rows], target.at[rows], sems.at[at])

    def drain():
        @pl.when((me == 0) | (me == count - 1))
        def _():
            @pl.loop(0, chunks)
            def _(at):
                copy(at).wait()

    return copy, drain


def middle_kernel(
    count, blocks, mixed_ref, weight_ref, tokens_hbm, gain_ref, cotangent_hbm, down_ref,
    out_ref, middle_ref, hidden_grad_ref,
    slots, land, send, recv, stored, part_ref, tokens_ref, cotangent_ref, middle, load_sem, half_sem,
):
    load, wait = loads_of([(tokens_hbm, tokens_ref), (cotangent_hbm, cotangent_ref)], load_sem)
    half_copy, half_drain = half_store(middle, middle_ref, half_sem, count)

    def start():
        load()
        greet(lax.axis_index("tp"), count)

        project(0)

    half_blocks = part_ref.shape[0] // 2 // BLOCK

    def project(at):
        for half in range(2):
            here = pl.ds(pl.multiple_of((half * half_blocks + at) * BLOCK, BLOCK), BLOCK)
            part_ref[here] = dot(mixed_ref[here], weight_ref[...], (1, 0)).astype(jnp.bfloat16)

    def finish(rows, local, total, at):
        value = tokens_ref[rows].astype(jnp.float32) + total
        middle[local] = value
        half_copy(at).start()
        return (value * unit_scale(value) * gain_ref[1:2]).astype(jnp.bfloat16)

    parts = chain_parts(
        count, part_ref, out_ref, slots, send, recv, finish, CHUNK, LAG, land, stored
    )
    tick = run_ticks(parts, start, wait, half_drain)

    @pl.when((tick >= 1) & (tick < half_blocks))
    def _():
        project(tick)

    @pl.when((tick % SPACING == SPACING - 1) & (tick < blocks * SPACING))
    def _():
        hidden_grad_ref[...] = dot(cotangent_ref[...], down_ref[...], (1, 1))


def middle_back_kernel(
    count, part_ref, middle_hbm, cotangent_hbm, gain_ref, hidden_hbm, down_ref,
    out_ref, grad_ref, gain_grad_ref, layer_ref,
    slots, land, send, recv, stored, middle_ref, cotangent_ref, hidden_ref, grad, load_sem, half_sem,
):
    load, wait = loads_of(
        [(middle_hbm, middle_ref), (cotangent_hbm, cotangent_ref), (hidden_hbm, hidden_ref)],
        load_sem,
    )
    half_copy, half_drain = half_store(grad, grad_ref, half_sem, count)

    def start():
        load()
        greet(lax.axis_index("tp"), count)
        gain_grad_ref[...] = jnp.zeros_like(gain_grad_ref)

    def finish(rows, local, total, at):
        value, gain_grad = norm_back(middle_ref[local], gain_ref[1:2], total)
        gain_grad_ref[...] += gain_grad
        value = cotangent_ref[rows].astype(jnp.float32) + value
        grad[local] = value
        half_copy(at).start()
        return value.astype(jnp.bfloat16)

    parts = chain_parts(
        count, part_ref, out_ref, slots, send, recv, finish, CHUNK, LAG, land, stored
    )
    tick = run_ticks(parts, start, wait, half_drain)

    @pl.when((tick % SPACING == SPACING - 1) & (tick < part_ref.shape[1] // WIDE * SPACING))
    def _():
        skip = down_ref.shape[0] - hidden_ref.shape[1]
        layer_ref[...] = dot(hidden_ref[...], down_ref[skip:], (1, 0)).astype(jnp.bfloat16)


def input_back_kernel(
    count, part_ref, tokens_hbm, grad_hbm, gain_ref, other_ref, out_ref, gains_ref,
    slots, land, send, recv, stored, tokens_ref, grad_ref, local, landed, along,
    load_sem, plane_send, plane_recv, line_send, line_recv,
):
    load, wait = loads_of([(tokens_hbm, tokens_ref), (grad_hbm, grad_ref)], load_sem)

    me = lax.axis_index("tp")
    size, index, peer = plane_peers()
    width = gains_ref.shape[1]
    last = (me == 0) | (me == count - 1)

    def start():
        load()

        @pl.when(last)
        def _():
            greet_plane(size, peer)

        greet(me, count, 0, size - 1)
        local[0:8] = jnp.zeros((8, local.shape[1]), jnp.float32)
        local[8:16] = other_ref[...]

    def finish(rows, part, total, at):
        grad, gain_grad = norm_back(tokens_ref[rows].astype(jnp.float32), gain_ref[0:1], total)
        local[0:8] += gain_grad
        return (grad_ref[part] + grad).astype(jnp.bfloat16)

    step, drain, ticks = chain_parts(
        count, part_ref, out_ref, slots, send, recv, finish, CHUNK, LAG, land, stored
    )

    def columns(at):
        return pl.ds(pl.multiple_of(at * width, width), width)

    def plane_copy(distance):
        at, device = peer(distance)
        return pltpu.make_async_remote_copy(
            src_ref=local.at[:, columns(at)], dst_ref=landed.at[distance],
            send_sem=plane_send.at[distance], recv_sem=plane_recv.at[distance],
            device_id=device, device_id_type=MESH,
        )

    def line_copy(way):
        which = 0 if way == 1 else 1
        return pltpu.make_async_remote_copy(
            src_ref=along.at[which], dst_ref=along.at[which],
            send_sem=line_send.at[which], recv_sem=line_recv.at[which],
            device_id={"tp": me + way}, device_id_type=MESH,
        )

    done = out_ref.shape[0] // 2 // CHUNK + LAG * (count - 1)

    tick = pl.program_id(0)
    pl.when(tick == 0)(start)
    pl.when(tick == SPACING - 2)(wait)
    step(tick)

    @pl.when(last & (tick == done - 1))
    def _():
        for distance in range(1, size):
            plane_copy(distance).start()

    @pl.when(last & (tick == done + LAG))
    def _():
        total = local[:, columns(index)]
        for distance in range(1, size):
            plane_copy(distance).wait()
            total = total + landed[distance]

        @pl.when(me == 0)
        def _():
            along[0] = total
            line_copy(1).start()

        @pl.when(me == count - 1)
        def _():
            along[1] = total
            line_copy(-1).start()

    for way in (1, -1):
        place = me if way == 1 else count - 1 - me

        @pl.when((place > 0) & (tick == jnp.minimum(done + LAG + place, ticks - 1)))
        def _():
            line_copy(way).wait_recv()

            @pl.when(place < count - 1)
            def _():
                line_copy(way).start()

    @pl.when(tick == ticks - 1)
    def _():
        for way in (1, -1):
            place = me if way == 1 else count - 1 - me

            @pl.when(place < count - 1)
            def _():
                line_copy(way).wait_send()

        sums = along[0] + along[1]
        gains_ref[0:1] = sums[0:8].sum(0, keepdims=True)
        gains_ref[1:2] = sums[8:16].sum(0, keepdims=True)
        drain()


def chain_call(kernel, name, number, count, shape, inputs, outs, scratch):
    rows, width = shape
    chunks = rows // 2 // CHUNK
    arrays, in_specs = zip(*inputs)
    out_shape, out_specs = zip(*outs)
    return pl.pallas_call(
        kernel,
        out_shape=out_shape,
        grid=(tick_count(rows, count),),
        in_specs=in_specs,
        out_specs=out_specs,
        scratch_shapes=[
            pltpu.VMEM((2, rows // 2, width), jnp.bfloat16),
            pltpu.VMEM((rows, width), jnp.bfloat16),
            pltpu.SemaphoreType.DMA((4, chunks)),
            pltpu.SemaphoreType.DMA((4, chunks)),
            pltpu.SemaphoreType.DMA((2, chunks)),
            *scratch,
        ],
        compiler_params=pltpu.CompilerParams(
            collective_id=number, has_side_effects=True, vmem_limit_bytes=60 * 2**20
        ),
        cost_estimate=pl.CostEstimate(
            flops=100 * 10**9, bytes_accessed=12 * rows * width, transcendentals=0
        ),
        name=name,
    )(*arrays)


def far(shape, dtype):
    return jax.ShapeDtypeStruct(shape, dtype), HBM_SPEC


def kept(shape, dtype):
    return jax.ShapeDtypeStruct(shape, dtype), VMEM_SPEC


def sum_middle(mixed, both, tokens, gain, cotangent, count):
    rows, width = tokens.shape
    inner = mixed.shape[1]
    hidden = both.shape[0] - inner
    last = hidden // WIDE - 1
    at = lambda i: jnp.minimum(i // SPACING, last)
    return chain_call(
        functools.partial(middle_kernel, count, last + 1), "sum_middle", 1, count, tokens.shape,
        [
            (mixed, VMEM_SPEC),
            (both, pl.BlockSpec((inner, width), lambda i: (0, 0), pipeline_mode=pl.Buffered(1))),
            (tokens, HBM_SPEC), (gain, VMEM_SPEC), (cotangent, HBM_SPEC),
            (both, pl.BlockSpec((WIDE, width), lambda i: (inner // WIDE + at(i), 0))),
        ],
        [
            far(tokens.shape, jnp.bfloat16),
            far((rows // 2, width), jnp.float32),
            (
                jax.ShapeDtypeStruct((rows, hidden), jnp.float32),
                pl.BlockSpec((rows, WIDE), lambda i: (0, at(i))),
            ),
        ],
        [
            *[pltpu.VMEM(tokens.shape, jnp.bfloat16)] * 3,
            pltpu.VMEM((rows // 2, width), jnp.float32),
            pltpu.SemaphoreType.DMA((2,)),
            pltpu.SemaphoreType.DMA((rows // 2 // CHUNK,)),
        ],
    )


def sum_middle_back(part, middle, cotangent, gain, hidden, both, count):
    rows, width = part.shape
    last = width // WIDE - 1
    at = lambda i: jnp.minimum(i // SPACING, last)
    return chain_call(
        functools.partial(middle_back_kernel, count), "sum_middle_back", 2, count, part.shape,
        [
            (part, VMEM_SPEC), (middle, HBM_SPEC), (cotangent, HBM_SPEC), (gain, VMEM_SPEC),
            (hidden, HBM_SPEC), (both, pl.BlockSpec((both.shape[0], WIDE), lambda i: (0, at(i)))),
        ],
        [
            far(part.shape, jnp.bfloat16),
            far((rows // 2, width), jnp.float32),
            kept((8, width), jnp.float32),
            (
                jax.ShapeDtypeStruct(part.shape, jnp.bfloat16),
                pl.BlockSpec((rows, WIDE), lambda i: (0, at(i))),
            ),
        ],
        [
            pltpu.VMEM((rows // 2, width), jnp.float32),
            pltpu.VMEM(part.shape, jnp.bfloat16),
            pltpu.VMEM(hidden.shape, jnp.bfloat16),
            pltpu.VMEM((rows // 2, width), jnp.float32),
            pltpu.SemaphoreType.DMA((3,)),
            pltpu.SemaphoreType.DMA((rows // 2 // CHUNK,)),
        ],
    )


def sum_input_back(part, tokens, grad, gain, other, size, count):
    width = part.shape[1]
    plane = width // size
    return chain_call(
        functools.partial(input_back_kernel, count), "sum_input_back", 3, count, part.shape,
        [
            (part, VMEM_SPEC), (tokens, HBM_SPEC), (grad, HBM_SPEC), (gain, VMEM_SPEC),
            (other, VMEM_SPEC),
        ],
        [far(part.shape, jnp.bfloat16), kept((2, size), jnp.float32)],
        [
            pltpu.VMEM(part.shape, jnp.bfloat16),
            pltpu.VMEM(grad.shape, jnp.float32),
            pltpu.VMEM((16, width), jnp.float32),
            pltpu.VMEM((plane, 16, size), jnp.float32),
            pltpu.VMEM((2, 16, size), jnp.float32),
            pltpu.SemaphoreType.DMA((2,)),
            pltpu.SemaphoreType.DMA((plane,)),
            pltpu.SemaphoreType.DMA((plane,)),
            pltpu.SemaphoreType.DMA((2,)),
            pltpu.SemaphoreType.DMA((2,)),
        ],
    )


def rotate_pairs(values, cosine, sine):
    parts = [
        rotate_lanes(values[:, at : at + PAIR], cosine, sine)
        for at in range(0, values.shape[1], PAIR)
    ]
    return jnp.concatenate(parts, 1)


def plane_peers():
    ctx = lax.axis_size("ctx")
    size = lax.axis_size("shard") * ctx
    mine = lax.axis_index("shard") * ctx + lax.axis_index("ctx")

    def peer(distance):
        index = lax.rem(mine + distance, size)
        return index, {"shard": index // ctx, "ctx": lax.rem(index, ctx)}

    return size, mine, peer


def greet_plane(size, peer):
    barrier = pltpu.get_barrier_semaphore()
    for distance in range(1, size):
        pl.semaphore_signal(barrier, inc=1, device_id=peer(distance)[1], device_id_type=MESH)


def front_kernel(
    live_ref, tokens_hbm, weight_hbm, own_gain_ref, cos_ref, sin_ref,
    h_hbm, q_ref, k_ref, v_ref, kp_ref, vp_ref, o_ref, l_ref, gain_ref,
    send, recv, gain_send, gain_recv, tokens_ref, weight_ref, h_ref, load_sem, store_sem,
):
    load, wait = loads_of([(tokens_hbm, tokens_ref), (weight_hbm, weight_ref)], load_sem)
    load()
    late = lax.axis_index("ctx")
    rows, width = q_ref.shape
    block = min(BLOCK, rows)
    blocks = rows // block
    pairs = width // PAIR
    size, index, peer = plane_peers()
    part = own_gain_ref.shape[1]
    greet_plane(size, peer)
    pl.semaphore_wait(pltpu.get_barrier_semaphore(), size - 1)
    mine = pl.ds(pl.multiple_of(index * part, part), part)
    gain_ref[:, mine] = own_gain_ref[...]

    def gain_copy(distance):
        return pltpu.make_async_remote_copy(
            src_ref=own_gain_ref, dst_ref=gain_ref.at[:, mine],
            send_sem=gain_send.at[distance], recv_sem=gain_recv.at[distance],
            device_id=peer(distance)[1], device_id_type=MESH,
        )

    for distance in range(1, size):
        gain_copy(distance).start()
    for distance in range(1, size):
        gain_copy(distance).wait()
    wait()

    def here(at):
        return pl.ds(pl.multiple_of(at * block, block), block)

    def lanes(pair):
        return pl.ds(pl.multiple_of(pair * PAIR, PAIR), PAIR)

    def h_store(at):
        return pltpu.make_async_copy(h_ref.at[here(at)], h_hbm.at[here(at)], store_sem.at[at])

    @pl.loop(0, blocks)
    def _(at):
        stream = tokens_ref[here(at)].astype(jnp.float32)
        normed = (stream * unit_scale(stream) * gain_ref[0:1]).astype(jnp.bfloat16)
        h_ref[here(at)] = normed
        h_store(at).start()
        keys = dot(normed, weight_ref[1], (1, 0))
        k_ref[here(at)] = rotate_pairs(keys, cos_ref[here(at)], sin_ref[here(at)]).astype(jnp.bfloat16)
        v_ref[here(at)] = dot(normed, weight_ref[2], (1, 0)).astype(jnp.bfloat16)

    def exchange(pair):
        return [
            pltpu.make_async_remote_copy(
                src_ref=own.at[:, lanes(pair)], dst_ref=prev.at[:, lanes(pair)],
                send_sem=send.at[which, pair], recv_sem=recv.at[which, pair],
                device_id={"ctx": 1 - late}, device_id_type=MESH,
            )
            for which, own, prev in ((0, k_ref, kp_ref), (1, v_ref, vp_ref))
        ]

    @pl.when(late == 0)
    def _():
        @pl.loop(0, pairs)
        def _(pair):
            for copy in exchange(pair):
                copy.start()

    @pl.loop(0, blocks)
    def _(at):
        query = dot(h_ref[here(at)], weight_ref[0], (1, 0))
        query = rotate_pairs(query, cos_ref[here(at)], sin_ref[here(at)]) * 0.125
        q_ref[here(at)] = query.astype(jnp.bfloat16)

    def attend(pair, own, with_prev):
        column = lanes(pair)
        mine = slice(own * block, (own + 1) * block)
        query = q_ref[mine, column]
        mixed = []
        for head in range(2):
            queries = one_head(query, head)
            parts = []
            if with_prev:
                parts.append((dot(kp_ref[:, column], queries, (1, 1)), vp_ref[:, column]))
            if own:
                before = slice(0, own * block)
                parts.append((dot(k_ref[before, column], queries, (1, 1)), v_ref[before, column]))
            parts.append((causal(dot(k_ref[mine, column], queries, (1, 1))), v_ref[mine, column]))
            peak = parts[0][0].max(0, keepdims=True)
            for scores, _ in parts[1:]:
                peak = jnp.maximum(peak, scores.max(0, keepdims=True))
            expo = [jnp.exp(scores - peak) for scores, _ in parts]
            denom = expo[0].sum(0, keepdims=True)
            for e in expo[1:]:
                denom = denom + e.sum(0, keepdims=True)
            inverse = 1.0 / denom
            total = None
            for e, (_, value) in zip(expo, parts):
                term = dot(value, (e * inverse).astype(jnp.bfloat16), (0, 0))
                total = term if total is None else total + term
            mixed.append(total[head * HEAD : (head + 1) * HEAD])
            index = late * rows + own * block + lax.broadcasted_iota(jnp.int32, peak.shape, 1)
            l_ref[pair, head : head + 1, mine] = jnp.where(
                index < live_ref[0], peak + jnp.log(denom), -MASKED
            )
        result = jnp.concatenate(mixed, 0).T
        index = late * rows + own * block + lax.broadcasted_iota(jnp.int32, result.shape, 0)
        own_value = v_ref[mine, column].astype(jnp.float32)
        o_ref[mine, column] = jnp.where(index < live_ref[0], result, own_value).astype(jnp.bfloat16)

    @pl.loop(0, pairs)
    def _(pair):
        @pl.when(late == 0)
        def _():
            for own in range(blocks):
                attend(pair, own, False)

        @pl.when(late == 1)
        def _():
            for copy in exchange(pair):
                copy.wait_recv()
            for own in range(blocks):
                attend(pair, own, True)

    @pl.when(late == 0)
    def _():
        @pl.loop(0, pairs)
        def _(pair):
            for copy in exchange(pair):
                copy.wait_send()

    @pl.loop(0, blocks)
    def _(at):
        h_store(at).wait()


def layer_front(live, tokens, weight, gain, cosine, sine):
    rows, depth = tokens.shape
    width = weight.shape[2]
    pairs = width // PAIR
    part = jax.ShapeDtypeStruct((rows, width), jnp.bfloat16)
    outs = (
        jax.ShapeDtypeStruct((rows, depth), jnp.bfloat16), part, part, part, part, part, part,
        jax.ShapeDtypeStruct((pairs, 2, rows), jnp.float32),
        jax.ShapeDtypeStruct((8, depth), jnp.float32),
    )
    size = lax.axis_size("shard") * lax.axis_size("ctx")
    return pl.pallas_call(
        front_kernel,
        out_shape=outs,
        in_specs=[SMEM_SPEC, HBM_SPEC, HBM_SPEC] + [VMEM_SPEC] * 3,
        out_specs=(HBM_SPEC,) + (VMEM_SPEC,) * (len(outs) - 1),
        scratch_shapes=[pltpu.SemaphoreType.DMA((2, pairs))] * 2
        + [pltpu.SemaphoreType.DMA((size,))] * 2
        + [
            pltpu.VMEM(tokens.shape, jnp.bfloat16),
            pltpu.VMEM(weight.shape, jnp.bfloat16),
            pltpu.VMEM(tokens.shape, jnp.bfloat16),
            pltpu.SemaphoreType.DMA((2,)),
            pltpu.SemaphoreType.DMA((rows // BLOCK,)),
        ],
        compiler_params=pltpu.CompilerParams(
            collective_id=4, has_side_effects=True, vmem_limit_bytes=56 * 2**20
        ),
        cost_estimate=pl.CostEstimate(
            flops=80 * 10**9, bytes_accessed=40 * 2**20, transcendentals=0
        ),
        name="layer_front",
    )(live, tokens, weight, gain, cosine, sine)


def attend_back_kernel(
    count, live_ref, q_hbm, k_hbm, v_hbm, kp_hbm, vp_hbm, o_hbm, l_ref, cos_ref, sin_ref,
    part_ref, middle_hbm, grad_ref, both_hbm, dq_ref, dk_ref, dv_ref, out_ref,
    q_ref, k_ref, v_ref, kp_ref, vp_ref, o_ref, do_ref, weight_ref, middle_ref, early_sem, late_sem,
    dq_acc, dk_acc, dv_acc, dkp_acc, dvp_acc, leave, arrive, slots, send, recv, chain_send, chain_recv,
):
    late = lax.axis_index("ctx")
    me = lax.axis_index("tp")
    rows, width = q_ref.shape
    block = min(BLOCK, rows)
    blocks = rows // block
    pairs = width // PAIR
    load_early, wait_early = loads_of(
        [(both_hbm.at[pl.ds(0, width)], weight_ref), (middle_hbm, middle_ref)], early_sem
    )
    load_late, wait_late = loads_of(
        [
            (o_hbm, o_ref), (q_hbm, q_ref), (kp_hbm, kp_ref), (vp_hbm, vp_ref), (k_hbm, k_ref),
            (v_hbm, v_ref),
        ],
        late_sem,
    )
    load_early()
    load_late()
    barrier = pltpu.get_barrier_semaphore()
    pl.semaphore_signal(barrier, inc=1, device_id={"ctx": 1 - late}, device_id_type=MESH)
    greet(me, count, 1)
    tick, drain, ticks = chain_parts(
        count, part_ref, out_ref, slots, chain_send, chain_recv,
        lambda rows, part, total, at: (middle_ref[part] + total).astype(jnp.bfloat16), BACK_CHUNK, BACK_LAG,
    )

    def here(at):
        return pl.ds(pl.multiple_of(at * block, block), block)

    def lanes(pair):
        return pl.ds(pl.multiple_of(pair * PAIR, PAIR), PAIR)

    def prepare(pair, step):
        column = lanes(pair)
        query = q_ref[here(step), column]
        upstream = do_ref[here(step), column]
        product = (upstream.astype(jnp.float32) * o_ref[here(step), column].astype(jnp.float32)).T
        queries = [one_head(query, head) for head in range(2)]
        upstreams = [one_head(upstream, head) for head in range(2)]
        inner = [
            product[head * HEAD : (head + 1) * HEAD].sum(0, keepdims=True) for head in range(2)
        ]
        totals = [l_ref[pair, head : head + 1, here(step)] for head in range(2)]
        query_both = jnp.concatenate(queries, 0)
        upstream_both = jnp.concatenate(upstreams, 0)

        def tile(keys, values, masked):
            grads, probs_all, out = [], [], []
            for head in range(2):
                scores = dot(keys, queries[head], (1, 1))
                if masked:
                    scores = causal(scores)
                probs = jnp.exp(scores - totals[head])
                prob_grad = dot(values, upstreams[head], (1, 1))
                score_grad = (probs * (prob_grad - inner[head])).astype(jnp.bfloat16)
                probs_all.append(probs.astype(jnp.bfloat16))
                grads.append(score_grad)
                out.append(dot(keys, score_grad, (0, 0))[head * HEAD : (head + 1) * HEAD])
            key_grad = dot(jnp.concatenate(grads, 1), query_both, (1, 0))
            value_grad = dot(jnp.concatenate(probs_all, 1), upstream_both, (1, 0))
            return jnp.concatenate(out, 0), key_grad, value_grad

        return tile, upstream

    def exchange(pair):
        return pltpu.make_async_remote_copy(
            src_ref=leave.at[pair], dst_ref=arrive.at[pair], send_sem=send.at[pair],
            recv_sem=recv.at[pair], device_id={"ctx": 1 - late}, device_id_type=MESH,
        )

    def prev_step(pair, step):
        column = lanes(pair)
        tile, _ = prepare(pair, step)

        @pl.when(step == 0)
        def _():
            dkp_acc[...] = jnp.zeros_like(dkp_acc)
            dvp_acc[...] = jnp.zeros_like(dvp_acc)

        query_grad = None
        for at in range(blocks):
            mine = slice(at * block, (at + 1) * block)
            more, key_grad, value_grad = tile(kp_ref[mine, column], vp_ref[mine, column], False)
            query_grad = more if query_grad is None else query_grad + more
            dkp_acc[mine] += key_grad
            dvp_acc[mine] += value_grad
        dq_acc[pair, :, here(step)] = query_grad

        @pl.when(step == blocks - 1)
        def _():
            leave[pair, 0] = dkp_acc[...].astype(jnp.bfloat16)
            leave[pair, 1] = dvp_acc[...].astype(jnp.bfloat16)
            exchange(pair).start()

    def own_step(pair, step):
        column = lanes(pair)
        tile, upstream = prepare(pair, step)
        query_grad, key_grad, value_grad = tile(k_ref[here(step), column], v_ref[here(step), column], True)
        index = late * rows + step * block + lax.broadcasted_iota(jnp.int32, upstream.shape, 0)
        dk_acc[here(step), column] = key_grad
        dv_acc[here(step), column] = value_grad + jnp.where(
            index < live_ref[0], 0.0, upstream.astype(jnp.float32)
        )
        dq_acc[pair, :, here(step)] += query_grad

        @pl.loop(0, step)
        def _(at):
            more, key_grad, value_grad = tile(k_ref[here(at), column], v_ref[here(at), column], False)
            dk_acc[here(at), column] += key_grad
            dv_acc[here(at), column] += value_grad
            dq_acc[pair, :, here(step)] += more

        grad = dq_acc[pair, :, here(step)].T * 0.125
        grad = rotate_lanes(grad, cos_ref[here(step)], -sin_ref[here(step)])
        dq_ref[here(step), column] = grad.astype(jnp.bfloat16)

    @pl.when(late == 0)
    def _():
        dq_acc[...] = jnp.zeros_like(dq_acc)

    wait_early()

    @pl.loop(0, blocks)
    def _(at):
        for more in range(LEAD):
            tick(at * LEAD + more)
        do_ref[here(at)] = dot(grad_ref[here(at)], weight_ref[...], (1, 1)).astype(jnp.bfloat16)

    wait_late()
    steps = pairs * blocks
    lead = blocks * LEAD

    @pl.loop(0, 2 * steps)
    def _(at):
        @pl.when(lead + at < ticks)
        def _():
            tick(lead + at)

        @pl.when((late == 1) & (at < steps))
        def _():
            prev_step(at // blocks, at % blocks)

        @pl.when(at >= steps)
        def _():
            own_step((at - steps) // blocks, at % blocks)

    if ticks > lead + 2 * steps:
        pl.loop(lead + 2 * steps, ticks)(tick)

    @pl.loop(0, pairs)
    def _(pair):
        column = lanes(pair)

        @pl.when(late == 0)
        def _():
            exchange(pair).wait_recv()
            dk_acc[:, column] += arrive[pair, 0].astype(jnp.float32)
            dv_acc[:, column] += arrive[pair, 1].astype(jnp.float32)

        @pl.when(late == 1)
        def _():
            exchange(pair).wait_send()

        dk_ref[:, column] = rotate_lanes(dk_acc[:, column], cos_ref[...], -sin_ref[...]).astype(
            jnp.bfloat16
        )
        dv_ref[:, column] = dv_acc[:, column].astype(jnp.bfloat16)

    drain()


def attend_back(live, arrays, cosine, sine, out_part, middle, grad, both, count):
    rows, width = arrays[0].shape
    pairs = width // PAIR
    part = jax.ShapeDtypeStruct((rows, width), jnp.bfloat16)
    outs = (
        part, part, part, jax.ShapeDtypeStruct(out_part.shape, jnp.bfloat16),
    )
    chunks = rows // 2 // BACK_CHUNK
    return pl.pallas_call(
        functools.partial(attend_back_kernel, count),
        out_shape=outs,
        in_specs=[SMEM_SPEC] + [HBM_SPEC] * 6 + [VMEM_SPEC] * 4 + [HBM_SPEC, VMEM_SPEC, HBM_SPEC],
        out_specs=(VMEM_SPEC,) * len(outs),
        scratch_shapes=[
            *[pltpu.VMEM((rows, width), jnp.bfloat16)] * 7,
            pltpu.VMEM((width, middle.shape[1]), jnp.bfloat16),
            pltpu.VMEM(middle.shape, jnp.float32),
            pltpu.SemaphoreType.DMA((2,)),
            pltpu.SemaphoreType.DMA((6,)),
            pltpu.VMEM((pairs, PAIR, rows), jnp.float32),
            pltpu.VMEM((rows, width), jnp.float32),
            pltpu.VMEM((rows, width), jnp.float32),
            pltpu.VMEM((rows, PAIR), jnp.float32),
            pltpu.VMEM((rows, PAIR), jnp.float32),
            pltpu.VMEM((pairs, 2, rows, PAIR), jnp.bfloat16),
            pltpu.VMEM((pairs, 2, rows, PAIR), jnp.bfloat16),
            pltpu.VMEM((2, rows // 2, out_part.shape[1]), jnp.bfloat16),
            pltpu.SemaphoreType.DMA((pairs,)),
            pltpu.SemaphoreType.DMA((pairs,)),
            pltpu.SemaphoreType.DMA((4, chunks)),
            pltpu.SemaphoreType.DMA((4, chunks)),
        ],
        compiler_params=pltpu.CompilerParams(
            collective_id=5, has_side_effects=True, vmem_limit_bytes=58 * 2**20
        ),
        cost_estimate=pl.CostEstimate(
            flops=100 * 10**9, bytes_accessed=40 * 2**20, transcendentals=0
        ),
        name="attend_back",
    )(live, *arrays, cosine, sine, out_part, middle, grad, both)


def narrow_kernel(
    out_ref, down_ref, gate_up_ref, cos_in, sin_in, both_ref, low_ref, cos_ref, sin_ref
):
    cos_ref[...] = cos_in[...]
    sin_ref[...] = sin_in[...]
    split = out_ref.shape[0]
    both_ref[:split] = out_ref[...].astype(jnp.bfloat16)
    both_ref[split:] = down_ref[...].astype(jnp.bfloat16)
    low_ref[...] = gate_up_ref[...].astype(jnp.bfloat16)


def narrow(out_weight, down_weight, gate_up_weight, cosine, sine):
    return pl.pallas_call(
        narrow_kernel,
        out_shape=(
            jax.ShapeDtypeStruct(
                (out_weight.shape[0] + down_weight.shape[0], out_weight.shape[1]), jnp.bfloat16
            ),
            jax.ShapeDtypeStruct(gate_up_weight.shape, jnp.bfloat16),
            jax.ShapeDtypeStruct(cosine.shape, jnp.float32),
            jax.ShapeDtypeStruct(sine.shape, jnp.float32),
        ),
        in_specs=[VMEM_SPEC] * 5,
        out_specs=(VMEM_SPEC,) * 4,
        compiler_params=pltpu.CompilerParams(vmem_limit_bytes=40 * 2**20),
        cost_estimate=pl.CostEstimate(flops=40 * 10**9, bytes_accessed=2**24, transcendentals=0),
        name="narrow",
    )(out_weight, down_weight, gate_up_weight, cosine, sine)


def mlp_kernel(
    normed_ref, weight_ref, hidden_grad_ref, cotangent_ref,
    hidden_ref, down_grad_ref, gate_up_grad_ref, back_ref, turned, total,
):
    step = pl.program_id(0)

    @pl.when(step == 0)
    def _():
        turned[...] = normed_ref[...].T
        total[...] = jnp.zeros_like(total)

    gate = dot(normed_ref[...], weight_ref[0], (1, 0))
    upward = dot(normed_ref[...], weight_ref[1], (1, 0))
    hidden_grad = hidden_grad_ref[...]
    sigma = jax.nn.sigmoid(gate)
    swish = gate * sigma
    hidden = (swish * upward).astype(jnp.bfloat16)
    hidden_ref[...] = hidden
    gate_grad = (hidden_grad * upward * sigma * (1.0 + gate * (1.0 - sigma))).astype(jnp.bfloat16)
    upward_grad = (hidden_grad * swish).astype(jnp.bfloat16)
    both = jnp.concatenate([gate_grad, upward_grad], 1)
    weights = jnp.concatenate([weight_ref[0], weight_ref[1]], 1)
    total[...] += dot(both, weights, (1, 1))
    gate_up_grad_ref[0] = dot(turned[...], gate_grad, (1, 0)).astype(jnp.bfloat16)
    gate_up_grad_ref[1] = dot(turned[...], upward_grad, (1, 0)).astype(jnp.bfloat16)
    down_grad_ref[...] = dot(hidden.T, cotangent_ref[...], (1, 0)).astype(jnp.bfloat16)

    @pl.when(step == pl.num_programs(0) - 1)
    def _():
        back_ref[...] = total[...].astype(jnp.bfloat16)


def mlp(normed, weight, hidden_grad, cotangent):
    rows, depth = normed.shape
    width = weight.shape[2]
    whole = pl.BlockSpec((rows, depth), lambda j: (0, 0), pipeline_mode=pl.Buffered(1))
    return pl.pallas_call(
        mlp_kernel,
        out_shape=(
            jax.ShapeDtypeStruct((rows, width), jnp.bfloat16),
            jax.ShapeDtypeStruct((width, depth), jnp.bfloat16),
            jax.ShapeDtypeStruct((2, depth, width), jnp.bfloat16),
            jax.ShapeDtypeStruct((rows, depth), jnp.bfloat16),
        ),
        grid=(width // MLP_WIDE,),
        in_specs=[
            whole,
            pl.BlockSpec((2, depth, MLP_WIDE), lambda j: (0, 0, j)),
            pl.BlockSpec((rows, MLP_WIDE), lambda j: (0, j)),
            whole,
        ],
        out_specs=(
            pl.BlockSpec((rows, MLP_WIDE), lambda j: (0, j)),
            pl.BlockSpec((MLP_WIDE, depth), lambda j: (j, 0)),
            pl.BlockSpec((2, depth, MLP_WIDE), lambda j: (0, 0, j)),
            pl.BlockSpec((rows, depth), lambda j: (0, 0)),
        ),
        scratch_shapes=[
            pltpu.VMEM((depth, rows), jnp.bfloat16), pltpu.VMEM((rows, depth), jnp.float32),
        ],
        compiler_params=pltpu.CompilerParams(vmem_limit_bytes=60 * 2**20),
        cost_estimate=pl.CostEstimate(
            flops=14 * rows * depth * width, bytes_accessed=80 * 2**20, transcendentals=rows * width
        ),
        name="mlp",
    )(normed, weight, hidden_grad, cotangent)


def projection_back_kernel(
    normed_ref, weight_ref, dq_ref, dk_ref, dv_ref, mixed_ref, middle_ref, grad_ref, back_ref,
    turned, total,
):
    step = pl.program_id(0)

    @pl.when(step == 0)
    def _():
        turned[...] = normed_ref[...].T

    for at, ref in enumerate((dq_ref, dk_ref, dv_ref)):

        @pl.when(step == at)
        def _():
            term = dot(ref[...], weight_ref[0], (1, 1))
            if at == 0:
                total[...] = term
            elif at == 1:
                total[...] += term
            else:
                back_ref[...] = (total[...] + term).astype(jnp.bfloat16)
            grad_ref[0] = dot(turned[...], ref[...], (1, 0)).astype(jnp.bfloat16)

    @pl.when(step == 3)
    def _():
        turned[...] = middle_ref[...].T
        grad_ref[0] = dot(turned[...], mixed_ref[...], (1, 0)).astype(jnp.bfloat16)


def projection_back(normed, weight, dq, dk, dv, mixed, middle):
    rows, depth = normed.shape
    width = dq.shape[1]
    whole = lambda w: pl.BlockSpec((rows, w), lambda j: (0, 0), pipeline_mode=pl.Buffered(1))
    return pl.pallas_call(
        projection_back_kernel,
        out_shape=(
            jax.ShapeDtypeStruct((4, depth, width), jnp.bfloat16),
            jax.ShapeDtypeStruct((rows, depth), jnp.bfloat16),
        ),
        grid=(4,),
        in_specs=[
            whole(depth),
            pl.BlockSpec((1, depth, width), lambda j: (jnp.minimum(j, 2), 0, 0)),
            whole(width), whole(width), whole(width), whole(width), whole(depth),
        ],
        out_specs=(
            pl.BlockSpec((1, depth, width), lambda j: (j, 0, 0)),
            pl.BlockSpec((rows, depth), lambda j: (0, 0)),
        ),
        scratch_shapes=[
            pltpu.VMEM((depth, rows), jnp.bfloat16), pltpu.VMEM((rows, depth), jnp.float32),
        ],
        compiler_params=pltpu.CompilerParams(vmem_limit_bytes=60 * 2**20),
        cost_estimate=pl.CostEstimate(
            flops=14 * rows * depth * width, bytes_accessed=40 * 2**20, transcendentals=0
        ),
        name="projection_back",
    )(normed, weight, dq, dk, dv, mixed, middle)


def tail_kernel(
    grad_ref, out_grad_ref, w_ref, m_ref, s_ref, ow_ref, om_ref, os_ref,
    g_out, w_out, m_out, s_out, og_out, step_out, om_out, os_out,
):
    grad = grad_ref[0:3].astype(jnp.float32)
    update, first, second = adam_update(w_ref[...], m_ref[...], s_ref[...], grad, decay_rate)
    g_out[...] = grad
    w_out[...] = w_ref[...] - update
    m_out[...] = first
    s_out[...] = second
    grad = out_grad_ref[0].astype(jnp.float32).T
    update, first, second = adam_update(ow_ref[...], om_ref[...], os_ref[...], grad, decay_rate)
    og_out[...] = grad
    step_out[...] = update
    om_out[...] = first
    os_out[...] = second


def adam_tail(grads, qkv, out):
    planes, rows, width = qkv[0].shape
    steps = width // PAIR
    mine = pl.BlockSpec((planes, rows // steps, width), lambda i: (0, i, 0))
    other = pl.BlockSpec((PAIR, rows), lambda i: (i, 0))
    shapes = [jax.ShapeDtypeStruct(qkv[0].shape, jnp.float32)] * 4
    shapes += [jax.ShapeDtypeStruct(out[0].shape, jnp.float32)] * 4
    results = pl.pallas_call(
        tail_kernel,
        out_shape=tuple(shapes),
        grid=(steps,),
        in_specs=[
            pl.BlockSpec((planes + 1, rows // steps, width), lambda i: (0, i, 0)),
            pl.BlockSpec((1, rows, PAIR), lambda i: (planes, 0, i)),
            mine, mine, mine, other, other, other,
        ],
        out_specs=(mine,) * 4 + (other,) * 4,
        compiler_params=pltpu.CompilerParams(vmem_limit_bytes=60 * 2**20),
        cost_estimate=pl.CostEstimate(
            flops=10**7, bytes_accessed=16 * 2**20, transcendentals=0
        ),
        name="adam_tail",
    )(grads, grads, *qkv, *out)
    return results[:4], results[4:]


def scatter_low(grad, axis=1):
    return lax.psum_scatter(
        grad.astype(jnp.bfloat16), ("shard", "ctx"), scatter_dimension=axis, tiled=True
    ).astype(jnp.float32)


def after(array, *others):
    return lax.optimization_barrier((array, *others))[0]


def adam_update(weight, first, second, grad, decay):
    first_new = beta_one * first + (1.0 - beta_one) * grad
    second_new = beta_two * second + (1.0 - beta_two) * grad * grad
    first_hat = first_new / (1.0 - beta_one**step_count)
    second_hat = second_new / (1.0 - beta_two**step_count)
    update = learn_rate * (first_hat / (jnp.sqrt(second_hat) + adam_eps) + decay * weight)
    return (update, first_new, second_new)


def body(
    tokens,
    cotangent,
    lengths,
    qkv_weight,
    out_weight,
    gate_up_weight,
    down_weight,
    norm_gains,
    qkv_first,
    out_first,
    gate_up_first,
    down_first,
    gains_first,
    qkv_second,
    out_second,
    gate_up_second,
    down_second,
    gains_second,
):
    row_count = tokens.shape[0]
    count = lax.axis_size("tp")
    offset = lax.axis_index("ctx") * row_count
    query_index = offset + jnp.arange(row_count, dtype=jnp.int32)
    qkv_low = qkv_weight.astype(jnp.bfloat16)
    cosine, sine = rotation(query_index, HEAD)
    cosine, sine = (jnp.concatenate([c[:, 0]] * 4, 1) for c in (cosine, sine))
    both_low, gate_up_low, cosine, sine = narrow(
        out_weight, down_weight, gate_up_weight, cosine, sine
    )
    gains_low = norm_gains.astype(jnp.bfloat16).astype(jnp.float32)
    gains_low = jnp.concatenate([gains_low] * 4, 0)
    gather = lambda a: lax.all_gather(a, ("shard", "ctx"), axis=1, tiled=True)
    qkv_full = gather(qkv_low)
    both_full = gather(after(both_low, qkv_full))
    normed_one, query, keys, values, keys_prev, values_prev, mixed_low, totals, gains_full = layer_front(
        lengths, tokens, qkv_full, gains_low, cosine, sine
    )
    gate_up_full = gather(after(gate_up_low, both_full, totals))
    normed_two, middle, hidden_grad = sum_middle(
        mixed_low, both_full, tokens, gains_full, cotangent, count
    )
    hidden, down_grad_local, gate_up_grad_local, mlp_back_part = mlp(
        normed_two, gate_up_full, hidden_grad, cotangent
    )
    down_grad = scatter_low(down_grad_local)
    middle_low, middle_grad, gain_two_grad, out_part = sum_middle_back(
        mlp_back_part, middle, cotangent, gains_full, hidden, both_full, count
    )
    gate_up_grad = scatter_low(after(gate_up_grad_local, down_grad, middle_low))
    query_low, key_low, value_low, out_tokens = attend_back(
        lengths,
        [query, keys, values, keys_prev, values_prev, mixed_low, totals],
        cosine, sine, out_part, middle, middle_low, both_full, count,
    )
    qkv_grad_local, attn_back_part = projection_back(
        normed_one, qkv_full, query_low, key_low, value_low, mixed_low, middle_low
    )
    attn_back_part, qkv_grad_local, _ = lax.optimization_barrier(
        (attn_back_part, qkv_grad_local, gate_up_grad)
    )
    tail_grads = lax.psum_scatter(
        qkv_grad_local, ("shard", "ctx"), scatter_dimension=1, tiled=True
    )
    input_grad, gains_grad = sum_input_back(
        attn_back_part, tokens, middle_grad, gains_full, gain_two_grad, norm_gains.shape[1], count
    )
    tail_grads, _ = lax.optimization_barrier((tail_grads, gains_grad))
    (qkv_grad, qkv_new, qkv_first_new, qkv_second_new), (
        out_grad, out_step, out_first_new, out_second_new,
    ) = adam_tail(
        tail_grads,
        (qkv_weight, qkv_first, qkv_second),
        (out_weight, out_first, out_second),
    )
    gate_up_step, gate_up_first_new, gate_up_second_new = adam_update(
        gate_up_weight, gate_up_first, gate_up_second, gate_up_grad, decay_rate
    )
    down_step, down_first_new, down_second_new = adam_update(
        down_weight, down_first, down_second, down_grad, decay_rate
    )
    gains_step, gains_first_new, gains_second_new = adam_update(
        norm_gains, gains_first, gains_second, gains_grad, 0.0
    )
    gate_up_new = gate_up_weight - gate_up_step
    down_new = down_weight - down_step
    return (
        out_tokens,
        input_grad,
        qkv_grad,
        out_grad,
        gate_up_grad,
        down_grad,
        gains_grad,
        qkv_new,
        out_step,
        gate_up_new,
        down_new,
        gains_step,
        qkv_first_new,
        out_first_new,
        gate_up_first_new,
        down_first_new,
        gains_first_new,
        qkv_second_new,
        out_second_new,
        gate_up_second_new,
        down_second_new,
        gains_second_new,
    )


def solution(mesh):
    return jax.shard_map(
        body,
        mesh=mesh,
        in_specs=(
            P(("shard", "ctx"), None),
            P(("shard", "ctx"), None),
            P("shard"),
            P(None, ("shard", "ctx"), "tp"),
            P("tp", ("shard", "ctx")),
            P(None, ("shard", "ctx"), "tp"),
            P("tp", ("shard", "ctx")),
            P(None, ("shard", "ctx")),
            P(None, ("shard", "ctx"), "tp"),
            P("tp", ("shard", "ctx")),
            P(None, ("shard", "ctx"), "tp"),
            P("tp", ("shard", "ctx")),
            P(None, ("shard", "ctx")),
            P(None, ("shard", "ctx"), "tp"),
            P("tp", ("shard", "ctx")),
            P(None, ("shard", "ctx"), "tp"),
            P("tp", ("shard", "ctx")),
            P(None, ("shard", "ctx")),
        ),
        out_specs=(
            P(("shard", "ctx"), None),
            P(("shard", "ctx"), None),
            P(None, ("shard", "ctx"), "tp"),
            P("tp", ("shard", "ctx")),
            P(None, ("shard", "ctx"), "tp"),
            P("tp", ("shard", "ctx")),
            P(None, ("shard", "ctx")),
            P(None, ("shard", "ctx"), "tp"),
            P("tp", ("shard", "ctx")),
            P(None, ("shard", "ctx"), "tp"),
            P("tp", ("shard", "ctx")),
            P(None, ("shard", "ctx")),
            P(None, ("shard", "ctx"), "tp"),
            P("tp", ("shard", "ctx")),
            P(None, ("shard", "ctx"), "tp"),
            P("tp", ("shard", "ctx")),
            P(None, ("shard", "ctx")),
            P(None, ("shard", "ctx"), "tp"),
            P("tp", ("shard", "ctx")),
            P(None, ("shard", "ctx"), "tp"),
            P("tp", ("shard", "ctx")),
            P(None, ("shard", "ctx")),
        ),
        check_vma=False,
    )
```

```python
import functools
import jax
import jax.numpy as jnp
from jax import lax
from jax.experimental import pallas as pl
from jax.experimental.pallas import tpu as pltpu
from jax.sharding import PartitionSpec as P

HEAD = 64
PAIR = 128
BLOCK = 256
CHUNK = 16
LAG = 2
BACK_CHUNK = 32
BACK_LAG = 3
WIDE = 256
SPACING = 5
LEAD = 1
MLP_WIDE = 256
MASKED = -1e30
MESH = pl.DeviceIdType.MESH
VMEM_SPEC = pl.BlockSpec(memory_space=pltpu.VMEM)
SMEM_SPEC = pl.BlockSpec(memory_space=pltpu.SMEM)
HBM_SPEC = pl.BlockSpec(memory_space=pl.ANY)


norm_eps = 1e-05
rope_base = 130000.0
beta_one = 0.9
beta_two = 0.95
learn_rate = 0.02
decay_rate = 0.1
adam_eps = 1e-08
step_count = 4.0


def rotation(position, head_size):
    half = head_size // 2
    freqs = rope_base ** (-(jnp.arange(half, dtype=jnp.float32) * 2.0) / head_size)
    angle = position.astype(jnp.float32)[:, None] * freqs[None, :]
    return (jnp.cos(angle)[:, None, :], jnp.sin(angle)[:, None, :])


def dot(left, right, contract):
    return lax.dot_general(
        left, right, ((contract[:1], contract[1:]), ((), ())), preferred_element_type=jnp.float32
    )


def one_head(values, head):
    lane = lax.broadcasted_iota(jnp.int32, values.shape, 1)
    return jnp.where((lane < HEAD) == (head == 0), values, jnp.zeros_like(values))


def causal(scores):
    key = lax.broadcasted_iota(jnp.int32, scores.shape, 0)
    query = lax.broadcasted_iota(jnp.int32, scores.shape, 1)
    return jnp.where(key <= query, scores, MASKED)


def rotate_lanes(values, cosine, sine):
    lane = lax.broadcasted_iota(jnp.int32, values.shape, 1) % HEAD
    width = values.shape[1]
    ahead = pltpu.roll(values, width - HEAD // 2, 1)
    behind = pltpu.roll(values, HEAD // 2, 1)
    return values * cosine + jnp.where(lane < HEAD // 2, -ahead, behind) * sine


def greet(me, count, more=0, more_ends=0):
    barrier = pltpu.get_barrier_semaphore()

    @pl.when(me > 0)
    def _():
        pl.semaphore_signal(barrier, inc=1, device_id={"tp": me - 1}, device_id_type=MESH)

    @pl.when(me < count - 1)
    def _():
        pl.semaphore_signal(barrier, inc=1, device_id={"tp": me + 1}, device_id_type=MESH)

    @pl.when((me > 0) & (me < count - 1))
    def _():
        pl.semaphore_wait(barrier, 2 + more)

    @pl.when((me == 0) | (me == count - 1))
    def _():
        pl.semaphore_wait(barrier, 1 + more + more_ends)


def chain_parts(count, part_ref, out_ref, slots, send, recv, finish, size, lag=1, land=None, stored=None):
    me = lax.axis_index("tp")
    apart = land is not None
    land = land if apart else out_ref
    half = out_ref.shape[0] // 2
    chunks = half // size

    def copy(stream, at, source, target, device):
        return pltpu.make_async_remote_copy(
            src_ref=source, dst_ref=target, send_sem=send.at[stream, at],
            recv_sem=recv.at[stream, at], device_id={"tp": device}, device_id_type=MESH,
        )

    def ends(way):
        place = me if way == 1 else count - 1 - me
        return place, me + way

    def reduce_copy(way, at, device):
        index = 0 if way == 1 else 1
        rows = pl.ds(pl.multiple_of(at * size, size), size)
        return copy(index, at, slots.at[index, rows], slots.at[index, rows], device)

    def spread_copy(way, at, device):
        base = 0 if way == 1 else half
        rows = pl.ds(pl.multiple_of(base + at * size, size), size)
        return copy(2 if way == 1 else 3, at, land.at[rows], land.at[rows], device)

    def store_copy(index, at):
        rows = pl.ds(pl.multiple_of(index * half + at * size, size), size)
        return pltpu.make_async_copy(land.at[rows], out_ref.at[rows], stored.at[index, at])

    def reduce_step(way, tick):
        place, ahead = ends(way)
        index = 0 if way == 1 else 1
        base = half if way == 1 else 0
        at = tick - lag * place

        @pl.when((at >= 0) & (at < chunks))
        def _():
            local = pl.ds(pl.multiple_of(at * size, size), size)
            rows = pl.ds(pl.multiple_of(base + at * size, size), size)

            @pl.when(place == 0)
            def _():
                slots[index, local] = part_ref[rows]

            @pl.when(place > 0)
            def _():
                reduce_copy(way, at, ahead).wait_recv()

            @pl.when((place > 0) & (place < count - 1))
            def _():
                slots[index, local] = (
                    slots[index, local].astype(jnp.float32) + part_ref[rows].astype(jnp.float32)
                ).astype(jnp.bfloat16)

            @pl.when(place < count - 1)
            def _():
                reduce_copy(way, at, ahead).start()

            @pl.when(place == count - 1)
            def _():
                total = slots[index, local].astype(jnp.float32) + part_ref[rows].astype(jnp.float32)
                land[rows] = finish(rows, local, total, at)
                if apart:
                    store_copy(1 if way == 1 else 0, at).start()
                spread_copy(-way, at, me - way).start()

    def spread_step(way, tick):
        place, ahead = ends(way)
        at = tick - lag * (count - 1) - lag * place

        @pl.when((at >= 0) & (at < chunks) & (place > 0))
        def _():
            spread_copy(way, at, ahead).wait_recv()

            @pl.when(place < count - 1)
            def _():
                spread_copy(way, at, ahead).start()

            if apart:
                store_copy(0 if way == 1 else 1, at).start()

    def step(tick):
        for way in (1, -1):
            reduce_step(way, tick)
        for way in (1, -1):
            spread_step(way, tick)

    def drain():
        @pl.loop(0, chunks)
        def _(at):
            if apart:
                for index in range(2):
                    store_copy(index, at).wait()

            for way in (1, -1):
                place, ahead = ends(way)

                @pl.when(place < count - 1)
                def _():
                    reduce_copy(way, at, ahead).wait_send()
                    spread_copy(way, at, ahead).wait_send()

    return step, drain, chunks + 2 * lag * (count - 1)


def run_ticks(parts, start, wait, finally_drain):
    step, drain, ticks = parts
    tick = pl.program_id(0)
    pl.when(tick == 0)(start)
    pl.when(tick == SPACING - 2)(wait)
    step(tick)

    @pl.when(tick == ticks - 1)
    def _():
        drain()
        finally_drain()

    return tick


def tick_count(rows, count):
    return rows // 2 // CHUNK + 2 * LAG * (count - 1)


def unit_scale(stream):
    return lax.rsqrt(jnp.mean(stream * stream, axis=-1, keepdims=True) + norm_eps)


def fold(values):
    return values.reshape(-1, 8, values.shape[1]).sum(0)


def norm_back(stream, gain, upstream):
    scale = unit_scale(stream)
    gain_grad = fold(upstream * stream * scale)
    inner = jnp.sum(upstream * gain * stream, axis=-1, keepdims=True)
    grad = scale * gain * upstream - stream * (scale * scale * scale / stream.shape[-1]) * inner
    return grad, gain_grad


def loads_of(pairs, sems):
    copies = [
        pltpu.make_async_copy(source, target, sems.at[at])
        for at, (source, target) in enumerate(pairs)
    ]

    def start():
        for copy in copies:
            copy.start()

    def wait():
        for copy in copies:
            copy.wait()

    return start, wait


def half_store(source, target, sems, count):
    chunks = source.shape[0] // CHUNK
    me = lax.axis_index("tp")

    def copy(at):
        rows = pl.ds(pl.multiple_of(at * CHUNK, CHUNK), CHUNK)
        return pltpu.make_async_copy(source.at[rows], target.at[rows], sems.at[at])

    def drain():
        @pl.when((me == 0) | (me == count - 1))
        def _():
            @pl.loop(0, chunks)
            def _(at):
                copy(at).wait()

    return copy, drain


def middle_kernel(
    count, blocks, mixed_ref, weight_ref, tokens_hbm, gain_ref, cotangent_hbm, down_ref,
    out_ref, middle_ref, hidden_grad_ref,
    slots, land, send, recv, stored, part_ref, tokens_ref, cotangent_ref, middle, load_sem, half_sem,
):
    load, wait = loads_of([(tokens_hbm, tokens_ref), (cotangent_hbm, cotangent_ref)], load_sem)
    half_copy, half_drain = half_store(middle, middle_ref, half_sem, count)

    def start():
        load()
        greet(lax.axis_index("tp"), count)

        project(0)

    half_blocks = part_ref.shape[0] // 2 // BLOCK

    def project(at):
        for half in range(2):
            here = pl.ds(pl.multiple_of((half * half_blocks + at) * BLOCK, BLOCK), BLOCK)
            part_ref[here] = dot(mixed_ref[here], weight_ref[...], (1, 0)).astype(jnp.bfloat16)

    def finish(rows, local, total, at):
        value = tokens_ref[rows].astype(jnp.float32) + total
        middle[local] = value
        half_copy(at).start()
        return (value * unit_scale(value) * gain_ref[1:2]).astype(jnp.bfloat16)

    parts = chain_parts(
        count, part_ref, out_ref, slots, send, recv, finish, CHUNK, LAG, land, stored
    )
    tick = run_ticks(parts, start, wait, half_drain)

    @pl.when((tick >= 1) & (tick < half_blocks))
    def _():
        project(tick)

    @pl.when((tick % SPACING == SPACING - 1) & (tick < blocks * SPACING))
    def _():
        hidden_grad_ref[...] = dot(cotangent_ref[...], down_ref[...], (1, 1))


def middle_back_kernel(
    count, part_ref, middle_hbm, cotangent_hbm, gain_ref, hidden_hbm, down_ref,
    out_ref, grad_ref, gain_grad_ref, layer_ref,
    slots, land, send, recv, stored, middle_ref, cotangent_ref, hidden_ref, grad, load_sem, half_sem,
):
    load, wait = loads_of(
        [(middle_hbm, middle_ref), (cotangent_hbm, cotangent_ref), (hidden_hbm, hidden_ref)],
        load_sem,
    )
    half_copy, half_drain = half_store(grad, grad_ref, half_sem, count)

    def start():
        load()
        greet(lax.axis_index("tp"), count)
        gain_grad_ref[...] = jnp.zeros_like(gain_grad_ref)

    def finish(rows, local, total, at):
        value, gain_grad = norm_back(middle_ref[local], gain_ref[1:2], total)
        gain_grad_ref[...] += gain_grad
        value = cotangent_ref[rows].astype(jnp.float32) + value
        grad[local] = value
        half_copy(at).start()
        return value.astype(jnp.bfloat16)

    parts = chain_parts(
        count, part_ref, out_ref, slots, send, recv, finish, CHUNK, LAG, land, stored
    )
    tick = run_ticks(parts, start, wait, half_drain)

    @pl.when((tick % SPACING == SPACING - 1) & (tick < part_ref.shape[1] // WIDE * SPACING))
    def _():
        skip = down_ref.shape[0] - hidden_ref.shape[1]
        layer_ref[...] = dot(hidden_ref[...], down_ref[skip:], (1, 0)).astype(jnp.bfloat16)


def input_back_kernel(
    count, part_ref, tokens_hbm, grad_hbm, gain_ref, other_ref, out_ref, gains_ref,
    slots, land, send, recv, stored, tokens_ref, grad_ref, local, landed, along,
    load_sem, plane_send, plane_recv, line_send, line_recv,
):
    load, wait = loads_of([(tokens_hbm, tokens_ref), (grad_hbm, grad_ref)], load_sem)

    me = lax.axis_index("tp")
    size, index, peer = plane_peers()
    width = gains_ref.shape[1]
    last = (me == 0) | (me == count - 1)

    def start():
        load()

        @pl.when(last)
        def _():
            greet_plane(size, peer)

        greet(me, count, 0, size - 1)
        local[0:8] = jnp.zeros((8, local.shape[1]), jnp.float32)
        local[8:16] = other_ref[...]

    def finish(rows, part, total, at):
        grad, gain_grad = norm_back(tokens_ref[rows].astype(jnp.float32), gain_ref[0:1], total)
        local[0:8] += gain_grad
        return (grad_ref[part] + grad).astype(jnp.bfloat16)

    step, drain, ticks = chain_parts(
        count, part_ref, out_ref, slots, send, recv, finish, CHUNK, LAG, land, stored
    )

    def columns(at):
        return pl.ds(pl.multiple_of(at * width, width), width)

    def plane_copy(distance):
        at, device = peer(distance)
        return pltpu.make_async_remote_copy(
            src_ref=local.at[:, columns(at)], dst_ref=landed.at[distance],
            send_sem=plane_send.at[distance], recv_sem=plane_recv.at[distance],
            device_id=device, device_id_type=MESH,
        )

    def line_copy(way):
        which = 0 if way == 1 else 1
        return pltpu.make_async_remote_copy(
            src_ref=along.at[which], dst_ref=along.at[which],
            send_sem=line_send.at[which], recv_sem=line_recv.at[which],
            device_id={"tp": me + way}, device_id_type=MESH,
        )

    done = out_ref.shape[0] // 2 // CHUNK + LAG * (count - 1)

    tick = pl.program_id(0)
    pl.when(tick == 0)(start)
    pl.when(tick == SPACING - 2)(wait)
    step(tick)

    @pl.when(last & (tick == done - 1))
    def _():
        for distance in range(1, size):
            plane_copy(distance).start()

    @pl.when(last & (tick == done + LAG))
    def _():
        total = local[:, columns(index)]
        for distance in range(1, size):
            plane_copy(distance).wait()
            total = total + landed[distance]

        @pl.when(me == 0)
        def _():
            along[0] = total
            line_copy(1).start()

        @pl.when(me == count - 1)
        def _():
            along[1] = total
            line_copy(-1).start()

    for way in (1, -1):
        place = me if way == 1 else count - 1 - me

        @pl.when((place > 0) & (tick == jnp.minimum(done + LAG + place, ticks - 1)))
        def _():
            line_copy(way).wait_recv()

            @pl.when(place < count - 1)
            def _():
                line_copy(way).start()

    @pl.when(tick == ticks - 1)
    def _():
        for way in (1, -1):
            place = me if way == 1 else count - 1 - me

            @pl.when(place < count - 1)
            def _():
                line_copy(way).wait_send()

        sums = along[0] + along[1]
        gains_ref[0:1] = sums[0:8].sum(0, keepdims=True)
        gains_ref[1:2] = sums[8:16].sum(0, keepdims=True)
        drain()


def chain_call(kernel, name, number, count, shape, inputs, outs, scratch):
    rows, width = shape
    chunks = rows // 2 // CHUNK
    arrays, in_specs = zip(*inputs)
    out_shape, out_specs = zip(*outs)
    return pl.pallas_call(
        kernel,
        out_shape=out_shape,
        grid=(tick_count(rows, count),),
        in_specs=in_specs,
        out_specs=out_specs,
        scratch_shapes=[
            pltpu.VMEM((2, rows // 2, width), jnp.bfloat16),
            pltpu.VMEM((rows, width), jnp.bfloat16),
            pltpu.SemaphoreType.DMA((4, chunks)),
            pltpu.SemaphoreType.DMA((4, chunks)),
            pltpu.SemaphoreType.DMA((2, chunks)),
            *scratch,
        ],
        compiler_params=pltpu.CompilerParams(
            collective_id=number, has_side_effects=True, vmem_limit_bytes=60 * 2**20
        ),
        cost_estimate=pl.CostEstimate(
            flops=100 * 10**9, bytes_accessed=12 * rows * width, transcendentals=0
        ),
        name=name,
    )(*arrays)


def far(shape, dtype):
    return jax.ShapeDtypeStruct(shape, dtype), HBM_SPEC


def kept(shape, dtype):
    return jax.ShapeDtypeStruct(shape, dtype), VMEM_SPEC


def sum_middle(mixed, both, tokens, gain, cotangent, count):
    rows, width = tokens.shape
    inner = mixed.shape[1]
    hidden = both.shape[0] - inner
    last = hidden // WIDE - 1
    at = lambda i: jnp.minimum(i // SPACING, last)
    return chain_call(
        functools.partial(middle_kernel, count, last + 1), "sum_middle", 1, count, tokens.shape,
        [
            (mixed, VMEM_SPEC),
            (both, pl.BlockSpec((inner, width), lambda i: (0, 0), pipeline_mode=pl.Buffered(1))),
            (tokens, HBM_SPEC), (gain, VMEM_SPEC), (cotangent, HBM_SPEC),
            (both, pl.BlockSpec((WIDE, width), lambda i: (inner // WIDE + at(i), 0))),
        ],
        [
            far(tokens.shape, jnp.bfloat16),
            far((rows // 2, width), jnp.float32),
            (
                jax.ShapeDtypeStruct((rows, hidden), jnp.float32),
                pl.BlockSpec((rows, WIDE), lambda i: (0, at(i))),
            ),
        ],
        [
            *[pltpu.VMEM(tokens.shape, jnp.bfloat16)] * 3,
            pltpu.VMEM((rows // 2, width), jnp.float32),
            pltpu.SemaphoreType.DMA((2,)),
            pltpu.SemaphoreType.DMA((rows // 2 // CHUNK,)),
        ],
    )


def sum_middle_back(part, middle, cotangent, gain, hidden, both, count):
    rows, width = part.shape
    last = width // WIDE - 1
    at = lambda i: jnp.minimum(i // SPACING, last)
    return chain_call(
        functools.partial(middle_back_kernel, count), "sum_middle_back", 2, count, part.shape,
        [
            (part, VMEM_SPEC), (middle, HBM_SPEC), (cotangent, HBM_SPEC), (gain, VMEM_SPEC),
            (hidden, HBM_SPEC), (both, pl.BlockSpec((both.shape[0], WIDE), lambda i: (0, at(i)))),
        ],
        [
            far(part.shape, jnp.bfloat16),
            far((rows // 2, width), jnp.float32),
            kept((8, width), jnp.float32),
            (
                jax.ShapeDtypeStruct(part.shape, jnp.bfloat16),
                pl.BlockSpec((rows, WIDE), lambda i: (0, at(i))),
            ),
        ],
        [
            pltpu.VMEM((rows // 2, width), jnp.float32),
            pltpu.VMEM(part.shape, jnp.bfloat16),
            pltpu.VMEM(hidden.shape, jnp.bfloat16),
            pltpu.VMEM((rows // 2, width), jnp.float32),
            pltpu.SemaphoreType.DMA((3,)),
            pltpu.SemaphoreType.DMA((rows // 2 // CHUNK,)),
        ],
    )


def sum_input_back(part, tokens, grad, gain, other, size, count):
    width = part.shape[1]
    plane = width // size
    return chain_call(
        functools.partial(input_back_kernel, count), "sum_input_back", 3, count, part.shape,
        [
            (part, VMEM_SPEC), (tokens, HBM_SPEC), (grad, HBM_SPEC), (gain, VMEM_SPEC),
            (other, VMEM_SPEC),
        ],
        [far(part.shape, jnp.bfloat16), kept((2, size), jnp.float32)],
        [
            pltpu.VMEM(part.shape, jnp.bfloat16),
            pltpu.VMEM(grad.shape, jnp.float32),
            pltpu.VMEM((16, width), jnp.float32),
            pltpu.VMEM((plane, 16, size), jnp.float32),
            pltpu.VMEM((2, 16, size), jnp.float32),
            pltpu.SemaphoreType.DMA((2,)),
            pltpu.SemaphoreType.DMA((plane,)),
            pltpu.SemaphoreType.DMA((plane,)),
            pltpu.SemaphoreType.DMA((2,)),
            pltpu.SemaphoreType.DMA((2,)),
        ],
    )


def rotate_pairs(values, cosine, sine):
    parts = [
        rotate_lanes(values[:, at : at + PAIR], cosine, sine)
        for at in range(0, values.shape[1], PAIR)
    ]
    return jnp.concatenate(parts, 1)


def plane_peers():
    ctx = lax.axis_size("ctx")
    size = lax.axis_size("shard") * ctx
    mine = lax.axis_index("shard") * ctx + lax.axis_index("ctx")

    def peer(distance):
        index = lax.rem(mine + distance, size)
        return index, {"shard": index // ctx, "ctx": lax.rem(index, ctx)}

    return size, mine, peer


def greet_plane(size, peer):
    barrier = pltpu.get_barrier_semaphore()
    for distance in range(1, size):
        pl.semaphore_signal(barrier, inc=1, device_id=peer(distance)[1], device_id_type=MESH)


def front_kernel(
    live_ref, tokens_hbm, weight_hbm, own_gain_ref, cos_ref, sin_ref,
    h_hbm, q_ref, k_ref, v_ref, kp_ref, vp_ref, o_ref, l_ref, gain_ref,
    send, recv, gain_send, gain_recv, tokens_ref, weight_ref, h_ref, load_sem, store_sem,
):
    load, wait = loads_of([(tokens_hbm, tokens_ref), (weight_hbm, weight_ref)], load_sem)
    load()
    late = lax.axis_index("ctx")
    rows, width = q_ref.shape
    block = min(BLOCK, rows)
    blocks = rows // block
    pairs = width // PAIR
    size, index, peer = plane_peers()
    part = own_gain_ref.shape[1]
    greet_plane(size, peer)
    pl.semaphore_wait(pltpu.get_barrier_semaphore(), size - 1)
    mine = pl.ds(pl.multiple_of(index * part, part), part)
    gain_ref[:, mine] = own_gain_ref[...]

    def gain_copy(distance):
        return pltpu.make_async_remote_copy(
            src_ref=own_gain_ref, dst_ref=gain_ref.at[:, mine],
            send_sem=gain_send.at[distance], recv_sem=gain_recv.at[distance],
            device_id=peer(distance)[1], device_id_type=MESH,
        )

    for distance in range(1, size):
        gain_copy(distance).start()
    for distance in range(1, size):
        gain_copy(distance).wait()
    wait()

    def here(at):
        return pl.ds(pl.multiple_of(at * block, block), block)

    def lanes(pair):
        return pl.ds(pl.multiple_of(pair * PAIR, PAIR), PAIR)

    def h_store(at):
        return pltpu.make_async_copy(h_ref.at[here(at)], h_hbm.at[here(at)], store_sem.at[at])

    @pl.loop(0, blocks)
    def _(at):
        stream = tokens_ref[here(at)].astype(jnp.float32)
        normed = (stream * unit_scale(stream) * gain_ref[0:1]).astype(jnp.bfloat16)
        h_ref[here(at)] = normed
        h_store(at).start()
        keys = dot(normed, weight_ref[1], (1, 0))
        k_ref[here(at)] = rotate_pairs(keys, cos_ref[here(at)], sin_ref[here(at)]).astype(jnp.bfloat16)
        v_ref[here(at)] = dot(normed, weight_ref[2], (1, 0)).astype(jnp.bfloat16)

    def exchange(pair):
        return [
            pltpu.make_async_remote_copy(
                src_ref=own.at[:, lanes(pair)], dst_ref=prev.at[:, lanes(pair)],
                send_sem=send.at[which, pair], recv_sem=recv.at[which, pair],
                device_id={"ctx": 1 - late}, device_id_type=MESH,
            )
            for which, own, prev in ((0, k_ref, kp_ref), (1, v_ref, vp_ref))
        ]

    @pl.when(late == 0)
    def _():
        @pl.loop(0, pairs)
        def _(pair):
            for copy in exchange(pair):
                copy.start()

    @pl.loop(0, blocks)
    def _(at):
        query = dot(h_ref[here(at)], weight_ref[0], (1, 0))
        query = rotate_pairs(query, cos_ref[here(at)], sin_ref[here(at)]) * 0.125
        q_ref[here(at)] = query.astype(jnp.bfloat16)

    def attend(pair, own, with_prev):
        column = lanes(pair)
        mine = slice(own * block, (own + 1) * block)
        query = q_ref[mine, column]
        mixed = []
        for head in range(2):
            queries = one_head(query, head)
            parts = []
            if with_prev:
                parts.append((dot(kp_ref[:, column], queries, (1, 1)), vp_ref[:, column]))
            if own:
                before = slice(0, own * block)
                parts.append((dot(k_ref[before, column], queries, (1, 1)), v_ref[before, column]))
            parts.append((causal(dot(k_ref[mine, column], queries, (1, 1))), v_ref[mine, column]))
            peak = parts[0][0].max(0, keepdims=True)
            for scores, _ in parts[1:]:
                peak = jnp.maximum(peak, scores.max(0, keepdims=True))
            expo = [jnp.exp(scores - peak) for scores, _ in parts]
            denom = expo[0].sum(0, keepdims=True)
            for e in expo[1:]:
                denom = denom + e.sum(0, keepdims=True)
            inverse = 1.0 / denom
            total = None
            for e, (_, value) in zip(expo, parts):
                term = dot(value, (e * inverse).astype(jnp.bfloat16), (0, 0))
                total = term if total is None else total + term
            mixed.append(total[head * HEAD : (head + 1) * HEAD])
            index = late * rows + own * block + lax.broadcasted_iota(jnp.int32, peak.shape, 1)
            l_ref[pair, head : head + 1, mine] = jnp.where(
                index < live_ref[0], peak + jnp.log(denom), -MASKED
            )
        result = jnp.concatenate(mixed, 0).T
        index = late * rows + own * block + lax.broadcasted_iota(jnp.int32, result.shape, 0)
        own_value = v_ref[mine, column].astype(jnp.float32)
        o_ref[mine, column] = jnp.where(index < live_ref[0], result, own_value).astype(jnp.bfloat16)

    @pl.loop(0, pairs)
    def _(pair):
        @pl.when(late == 0)
        def _():
            for own in range(blocks):
                attend(pair, own, False)

        @pl.when(late == 1)
        def _():
            for copy in exchange(pair):
                copy.wait_recv()
            for own in range(blocks):
                attend(pair, own, True)

    @pl.when(late == 0)
    def _():
        @pl.loop(0, pairs)
        def _(pair):
            for copy in exchange(pair):
                copy.wait_send()

    @pl.loop(0, blocks)
    def _(at):
        h_store(at).wait()


def layer_front(live, tokens, weight, gain, cosine, sine):
    rows, depth = tokens.shape
    width = weight.shape[2]
    pairs = width // PAIR
    part = jax.ShapeDtypeStruct((rows, width), jnp.bfloat16)
    outs = (
        jax.ShapeDtypeStruct((rows, depth), jnp.bfloat16), part, part, part, part, part, part,
        jax.ShapeDtypeStruct((pairs, 2, rows), jnp.float32),
        jax.ShapeDtypeStruct((8, depth), jnp.float32),
    )
    size = lax.axis_size("shard") * lax.axis_size("ctx")
    return pl.pallas_call(
        front_kernel,
        out_shape=outs,
        in_specs=[SMEM_SPEC, HBM_SPEC, HBM_SPEC] + [VMEM_SPEC] * 3,
        out_specs=(HBM_SPEC,) + (VMEM_SPEC,) * (len(outs) - 1),
        scratch_shapes=[pltpu.SemaphoreType.DMA((2, pairs))] * 2
        + [pltpu.SemaphoreType.DMA((size,))] * 2
        + [
            pltpu.VMEM(tokens.shape, jnp.bfloat16),
            pltpu.VMEM(weight.shape, jnp.bfloat16),
            pltpu.VMEM(tokens.shape, jnp.bfloat16),
            pltpu.SemaphoreType.DMA((2,)),
            pltpu.SemaphoreType.DMA((rows // BLOCK,)),
        ],
        compiler_params=pltpu.CompilerParams(
            collective_id=4, has_side_effects=True, vmem_limit_bytes=56 * 2**20
        ),
        cost_estimate=pl.CostEstimate(
            flops=80 * 10**9, bytes_accessed=40 * 2**20, transcendentals=0
        ),
        name="layer_front",
    )(live, tokens, weight, gain, cosine, sine)


def attend_back_kernel(
    count, live_ref, q_hbm, k_hbm, v_hbm, kp_hbm, vp_hbm, o_hbm, l_ref, cos_ref, sin_ref,
    part_hbm, middle_hbm, grad_hbm, both_hbm, dq_ref, dk_ref, dv_ref, out_ref,
    part_ref, grad_ref,
    q_ref, k_ref, v_ref, kp_ref, vp_ref, o_ref, do_ref, weight_ref, middle_ref, early_sem, late_sem,
    dq_acc, dk_acc, dv_acc, dkp_acc, dvp_acc, leave, arrive, slots, send, recv, chain_send, chain_recv,
):
    late = lax.axis_index("ctx")
    me = lax.axis_index("tp")
    rows, width = q_ref.shape
    block = min(BLOCK, rows)
    blocks = rows // block
    pairs = width // PAIR
    load_early, wait_early = loads_of(
        [
            (part_hbm, part_ref), (grad_hbm, grad_ref), (both_hbm.at[pl.ds(0, width)], weight_ref),
            (middle_hbm, middle_ref),
        ],
        early_sem,
    )
    load_late, wait_late = loads_of(
        [
            (o_hbm, o_ref), (q_hbm, q_ref), (kp_hbm, kp_ref), (vp_hbm, vp_ref), (k_hbm, k_ref),
            (v_hbm, v_ref),
        ],
        late_sem,
    )
    load_early()
    load_late()
    barrier = pltpu.get_barrier_semaphore()
    pl.semaphore_signal(barrier, inc=1, device_id={"ctx": 1 - late}, device_id_type=MESH)
    greet(me, count, 1)
    tick, drain, ticks = chain_parts(
        count, part_ref, out_ref, slots, chain_send, chain_recv,
        lambda rows, part, total, at: (middle_ref[part] + total).astype(jnp.bfloat16), BACK_CHUNK, BACK_LAG,
    )

    def here(at):
        return pl.ds(pl.multiple_of(at * block, block), block)

    def lanes(pair):
        return pl.ds(pl.multiple_of(pair * PAIR, PAIR), PAIR)

    def prepare(pair, step):
        column = lanes(pair)
        query = q_ref[here(step), column]
        upstream = do_ref[here(step), column]
        product = (upstream.astype(jnp.float32) * o_ref[here(step), column].astype(jnp.float32)).T
        queries = [one_head(query, head) for head in range(2)]
        upstreams = [one_head(upstream, head) for head in range(2)]
        inner = [
            product[head * HEAD : (head + 1) * HEAD].sum(0, keepdims=True) for head in range(2)
        ]
        totals = [l_ref[pair, head : head + 1, here(step)] for head in range(2)]
        query_both = jnp.concatenate(queries, 0)
        upstream_both = jnp.concatenate(upstreams, 0)

        def tile(keys, values, masked):
            grads, probs_all, out = [], [], []
            for head in range(2):
                scores = dot(keys, queries[head], (1, 1))
                if masked:
                    scores = causal(scores)
                probs = jnp.exp(scores - totals[head])
                prob_grad = dot(values, upstreams[head], (1, 1))
                score_grad = (probs * (prob_grad - inner[head])).astype(jnp.bfloat16)
                probs_all.append(probs.astype(jnp.bfloat16))
                grads.append(score_grad)
                out.append(dot(keys, score_grad, (0, 0))[head * HEAD : (head + 1) * HEAD])
            key_grad = dot(jnp.concatenate(grads, 1), query_both, (1, 0))
            value_grad = dot(jnp.concatenate(probs_all, 1), upstream_both, (1, 0))
            return jnp.concatenate(out, 0), key_grad, value_grad

        return tile, upstream

    def exchange(pair):
        return pltpu.make_async_remote_copy(
            src_ref=leave.at[pair], dst_ref=arrive.at[pair], send_sem=send.at[pair],
            recv_sem=recv.at[pair], device_id={"ctx": 1 - late}, device_id_type=MESH,
        )

    def prev_step(pair, step):
        column = lanes(pair)
        tile, _ = prepare(pair, step)

        @pl.when(step == 0)
        def _():
            dkp_acc[...] = jnp.zeros_like(dkp_acc)
            dvp_acc[...] = jnp.zeros_like(dvp_acc)

        query_grad = None
        for at in range(blocks):
            mine = slice(at * block, (at + 1) * block)
            more, key_grad, value_grad = tile(kp_ref[mine, column], vp_ref[mine, column], False)
            query_grad = more if query_grad is None else query_grad + more
            dkp_acc[mine] += key_grad
            dvp_acc[mine] += value_grad
        dq_acc[pair, :, here(step)] = query_grad

        @pl.when(step == blocks - 1)
        def _():
            leave[pair, 0] = dkp_acc[...].astype(jnp.bfloat16)
            leave[pair, 1] = dvp_acc[...].astype(jnp.bfloat16)
            exchange(pair).start()

    def own_step(pair, step):
        column = lanes(pair)
        tile, upstream = prepare(pair, step)
        query_grad, key_grad, value_grad = tile(k_ref[here(step), column], v_ref[here(step), column], True)
        index = late * rows + step * block + lax.broadcasted_iota(jnp.int32, upstream.shape, 0)
        dk_acc[here(step), column] = key_grad
        dv_acc[here(step), column] = value_grad + jnp.where(
            index < live_ref[0], 0.0, upstream.astype(jnp.float32)
        )
        dq_acc[pair, :, here(step)] += query_grad

        @pl.loop(0, step)
        def _(at):
            more, key_grad, value_grad = tile(k_ref[here(at), column], v_ref[here(at), column], False)
            dk_acc[here(at), column] += key_grad
            dv_acc[here(at), column] += value_grad
            dq_acc[pair, :, here(step)] += more

        grad = dq_acc[pair, :, here(step)].T * 0.125
        grad = rotate_lanes(grad, cos_ref[here(step)], -sin_ref[here(step)])
        dq_ref[here(step), column] = grad.astype(jnp.bfloat16)

    @pl.when(late == 0)
    def _():
        dq_acc[...] = jnp.zeros_like(dq_acc)

    wait_early()

    @pl.loop(0, blocks)
    def _(at):
        for more in range(LEAD):
            tick(at * LEAD + more)
        do_ref[here(at)] = dot(grad_ref[here(at)], weight_ref[...], (1, 1)).astype(jnp.bfloat16)

    wait_late()
    steps = pairs * blocks
    lead = blocks * LEAD

    @pl.loop(0, 2 * steps)
    def _(at):
        @pl.when(lead + at < ticks)
        def _():
            tick(lead + at)

        @pl.when((late == 1) & (at < steps))
        def _():
            prev_step(at // blocks, at % blocks)

        @pl.when(at >= steps)
        def _():
            own_step((at - steps) // blocks, at % blocks)

    if ticks > lead + 2 * steps:
        pl.loop(lead + 2 * steps, ticks)(tick)

    @pl.loop(0, pairs)
    def _(pair):
        column = lanes(pair)

        @pl.when(late == 0)
        def _():
            exchange(pair).wait_recv()
            dk_acc[:, column] += arrive[pair, 0].astype(jnp.float32)
            dv_acc[:, column] += arrive[pair, 1].astype(jnp.float32)

        @pl.when(late == 1)
        def _():
            exchange(pair).wait_send()

        dk_ref[:, column] = rotate_lanes(dk_acc[:, column], cos_ref[...], -sin_ref[...]).astype(
            jnp.bfloat16
        )
        dv_ref[:, column] = dv_acc[:, column].astype(jnp.bfloat16)

    drain()


def attend_back(live, arrays, cosine, sine, out_part, middle, grad, both, count):
    rows, width = arrays[0].shape
    pairs = width // PAIR
    part = jax.ShapeDtypeStruct((rows, width), jnp.bfloat16)
    outs = (
        part, part, part, jax.ShapeDtypeStruct(out_part.shape, jnp.bfloat16),
    )
    chunks = rows // 2 // BACK_CHUNK
    return pl.pallas_call(
        functools.partial(attend_back_kernel, count),
        out_shape=outs,
        in_specs=[SMEM_SPEC] + [HBM_SPEC] * 6 + [VMEM_SPEC] * 3 + [HBM_SPEC] * 4,
        out_specs=(VMEM_SPEC,) * len(outs),
        scratch_shapes=[
            *[pltpu.VMEM(out_part.shape, jnp.bfloat16)] * 2,
            *[pltpu.VMEM((rows, width), jnp.bfloat16)] * 7,
            pltpu.VMEM((width, middle.shape[1]), jnp.bfloat16),
            pltpu.VMEM(middle.shape, jnp.float32),
            pltpu.SemaphoreType.DMA((4,)),
            pltpu.SemaphoreType.DMA((6,)),
            pltpu.VMEM((pairs, PAIR, rows), jnp.float32),
            pltpu.VMEM((rows, width), jnp.float32),
            pltpu.VMEM((rows, width), jnp.float32),
            pltpu.VMEM((rows, PAIR), jnp.float32),
            pltpu.VMEM((rows, PAIR), jnp.float32),
            pltpu.VMEM((pairs, 2, rows, PAIR), jnp.bfloat16),
            pltpu.VMEM((pairs, 2, rows, PAIR), jnp.bfloat16),
            pltpu.VMEM((2, rows // 2, out_part.shape[1]), jnp.bfloat16),
            pltpu.SemaphoreType.DMA((pairs,)),
            pltpu.SemaphoreType.DMA((pairs,)),
            pltpu.SemaphoreType.DMA((4, chunks)),
            pltpu.SemaphoreType.DMA((4, chunks)),
        ],
        compiler_params=pltpu.CompilerParams(
            collective_id=5, has_side_effects=True, vmem_limit_bytes=58 * 2**20
        ),
        cost_estimate=pl.CostEstimate(
            flops=100 * 10**9, bytes_accessed=40 * 2**20, transcendentals=0
        ),
        name="attend_back",
    )(live, *arrays, cosine, sine, out_part, middle, grad, both)


def narrow_kernel(
    out_ref, down_ref, gate_up_ref, cos_in, sin_in, both_ref, low_ref, cos_ref, sin_ref
):
    cos_ref[...] = cos_in[...]
    sin_ref[...] = sin_in[...]
    split = out_ref.shape[0]
    both_ref[:split] = out_ref[...].astype(jnp.bfloat16)
    both_ref[split:] = down_ref[...].astype(jnp.bfloat16)
    low_ref[...] = gate_up_ref[...].astype(jnp.bfloat16)


def narrow(out_weight, down_weight, gate_up_weight, cosine, sine):
    return pl.pallas_call(
        narrow_kernel,
        out_shape=(
            jax.ShapeDtypeStruct(
                (out_weight.shape[0] + down_weight.shape[0], out_weight.shape[1]), jnp.bfloat16
            ),
            jax.ShapeDtypeStruct(gate_up_weight.shape, jnp.bfloat16),
            jax.ShapeDtypeStruct(cosine.shape, jnp.float32),
            jax.ShapeDtypeStruct(sine.shape, jnp.float32),
        ),
        in_specs=[VMEM_SPEC] * 5,
        out_specs=(VMEM_SPEC,) * 4,
        compiler_params=pltpu.CompilerParams(vmem_limit_bytes=40 * 2**20),
        cost_estimate=pl.CostEstimate(flops=40 * 10**9, bytes_accessed=2**24, transcendentals=0),
        name="narrow",
    )(out_weight, down_weight, gate_up_weight, cosine, sine)


def mlp_kernel(
    normed_ref, weight_ref, hidden_grad_ref, cotangent_ref,
    hidden_ref, down_grad_ref, gate_up_grad_ref, back_ref, turned, total,
):
    step = pl.program_id(0)

    @pl.when(step == 0)
    def _():
        turned[...] = normed_ref[...].T
        total[...] = jnp.zeros_like(total)

    gate = dot(normed_ref[...], weight_ref[0], (1, 0))
    upward = dot(normed_ref[...], weight_ref[1], (1, 0))
    hidden_grad = hidden_grad_ref[...]
    sigma = jax.nn.sigmoid(gate)
    swish = gate * sigma
    hidden = (swish * upward).astype(jnp.bfloat16)
    hidden_ref[...] = hidden
    gate_grad = (hidden_grad * upward * sigma * (1.0 + gate * (1.0 - sigma))).astype(jnp.bfloat16)
    upward_grad = (hidden_grad * swish).astype(jnp.bfloat16)
    both = jnp.concatenate([gate_grad, upward_grad], 1)
    weights = jnp.concatenate([weight_ref[0], weight_ref[1]], 1)
    total[...] += dot(both, weights, (1, 1))
    gate_up_grad_ref[0] = dot(turned[...], gate_grad, (1, 0)).astype(jnp.bfloat16)
    gate_up_grad_ref[1] = dot(turned[...], upward_grad, (1, 0)).astype(jnp.bfloat16)
    down_grad_ref[...] = dot(hidden.T, cotangent_ref[...], (1, 0)).astype(jnp.bfloat16)

    @pl.when(step == pl.num_programs(0) - 1)
    def _():
        back_ref[...] = total[...].astype(jnp.bfloat16)


def mlp(normed, weight, hidden_grad, cotangent):
    rows, depth = normed.shape
    width = weight.shape[2]
    whole = pl.BlockSpec((rows, depth), lambda j: (0, 0), pipeline_mode=pl.Buffered(1))
    return pl.pallas_call(
        mlp_kernel,
        out_shape=(
            jax.ShapeDtypeStruct((rows, width), jnp.bfloat16),
            jax.ShapeDtypeStruct((width, depth), jnp.bfloat16),
            jax.ShapeDtypeStruct((2, depth, width), jnp.bfloat16),
            jax.ShapeDtypeStruct((rows, depth), jnp.bfloat16),
        ),
        grid=(width // MLP_WIDE,),
        in_specs=[
            whole,
            pl.BlockSpec((2, depth, MLP_WIDE), lambda j: (0, 0, j)),
            pl.BlockSpec((rows, MLP_WIDE), lambda j: (0, j)),
            whole,
        ],
        out_specs=(
            pl.BlockSpec((rows, MLP_WIDE), lambda j: (0, j)),
            pl.BlockSpec((MLP_WIDE, depth), lambda j: (j, 0)),
            pl.BlockSpec((2, depth, MLP_WIDE), lambda j: (0, 0, j)),
            pl.BlockSpec((rows, depth), lambda j: (0, 0)),
        ),
        scratch_shapes=[
            pltpu.VMEM((depth, rows), jnp.bfloat16), pltpu.VMEM((rows, depth), jnp.float32),
        ],
        compiler_params=pltpu.CompilerParams(vmem_limit_bytes=60 * 2**20),
        cost_estimate=pl.CostEstimate(
            flops=14 * rows * depth * width, bytes_accessed=80 * 2**20, transcendentals=rows * width
        ),
        name="mlp",
    )(normed, weight, hidden_grad, cotangent)


def projection_back_kernel(
    normed_ref, weight_ref, dq_ref, dk_ref, dv_ref, mixed_ref, middle_ref, grad_ref, back_ref,
    turned, total,
):
    step = pl.program_id(0)

    @pl.when(step == 0)
    def _():
        turned[...] = normed_ref[...].T

    for at, ref in enumerate((dq_ref, dk_ref, dv_ref)):

        @pl.when(step == at)
        def _():
            term = dot(ref[...], weight_ref[0], (1, 1))
            if at == 0:
                total[...] = term
            elif at == 1:
                total[...] += term
            else:
                back_ref[...] = (total[...] + term).astype(jnp.bfloat16)
            grad_ref[0] = dot(turned[...], ref[...], (1, 0)).astype(jnp.bfloat16)

    @pl.when(step == 3)
    def _():
        turned[...] = middle_ref[...].T
        grad_ref[0] = dot(turned[...], mixed_ref[...], (1, 0)).astype(jnp.bfloat16)


def projection_back(normed, weight, dq, dk, dv, mixed, middle):
    rows, depth = normed.shape
    width = dq.shape[1]
    whole = lambda w: pl.BlockSpec((rows, w), lambda j: (0, 0), pipeline_mode=pl.Buffered(1))
    return pl.pallas_call(
        projection_back_kernel,
        out_shape=(
            jax.ShapeDtypeStruct((4, depth, width), jnp.bfloat16),
            jax.ShapeDtypeStruct((rows, depth), jnp.bfloat16),
        ),
        grid=(4,),
        in_specs=[
            whole(depth),
            pl.BlockSpec((1, depth, width), lambda j: (jnp.minimum(j, 2), 0, 0)),
            whole(width), whole(width), whole(width), whole(width), whole(depth),
        ],
        out_specs=(
            pl.BlockSpec((1, depth, width), lambda j: (j, 0, 0)),
            pl.BlockSpec((rows, depth), lambda j: (0, 0)),
        ),
        scratch_shapes=[
            pltpu.VMEM((depth, rows), jnp.bfloat16), pltpu.VMEM((rows, depth), jnp.float32),
        ],
        compiler_params=pltpu.CompilerParams(vmem_limit_bytes=60 * 2**20),
        cost_estimate=pl.CostEstimate(
            flops=14 * rows * depth * width, bytes_accessed=40 * 2**20, transcendentals=0
        ),
        name="projection_back",
    )(normed, weight, dq, dk, dv, mixed, middle)


def tail_kernel(
    grad_ref, out_grad_ref, w_ref, m_ref, s_ref, ow_ref, om_ref, os_ref,
    g_out, w_out, m_out, s_out, og_out, step_out, om_out, os_out,
):
    grad = grad_ref[0:3].astype(jnp.float32)
    update, first, second = adam_update(w_ref[...], m_ref[...], s_ref[...], grad, decay_rate)
    g_out[...] = grad
    w_out[...] = w_ref[...] - update
    m_out[...] = first
    s_out[...] = second
    grad = out_grad_ref[0].astype(jnp.float32).T
    update, first, second = adam_update(ow_ref[...], om_ref[...], os_ref[...], grad, decay_rate)
    og_out[...] = grad
    step_out[...] = update
    om_out[...] = first
    os_out[...] = second


def adam_tail(grads, qkv, out):
    planes, rows, width = qkv[0].shape
    steps = width // PAIR
    mine = pl.BlockSpec((planes, rows // steps, width), lambda i: (0, i, 0))
    other = pl.BlockSpec((PAIR, rows), lambda i: (i, 0))
    shapes = [jax.ShapeDtypeStruct(qkv[0].shape, jnp.float32)] * 4
    shapes += [jax.ShapeDtypeStruct(out[0].shape, jnp.float32)] * 4
    results = pl.pallas_call(
        tail_kernel,
        out_shape=tuple(shapes),
        grid=(steps,),
        in_specs=[
            pl.BlockSpec((planes + 1, rows // steps, width), lambda i: (0, i, 0)),
            pl.BlockSpec((1, rows, PAIR), lambda i: (planes, 0, i)),
            mine, mine, mine, other, other, other,
        ],
        out_specs=(mine,) * 4 + (other,) * 4,
        compiler_params=pltpu.CompilerParams(vmem_limit_bytes=60 * 2**20),
        cost_estimate=pl.CostEstimate(
            flops=10**7, bytes_accessed=16 * 2**20, transcendentals=0
        ),
        name="adam_tail",
    )(grads, grads, *qkv, *out)
    return results[:4], results[4:]


def scatter_low(grad, axis=1):
    return lax.psum_scatter(
        grad.astype(jnp.bfloat16), ("shard", "ctx"), scatter_dimension=axis, tiled=True
    ).astype(jnp.float32)


def after(array, *others):
    return lax.optimization_barrier((array, *others))[0]


def adam_update(weight, first, second, grad, decay):
    first_new = beta_one * first + (1.0 - beta_one) * grad
    second_new = beta_two * second + (1.0 - beta_two) * grad * grad
    first_hat = first_new / (1.0 - beta_one**step_count)
    second_hat = second_new / (1.0 - beta_two**step_count)
    update = learn_rate * (first_hat / (jnp.sqrt(second_hat) + adam_eps) + decay * weight)
    return (update, first_new, second_new)


def body(
    tokens,
    cotangent,
    lengths,
    qkv_weight,
    out_weight,
    gate_up_weight,
    down_weight,
    norm_gains,
    qkv_first,
    out_first,
    gate_up_first,
    down_first,
    gains_first,
    qkv_second,
    out_second,
    gate_up_second,
    down_second,
    gains_second,
):
    row_count = tokens.shape[0]
    count = lax.axis_size("tp")
    offset = lax.axis_index("ctx") * row_count
    query_index = offset + jnp.arange(row_count, dtype=jnp.int32)
    qkv_low = qkv_weight.astype(jnp.bfloat16)
    cosine, sine = rotation(query_index, HEAD)
    cosine, sine = (jnp.concatenate([c[:, 0]] * 4, 1) for c in (cosine, sine))
    both_low, gate_up_low, cosine, sine = narrow(
        out_weight, down_weight, gate_up_weight, cosine, sine
    )
    gains_low = norm_gains.astype(jnp.bfloat16).astype(jnp.float32)
    gains_low = jnp.concatenate([gains_low] * 4, 0)
    gather = lambda a: lax.all_gather(a, ("shard", "ctx"), axis=1, tiled=True)
    qkv_full = gather(qkv_low)
    both_full = gather(after(both_low, qkv_full))
    normed_one, query, keys, values, keys_prev, values_prev, mixed_low, totals, gains_full = layer_front(
        lengths, tokens, qkv_full, gains_low, cosine, sine
    )
    gate_up_full = gather(after(gate_up_low, both_full, totals))
    normed_two, middle, hidden_grad = sum_middle(
        mixed_low, both_full, tokens, gains_full, cotangent, count
    )
    hidden, down_grad_local, gate_up_grad_local, mlp_back_part = mlp(
        normed_two, gate_up_full, hidden_grad, cotangent
    )
    down_grad = scatter_low(down_grad_local)
    middle_low, middle_grad, gain_two_grad, out_part = sum_middle_back(
        mlp_back_part, middle, cotangent, gains_full, hidden, both_full, count
    )
    gate_up_grad = scatter_low(after(gate_up_grad_local, down_grad, middle_low))
    query_low, key_low, value_low, out_tokens = attend_back(
        lengths,
        [query, keys, values, keys_prev, values_prev, mixed_low, totals],
        cosine, sine, out_part, middle, middle_low, both_full, count,
    )
    qkv_grad_local, attn_back_part = projection_back(
        normed_one, qkv_full, query_low, key_low, value_low, mixed_low, middle_low
    )
    attn_back_part, qkv_grad_local, _ = lax.optimization_barrier(
        (attn_back_part, qkv_grad_local, gate_up_grad)
    )
    tail_grads = lax.psum_scatter(
        qkv_grad_local, ("shard", "ctx"), scatter_dimension=1, tiled=True
    )
    input_grad, gains_grad = sum_input_back(
        attn_back_part, tokens, middle_grad, gains_full, gain_two_grad, norm_gains.shape[1], count
    )
    tail_grads, _ = lax.optimization_barrier((tail_grads, gains_grad))
    (qkv_grad, qkv_new, qkv_first_new, qkv_second_new), (
        out_grad, out_step, out_first_new, out_second_new,
    ) = adam_tail(
        tail_grads,
        (qkv_weight, qkv_first, qkv_second),
        (out_weight, out_first, out_second),
    )
    gate_up_step, gate_up_first_new, gate_up_second_new = adam_update(
        gate_up_weight, gate_up_first, gate_up_second, gate_up_grad, decay_rate
    )
    down_step, down_first_new, down_second_new = adam_update(
        down_weight, down_first, down_second, down_grad, decay_rate
    )
    gains_step, gains_first_new, gains_second_new = adam_update(
        norm_gains, gains_first, gains_second, gains_grad, 0.0
    )
    gate_up_new = gate_up_weight - gate_up_step
    down_new = down_weight - down_step
    return (
        out_tokens,
        input_grad,
        qkv_grad,
        out_grad,
        gate_up_grad,
        down_grad,
        gains_grad,
        qkv_new,
        out_step,
        gate_up_new,
        down_new,
        gains_step,
        qkv_first_new,
        out_first_new,
        gate_up_first_new,
        down_first_new,
        gains_first_new,
        qkv_second_new,
        out_second_new,
        gate_up_second_new,
        down_second_new,
        gains_second_new,
    )


def solution(mesh):
    return jax.shard_map(
        body,
        mesh=mesh,
        in_specs=(
            P(("shard", "ctx"), None),
            P(("shard", "ctx"), None),
            P("shard"),
            P(None, ("shard", "ctx"), "tp"),
            P("tp", ("shard", "ctx")),
            P(None, ("shard", "ctx"), "tp"),
            P("tp", ("shard", "ctx")),
            P(None, ("shard", "ctx")),
            P(None, ("shard", "ctx"), "tp"),
            P("tp", ("shard", "ctx")),
            P(None, ("shard", "ctx"), "tp"),
            P("tp", ("shard", "ctx")),
            P(None, ("shard", "ctx")),
            P(None, ("shard", "ctx"), "tp"),
            P("tp", ("shard", "ctx")),
            P(None, ("shard", "ctx"), "tp"),
            P("tp", ("shard", "ctx")),
            P(None, ("shard", "ctx")),
        ),
        out_specs=(
            P(("shard", "ctx"), None),
            P(("shard", "ctx"), None),
            P(None, ("shard", "ctx"), "tp"),
            P("tp", ("shard", "ctx")),
            P(None, ("shard", "ctx"), "tp"),
            P("tp", ("shard", "ctx")),
            P(None, ("shard", "ctx")),
            P(None, ("shard", "ctx"), "tp"),
            P("tp", ("shard", "ctx")),
            P(None, ("shard", "ctx"), "tp"),
            P("tp", ("shard", "ctx")),
            P(None, ("shard", "ctx")),
            P(None, ("shard", "ctx"), "tp"),
            P("tp", ("shard", "ctx")),
            P(None, ("shard", "ctx"), "tp"),
            P("tp", ("shard", "ctx")),
            P(None, ("shard", "ctx")),
            P(None, ("shard", "ctx"), "tp"),
            P("tp", ("shard", "ctx")),
            P(None, ("shard", "ctx"), "tp"),
            P("tp", ("shard", "ctx")),
            P(None, ("shard", "ctx")),
        ),
        check_vma=False,
    )
```
